512 devices in a mesh: img: 8 (over x, core), dev: 64 (over z, y).
Axes of the slice: x: 4, y: 8, z: 8, core: 2. Of those that a mesh axis runs over, the one named last changes fastest.
Arguments:
- params: float32 [59, 1048576], P(None, ('img', 'dev')), may hold values from -6 to 2.5, as said below
- first_moment: float32 [59, 1048576], P(None, ('img', 'dev')), may hold values from -0.12 to 0.12
- second_moment: float32 [59, 1048576], P(None, ('img', 'dev')), may hold values from 0.001 to 0.1
- send_blocks: int32 [512, 512], P(('img', 'dev')), may hold values from 0 to 511, as said below
- tile_blocks: int32 [8, 64, 512], P('img', 'dev'), may hold values from 0 to 511, as said below
- tile_live: int32 [8, 512], P('img', 'dev'), may hold values from 32 to 64
- depth_order: int32 [8, 512, 256], P('img', 'dev'), may hold values from 0 to 255, each once within a row
- tile_where: int32 [8, 512], P('img', 'dev'), may hold values from 0 to 511, as said below
- target: float32 [8, 512, 768], P('img', 'dev'), may hold values from 0 to 1
- camera: float32 [8, 12], P('img'), may hold values from -0.2 to 6, as said below
Outputs:
- new_params: float32 [59, 1048576], P(None, ('img', 'dev'))
- new_first: float32 [59, 1048576], P(None, ('img', 'dev'))
- new_second: float32 [59, 1048576], P(None, ('img', 'dev'))
The draws below stay inside these ranges and needn't reach their ends.
Inputs may be any that keep to these rules, and one draw needn't show every extreme that they name: `send_blocks`: an owner sends a different block to each renderer. `tile_blocks`: each renderer's list names every owner once. `tile_where`: each image's tile slots render every tile of the image once. `params`: positions lie within [-2.5, 2.5], the quaternion's real part within [1, 2]. `camera`: the view matrix lies within 0.05 of the identity entrywise, the translation's third entry within [5, 6].
All inputs are finite; a program needn't handle non-finite values.
Results may differ from the reference program's by a relative error of at most 0.0003.
Values sent between devices are 32-bit elements; how exact they have to be, the bound alone decides.
A program may use at most 64 MiB of HBM per device.

```python
import math
import jax
import jax.numpy as jnp
from jax import lax

VALUES = 59
TILES_DEV = 8
CAND = 256
TILES_ACROSS = 32
OWNERS = 512
BLK_DEV = 512
TILES = 512
TILES_DOWN = 16
SLOTS = 64
BLOCK = 4
G_DEV = 2048
GAUSS = 1048576
N_IMG = 8
N_DEV = 64


def first_blocks(key):
    return jax.random.permutation(key, BLK_DEV)[:OWNERS].astype(jnp.int32)


def owner_order(key):
    return jax.random.permutation(key, OWNERS).astype(jnp.int32)


def tile_order(key):
    return jax.random.permutation(key, TILES).astype(jnp.int32)


def layout_tables(key):
    subkeys = jax.random.split(jax.random.fold_in(key, 101), 3)
    sent_table = jax.vmap(first_blocks)(jax.random.split(subkeys[0], OWNERS))
    tile_lists = jax.vmap(owner_order)(jax.random.split(subkeys[1], OWNERS)).reshape(N_IMG, N_DEV, OWNERS)
    placements = jax.vmap(tile_order)(jax.random.split(subkeys[2], N_IMG))
    return (sent_table, tile_lists, placements)


def camera_parts(key):
    subkeys = jax.random.split(jax.random.fold_in(key, 211), 3)
    matrix = jnp.eye(3, dtype=jnp.float32)[None] + 0.05 * jax.random.uniform(subkeys[0], (N_IMG, 3, 3), jnp.float32, -1.0, 1.0)
    sideways = 0.2 * jax.random.uniform(subkeys[1], (N_IMG, 2), jnp.float32, -1.0, 1.0)
    distance = jax.random.uniform(subkeys[2], (N_IMG, 1), jnp.float32, 5.0, 6.0)
    return (matrix, jnp.concatenate([sideways, distance], axis=1))


def spread_blocks(table):
    return jnp.broadcast_to(table[:, :, None], (OWNERS, BLK_DEV, BLOCK)).reshape(GAUSS)


def colour_reach():
    per_degree = jnp.array([0.5, 1.0, 1.0, 1.0, 2.0, 2.0, 2.0, 2.0, 2.0, 2.5, 2.5, 2.5, 2.5, 2.5, 2.5, 2.5], jnp.float32)
    return jnp.repeat(per_degree, 3)[:, None]


def draw_params(key, part):
    sent_table, tile_lists, placements = layout_tables(key)
    matrix, translation = camera_parts(key)
    key = jax.random.fold_in(key, 11)
    subkeys = jax.random.split(key, 11)
    owner_ids = jnp.arange(OWNERS, dtype=jnp.int32)
    square_ids = jnp.broadcast_to(owner_ids[None, :], (OWNERS, OWNERS))
    receiver = jnp.full((OWNERS, BLK_DEV), -1, jnp.int32).at[owner_ids[:, None], sent_table].set(square_ids)
    slot_index = jnp.zeros((OWNERS, OWNERS), jnp.int32).at[owner_ids[:, None], tile_lists.reshape(OWNERS, OWNERS)].set(square_ids)
    renderer = jnp.maximum(receiver, 0)
    owner_grid = jnp.broadcast_to(owner_ids[:, None], (OWNERS, BLK_DEV))
    slot_of_block = slot_index[renderer, owner_grid]
    image_of = renderer // N_DEV
    tile_slot = renderer % N_DEV * TILES_DEV + slot_of_block // SLOTS
    tile_id = placements[image_of, tile_slot]
    is_sent = spread_blocks(receiver) >= 0
    image_gauss = spread_blocks(image_of)
    tile_gauss = spread_blocks(tile_id)
    pixel_x = (16 * (tile_gauss % TILES_ACROSS) + 8).astype(jnp.float32) + jax.random.uniform(subkeys[0], (GAUSS,), jnp.float32, -10.0, 10.0)
    pixel_y = (16 * (tile_gauss // TILES_ACROSS) + 8).astype(jnp.float32) + jax.random.uniform(subkeys[1], (GAUSS,), jnp.float32, -10.0, 10.0)
    offset = translation[image_gauss]
    depth_shift = jax.random.uniform(subkeys[2], (GAUSS,), jnp.float32, -0.8, 0.8)
    depth = offset[:, 2] + depth_shift
    focal_len = 32.0 * TILES_ACROSS
    rel_x = (pixel_x - 8.0 * TILES_ACROSS) * depth / focal_len - offset[:, 0]
    rel_y = (pixel_y - 8.0 * TILES_DOWN) * depth / focal_len - offset[:, 1]
    rel_z = depth_shift
    tilt = matrix[image_gauss] - jnp.eye(3, dtype=jnp.float32)[None]
    placed = jnp.stack([(rel_x, rel_y, rel_z)[row_id] - tilt[:, row_id, 0] * rel_x - tilt[:, row_id, 1] * rel_y - tilt[:, row_id, 2] * rel_z for row_id in range(3)], axis=0)
    placed = jnp.clip(placed, -2.4, 2.4)
    free_x = jax.random.uniform(subkeys[3], (1, GAUSS), jnp.float32, -1.0, 1.0)
    free_y = jax.random.uniform(subkeys[4], (1, GAUSS), jnp.float32, -0.5, 0.5)
    free_z = jax.random.uniform(subkeys[5], (1, GAUSS), jnp.float32, -1.0, 1.0)
    free_pos = jnp.concatenate([free_x, free_y, free_z], axis=0)
    position = jnp.where(is_sent[None, :], placed, free_pos)
    log_scale = jax.random.uniform(subkeys[6], (3, GAUSS), jnp.float32, -4.8, -3.4)
    real_part = jax.random.uniform(subkeys[7], (1, GAUSS), jnp.float32, 1.0, 2.0)
    imag_parts = jax.random.uniform(subkeys[8], (3, GAUSS), jnp.float32, -1.0, 1.0)
    opacity = jax.random.uniform(subkeys[9], (1, GAUSS), jnp.float32, -3.0, 0.0)
    colour = colour_reach() * jax.random.uniform(subkeys[10], (48, GAUSS), jnp.float32, -1.0, 1.0)
    return jnp.concatenate([position, log_scale, real_part, imag_parts, opacity, colour], axis=0)


def draw_send_blocks(key, part):
    sent_table, tile_lists, placements = layout_tables(key)
    return sent_table


def draw_tile_blocks(key, part):
    sent_table, tile_lists, placements = layout_tables(key)
    return tile_lists


def draw_tile_where(key, part):
    sent_table, tile_lists, placements = layout_tables(key)
    return placements


def draw_camera(key, part):
    matrix, translation = camera_parts(key)
    return jnp.concatenate([matrix.reshape(N_IMG, 9), translation], axis=1)


def place_ends(drawn, own_key, smallest, top_value):
    longest = drawn.shape.index(max(drawn.shape))
    spots = []
    for shift in (0, 1):
        where = [jax.random.randint(jax.random.fold_in(own_key, axis), (), 0, length) for axis, length in enumerate(drawn.shape)]
        where[longest] = (where[longest] + shift) % drawn.shape[longest]
        spots.append(tuple(where))
    return drawn.at[spots[0]].set(smallest).at[spots[1]].set(top_value)


def levels(stream_key, shape, cuts, smallest, high):
    def one(dim, blocks):
        draws = jax.random.uniform(jax.random.fold_in(jax.random.fold_in(stream_key, 6), dim), (blocks,), jnp.float32, smallest / len(cuts), high / len(cuts))
        return jnp.repeat(jnp.exp(draws), shape[dim] // blocks).reshape((-1,) + (1,) * (len(shape) - dim - 1))

    gain = one(*cuts[0])
    for cut in cuts[1:]:
        gain = gain * one(*cut)
    return gain


def normal_values(own_key, shape, deviation, limit, cuts=(), held_as=jnp.bfloat16):
    result = jax.random.normal(own_key, shape, jnp.float32) * deviation
    if len(cuts) > 0:
        result = levels(own_key, shape, cuts, -0.22, 0.18) * result
    return jnp.clip(result, min=-limit, max=limit).astype(held_as)


def setup_inputs(seed: int = 0) -> dict:
    keys = jax.random.split(jax.random.key(seed), 11)
    params = draw_params(jax.random.fold_in(keys[10], 71), 0)
    first_moment = normal_values(keys[1], (VALUES, GAUSS), 0.02, 0.12, ((1, 512),), jnp.float32)
    second_moment = jnp.clip(jnp.exp(math.log(0.1) - 4.6051702 * jax.random.uniform(keys[2], (VALUES, GAUSS), jnp.float32) ** levels(keys[2], (VALUES, GAUSS), ((1, 512),), -0.2, 0.2)), 0.001, 0.1)
    send_blocks = draw_send_blocks(jax.random.fold_in(keys[10], 71), 0)
    tile_blocks = draw_tile_blocks(jax.random.fold_in(keys[10], 71), 0)
    tile_live = place_ends(jax.random.randint(keys[5], (N_IMG, TILES), SLOTS // 2, SLOTS + 1), jax.random.fold_in(keys[5], 1), SLOTS // 2, SLOTS).astype(jnp.int32)
    depth_order = jax.vmap(lambda own: jax.random.permutation(own, CAND))(jax.random.split(keys[6], N_IMG * TILES)).reshape((N_IMG, TILES, CAND)).astype(jnp.int32)
    tile_where = draw_tile_where(jax.random.fold_in(keys[10], 71), 0)
    target = jnp.clip(1.0 * jax.random.uniform(keys[8], (N_IMG, TILES, 768), jnp.float32) ** levels(keys[8], (N_IMG, TILES, 768), ((0, 8), (1, 64)), -0.2, 0.2), 0.0, 1.0)
    camera = draw_camera(jax.random.fold_in(keys[10], 71), 0)
    return dict(params=params, first_moment=first_moment, second_moment=second_moment, send_blocks=send_blocks, tile_blocks=tile_blocks, tile_live=tile_live, depth_order=depth_order, tile_where=tile_where, target=target, camera=camera)


HARMONIC_ZERO = 0.28209479177387814
HARMONIC_ONE = 0.4886025119029199
HARMONIC_TWO = (1.0925484305920792, -1.0925484305920792, 0.31539156525252005, -1.0925484305920792, 0.5462742152960396)
HARMONIC_THREE = (-0.5900435899266435, 2.890611442640554, -0.4570457994644658, 0.3731763325901154, -0.4570457994644658, 1.445305721320277, -0.5900435899266435)

def harmonics(dir_x, dir_y, dir_z):
    square_x = dir_x * dir_x
    square_y = dir_y * dir_y
    square_z = dir_z * dir_z
    return [HARMONIC_ZERO + 0.0 * dir_x, -HARMONIC_ONE * dir_y, HARMONIC_ONE * dir_z, -HARMONIC_ONE * dir_x, HARMONIC_TWO[0] * dir_x * dir_y, HARMONIC_TWO[1] * dir_y * dir_z, HARMONIC_TWO[2] * (2.0 * square_z - square_x - square_y), HARMONIC_TWO[3] * dir_x * dir_z, HARMONIC_TWO[4] * (square_x - square_y), HARMONIC_THREE[0] * dir_y * (3.0 * square_x - square_y), HARMONIC_THREE[1] * dir_x * dir_y * dir_z, HARMONIC_THREE[2] * dir_y * (4.0 * square_z - square_x - square_y), HARMONIC_THREE[3] * dir_z * (2.0 * square_z - 3.0 * square_x - 3.0 * square_y), HARMONIC_THREE[4] * dir_x * (4.0 * square_z - square_x - square_y), HARMONIC_THREE[5] * dir_z * (square_x - square_y), HARMONIC_THREE[6] * dir_x * (square_x - 3.0 * square_y)]

def shade(harmonic_terms, coefficients):
    channels = []
    for channel in range(3):
        total = 0.5 + harmonic_terms[0] * coefficients[channel]
        for coef_id in range(1, 16):
            total = total + harmonic_terms[coef_id] * coefficients[3 * coef_id + channel]
        channels.append(jnp.maximum(total, 0.0))
    return channels

def choose_columns(fetched, slot_list, tile_count, candidates):
    per_tile = slot_list.shape[0] // tile_count
    block_size = candidates // per_tile
    within = jnp.arange(block_size, dtype=jnp.int32)
    columns = (slot_list.reshape(tile_count, per_tile)[:, :, None] * block_size + within[None, None, :]).reshape(tile_count, candidates)
    return fetched[:, columns]

def project(chosen, camera, width_tiles, height_tiles):
    matrix = camera[:9].reshape(3, 3)
    translation = camera[9:]
    viewed = [matrix[row_id, 0] * chosen[0] + matrix[row_id, 1] * chosen[1] + matrix[row_id, 2] * chosen[2] + translation[row_id] for row_id in range(3)]
    inverse_z = 1.0 / viewed[2]
    focal_len = 32.0 * width_tiles
    centre_u = focal_len * viewed[0] * inverse_z + 8.0 * width_tiles
    centre_v = focal_len * viewed[1] * inverse_z + 8.0 * height_tiles
    scales = jnp.exp(chosen[3:6])
    quat_norm = jnp.sqrt(lax.optimization_barrier(jnp.sum(chosen[6:10] * chosen[6:10], axis=0)))
    real_part = chosen[6] / quat_norm
    imag_x = chosen[7] / quat_norm
    imag_y = chosen[8] / quat_norm
    imag_z = chosen[9] / quat_norm
    rot_matrix = [[1.0 - 2.0 * (imag_y * imag_y + imag_z * imag_z), 2.0 * (imag_x * imag_y - real_part * imag_z), 2.0 * (imag_x * imag_z + real_part * imag_y)], [2.0 * (imag_x * imag_y + real_part * imag_z), 1.0 - 2.0 * (imag_x * imag_x + imag_z * imag_z), 2.0 * (imag_y * imag_z - real_part * imag_x)], [2.0 * (imag_x * imag_z - real_part * imag_y), 2.0 * (imag_y * imag_z + real_part * imag_x), 1.0 - 2.0 * (imag_x * imag_x + imag_y * imag_y)]]
    spread = [[rot_matrix[row_id][col_id] * scales[col_id] for col_id in range(3)] for row_id in range(3)]
    jacobian = [[focal_len * inverse_z * matrix[row_id, col_id] - focal_len * viewed[row_id] * inverse_z * inverse_z * matrix[2, col_id] for col_id in range(3)] for row_id in range(2)]
    projected = [[jacobian[row_id][0] * spread[0][col_id] + jacobian[row_id][1] * spread[1][col_id] + jacobian[row_id][2] * spread[2][col_id] for col_id in range(3)] for row_id in range(2)]
    cov_xx = projected[0][0] * projected[0][0] + projected[0][1] * projected[0][1] + projected[0][2] * projected[0][2] + 0.3
    cov_xy = projected[0][0] * projected[1][0] + projected[0][1] * projected[1][1] + projected[0][2] * projected[1][2]
    cov_yy = projected[1][0] * projected[1][0] + projected[1][1] * projected[1][1] + projected[1][2] * projected[1][2] + 0.3
    determinant = cov_xx * cov_yy - cov_xy * cov_xy
    conic_xx = cov_yy / determinant
    conic_xy = -cov_xy / determinant
    conic_yy = cov_xx / determinant
    opacity = jax.nn.sigmoid(chosen[10])
    distance = jnp.sqrt(viewed[0] * viewed[0] + viewed[1] * viewed[1] + viewed[2] * viewed[2])
    harmonic_terms = harmonics(viewed[0] / distance, viewed[1] / distance, viewed[2] / distance)
    colour = shade(harmonic_terms, chosen[11:])
    return jnp.stack([centre_u, centre_v, conic_xx, conic_xy, conic_yy, opacity, colour[0], colour[1], colour[2]], axis=0)

def composite(shown, live_count, depth_rank, tile_place, target, width_tiles, block_size):
    tile_count, candidates = depth_rank.shape
    centre_u = shown[0]
    centre_v = shown[1]
    conic_xx = shown[2]
    conic_xy = shown[3]
    conic_yy = shown[4]
    opacity = shown[5]
    colour = jnp.transpose(shown[6:9], (1, 0, 2))
    pixel_id = jnp.arange(256, dtype=jnp.int32)
    tile_col = tile_place % width_tiles
    tile_row = tile_place // width_tiles
    pixel_x = (tile_col[:, None] * 16 + pixel_id[None, :] % 16).astype(jnp.float32) + 0.5
    pixel_y = (tile_row[:, None] * 16 + pixel_id[None, :] // 16).astype(jnp.float32) + 0.5
    offset_x = pixel_x[:, :, None] - centre_u[:, None, :]
    offset_y = pixel_y[:, :, None] - centre_v[:, None, :]
    exponent = conic_xx[:, None, :] * offset_x * offset_x + 2.0 * conic_xy[:, None, :] * offset_x * offset_y + conic_yy[:, None, :] * offset_y * offset_y
    live_mask = ((jnp.arange(candidates, dtype=jnp.int32) // block_size)[None, :] < live_count[:, None]).astype(jnp.float32)
    alphas = (opacity * live_mask)[:, None, :] * jnp.exp(-0.5 * exponent)
    sorted_alpha = jnp.take_along_axis(alphas, depth_rank[:, None, :], axis=2)
    sorted_colour = jnp.take_along_axis(colour, depth_rank[:, None, :], axis=2)
    log_keep = jnp.log1p(-sorted_alpha)
    before = jnp.cumsum(log_keep, axis=2) - log_keep
    weights = jnp.exp(before) * sorted_alpha
    rendered = jnp.einsum('tpc,tkc->tkp', weights, sorted_colour, precision=lax.Precision.HIGHEST)
    residual = rendered - target.reshape(tile_count, 3, 256)
    return 0.5 * jnp.sum(residual * residual)

def step_rates():
    return jnp.concatenate([jnp.full((3,), 0.00016), jnp.full((3,), 0.005), jnp.full((4,), 0.001), jnp.full((1,), 0.05), jnp.full((3,), 0.0025), jnp.full((45,), 0.000125)]).astype(jnp.float32)

def adam_update(params, first_moment, second_moment, gradient):
    new_first = 0.9 * first_moment + 0.1 * gradient
    new_second = 0.999 * second_moment + 0.001 * gradient * gradient
    new_params = params - step_rates()[:, None] * new_first / (jnp.sqrt(new_second) + 1e-15)
    return (new_params, new_first, new_second)

def reference(params, first_moment, second_moment, send_blocks, tile_blocks, tile_live, depth_order, tile_where, target, camera):
    renderers = jnp.arange(OWNERS, dtype=jnp.int32)
    slot_lists = tile_blocks.reshape(OWNERS, OWNERS)
    live_rows = tile_live.reshape(OWNERS, TILES_DEV)
    rank_rows = depth_order.reshape(OWNERS, TILES_DEV, CAND)
    place_rows = tile_where.reshape(OWNERS, TILES_DEV)
    target_rows = target.reshape(OWNERS, TILES_DEV, 768)
    owner_base = jnp.arange(OWNERS, dtype=jnp.int32) * G_DEV
    within = jnp.arange(BLOCK, dtype=jnp.int32)

    def one_renderer(gradient, inputs):
        render_id, slot_list, live_count, depth_rank, tile_place, pixels = inputs
        columns = (owner_base[:, None] + send_blocks[:, render_id][:, None] * BLOCK + within[None, :]).reshape(-1)
        fetched = params[:, columns]
        view_row = camera[render_id // N_DEV]

        def error_of(fetched_values):
            chosen = choose_columns(fetched_values, slot_list, TILES_DEV, CAND)
            shown = project(chosen, view_row, TILES_ACROSS, TILES_DOWN)
            return composite(shown, live_count, depth_rank, tile_place, pixels, TILES_ACROSS, BLOCK)
        sq_error, pullback = jax.vjp(error_of, fetched)
        grad_fetched, = pullback(jnp.ones_like(sq_error))
        return (gradient.at[:, columns].add(grad_fetched), None)
    gradient, _ = lax.scan(one_renderer, jnp.zeros_like(params), (renderers, slot_lists, live_rows, rank_rows, place_rows, target_rows))
    new_params, new_first, new_second = adam_update(params, first_moment, second_moment, gradient)
    return (new_params, new_first, new_second)
```

```python
import functools

import jax
import jax.numpy as jnp
from jax import lax
from jax.experimental import pallas as pl
from jax.experimental.pallas import tpu as pltpu
from jax.sharding import PartitionSpec as P

F32, BF16 = jnp.float32, jnp.bfloat16
LOG2E = 1.4426950408889634
FOCAL = 1024.0
CENTRE_U, CENTRE_V = 256.0, 128.0

HARMONIC_ZERO = 0.28209479177387814
HARMONIC_ONE = 0.4886025119029199
HARMONIC_TWO = (
    1.0925484305920792,
    -1.0925484305920792,
    0.31539156525252005,
    -1.0925484305920792,
    0.5462742152960396,
)
HARMONIC_THREE = (
    -0.5900435899266435,
    2.890611442640554,
    -0.4570457994644658,
    0.3731763325901154,
    -0.4570457994644658,
    1.445305721320277,
    -0.5900435899266435,
)


def harmonics(dir_x, dir_y, dir_z):
    square_x = dir_x * dir_x
    square_y = dir_y * dir_y
    square_z = dir_z * dir_z
    return [
        -HARMONIC_ONE * dir_y,
        HARMONIC_ONE * dir_z,
        -HARMONIC_ONE * dir_x,
        HARMONIC_TWO[0] * dir_x * dir_y,
        HARMONIC_TWO[1] * dir_y * dir_z,
        HARMONIC_TWO[2] * (2.0 * square_z - square_x - square_y),
        HARMONIC_TWO[3] * dir_x * dir_z,
        HARMONIC_TWO[4] * (square_x - square_y),
        HARMONIC_THREE[0] * dir_y * (3.0 * square_x - square_y),
        HARMONIC_THREE[1] * dir_x * dir_y * dir_z,
        HARMONIC_THREE[2] * dir_y * (4.0 * square_z - square_x - square_y),
        HARMONIC_THREE[3] * dir_z * (2.0 * square_z - 3.0 * square_x - 3.0 * square_y),
        HARMONIC_THREE[4] * dir_x * (4.0 * square_z - square_x - square_y),
        HARMONIC_THREE[5] * dir_z * (square_x - square_y),
        HARMONIC_THREE[6] * dir_x * (square_x - 3.0 * square_y),
    ]


def project(values, cam):
    m = [[cam[3 * r + c] for c in range(3)] for r in range(3)]
    viewed = [m[r][0] * values[0] + m[r][1] * values[1] + m[r][2] * values[2] + cam[9 + r] for r in range(3)]
    inverse_z = 1.0 / viewed[2]
    centre_u = FOCAL * viewed[0] * inverse_z + CENTRE_U
    centre_v = FOCAL * viewed[1] * inverse_z + CENTRE_V
    scales = [jnp.exp(values[3 + c]) for c in range(3)]
    norm = jnp.sqrt(values[6] * values[6] + values[7] * values[7] + values[8] * values[8] + values[9] * values[9])
    inverse_norm = 1.0 / norm
    w, x, y, z = (values[6 + c] * inverse_norm for c in range(4))
    rot = [
        [1.0 - 2.0 * (y * y + z * z), 2.0 * (x * y - w * z), 2.0 * (x * z + w * y)],
        [2.0 * (x * y + w * z), 1.0 - 2.0 * (x * x + z * z), 2.0 * (y * z - w * x)],
        [2.0 * (x * z - w * y), 2.0 * (y * z + w * x), 1.0 - 2.0 * (x * x + y * y)],
    ]
    focal_z = FOCAL * inverse_z
    jac = [[focal_z * (m[r][c] - viewed[r] * inverse_z * m[2][c]) for c in range(3)] for r in range(2)]
    proj = [
        [(jac[r][0] * rot[0][c] + jac[r][1] * rot[1][c] + jac[r][2] * rot[2][c]) * scales[c] for c in range(3)]
        for r in range(2)
    ]
    cov_xx = proj[0][0] * proj[0][0] + proj[0][1] * proj[0][1] + proj[0][2] * proj[0][2] + 0.3
    cov_xy = proj[0][0] * proj[1][0] + proj[0][1] * proj[1][1] + proj[0][2] * proj[1][2]
    cov_yy = proj[1][0] * proj[1][0] + proj[1][1] * proj[1][1] + proj[1][2] * proj[1][2] + 0.3
    inverse_det = 1.0 / (cov_xx * cov_yy - cov_xy * cov_xy)
    log_opacity = -jnp.log(1.0 + jnp.exp(-values[10]))
    inverse_distance = 1.0 / jnp.sqrt(viewed[0] * viewed[0] + viewed[1] * viewed[1] + viewed[2] * viewed[2])
    terms = harmonics(*[viewed[c] * inverse_distance for c in range(3)])
    colour = []
    for ch in range(3):
        total = 0.5 + HARMONIC_ZERO * values[11 + ch]
        for k in range(1, 16):
            total = total + terms[k - 1] * values[11 + 3 * k + ch]
        colour.append(jnp.maximum(total, 0.0))
    return [centre_u, centre_v, cov_yy * inverse_det, -cov_xy * inverse_det, cov_xx * inverse_det, log_opacity] + colour


def iota(shape, dim):
    return lax.broadcasted_iota(jnp.int32, shape, dim)


def one_hot(truth):
    return jnp.where(truth, 1.0, 0.0).astype(BF16)


def pieces(x, count):
    out = []
    for _ in range(count - 1):
        part = x.astype(BF16)
        out.append(part)
        x = x - part.astype(F32)
    out.append(x.astype(BF16))
    return out


def nn(a, b):
    return lax.dot_general(a, b, (((1,), (0,)), ((), ())), preferred_element_type=F32)


def nt(a, b):
    return lax.dot_general(a, b, (((1,), (1,)), ((), ())), preferred_element_type=F32)


def fold(x, count):
    rows = x.shape[0] // count
    total = x[:rows]
    for c in range(1, count):
        total = total + x[c * rows:(c + 1) * rows]
    return total


def owner_tables(send_ref, params_ref, pick, image_of, par3):
    send = send_ref[...]

    def chunk(g, carry):
        lanes = pl.ds(pl.multiple_of(g * 256, 256), 256)
        pick[lanes, :] = one_hot(iota((256, 512), 0) // 4 + g * 64 == send)
        return carry

    lax.fori_loop(0, 8, chunk, 0)
    image_row = jnp.broadcast_to((iota((8, 512), 1) // 64).astype(F32), (8, 512)).astype(BF16)
    images = nt(image_row, pick[...])
    for g in range(8):
        image_of[g:g + 1, :] = images[0:1, 256 * g:256 * (g + 1)]
        par3[:, g, :] = params_ref[:, 256 * g:256 * (g + 1)]


def cameras_of(cam_ref, image_of):
    image = image_of[...]
    masks = [image == float(i) for i in range(8)]
    cams = cam_ref[...]
    out = []
    for t in range(12):
        value = jnp.zeros((8, 256), F32)
        for i in range(8):
            value = jnp.where(masks[i], cams[i:i + 1, t:t + 1], value)
        out.append(value)
    return out


def owner_forward(cam_ref, pick, image_of, par3, shown3, put):
    shown = project([par3[c] for c in range(59)], cameras_of(cam_ref, image_of))
    for q in range(9):
        shown3[q] = shown[q]
    for q in range(9, 16):
        shown3[q] = jnp.zeros((8, 256), F32)
    within = iota((16, 256), 1) % 4
    total = jnp.zeros((192, 512), F32)
    for g in range(8):
        rows = []
        for b in range(4):
            rows.append(jnp.where(within == b, shown3[:, g, :], 0.0))
        rows = jnp.concatenate(rows, axis=0)
        total = total + nn(jnp.concatenate(pieces(rows, 3), axis=0), pick[256 * g:256 * (g + 1), :])
    sums = fold(total, 3)
    put(jnp.transpose(jnp.concatenate([sums, jnp.zeros((64, 512), F32)], axis=0)))


def owner_gradient(got, cam_ref, pick, image_of, par3, shown3, grad3):
    rows = jnp.transpose(got)[0:64]
    parts = jnp.concatenate(pieces(rows, 3), axis=0)
    within = iota((16, 256), 1) % 4
    for g in range(8):
        spread = fold(nt(parts, pick[256 * g:256 * (g + 1), :]), 3)
        total = jnp.zeros((16, 256), F32)
        for b in range(4):
            total = total + jnp.where(within == b, spread[16 * b:16 * (b + 1)], 0.0)
        shown3[:, g, :] = total
    values = [par3[c] for c in range(59)]
    cams = cameras_of(cam_ref, image_of)
    _, pullback = jax.vjp(lambda v: project(v, cams), values)
    (grads,) = pullback([shown3[q] for q in range(9)])
    for c in range(59):
        grad3[c] = grads[c]


def renderer_tables(lists_ref, order_ref, where_ref, live_ref, listed, sort, place, tri):
    listed[...] = one_hot(iota((512, 512), 0) == lists_ref[...])

    def one_tile(n, carry):
        order = order_ref[pl.ds(n, 1), :]
        key = (order % 4) * 128 + (n % 2) * 64 + order // 4
        sort[n] = one_hot(iota((512, 256), 0) == key)
        return carry

    lax.fori_loop(0, 8, one_tile, 0)
    lane = iota((8, 512), 1)
    tile = lane // 64
    where = jnp.zeros((8, 512), jnp.int32)
    live = jnp.zeros((8, 512), jnp.int32)
    for n in range(8):
        where = jnp.where(tile == n, where_ref[0, n], where)
        live = jnp.where(tile == n, live_ref[0, n], live)
    place[0] = (where % 32 * 16 + 8).astype(F32)
    place[1] = (where // 32 * 16 + 8).astype(F32)
    place[2] = jnp.where(lane % 64 < live, 1.0, 0.0)
    tri[...] = one_hot(iota((256, 256), 0) < iota((256, 256), 1))


def monomials(pixel, term):
    x = (pixel % 16).astype(F32) - 7.5
    y = (pixel // 16).astype(F32) - 7.5
    out = jnp.zeros(pixel.shape, F32)
    for t, value in enumerate((jnp.ones_like(x), x, y, x * x, x * y, y * y)):
        out = jnp.where(term == t, value, out)
    return out.astype(BF16)


def render(got, listed, sort, place, tri, target_ref, tile3, coef3, grad3, put):
    rows = jnp.transpose(got)[0:64]
    tiles = fold(nn(jnp.concatenate(pieces(rows, 3), axis=0), listed[...]), 3)
    for b in range(4):
        tile3[:, b, :] = tiles[16 * b:16 * (b + 1)]
    centre_x, centre_y, live = place[0, 0:4], place[1, 0:4], place[2, 0:4]

    def geometry():
        u, v, cxx, cxy, cyy, log_op = (tile3[q, 0:4] for q in range(6))
        return u - centre_x, v - centre_y, cxx, cxy, cyy, log_op

    u, v, cxx, cxy, cyy, log_op = geometry()
    a, b2, c2 = -0.5 * LOG2E * cxx, -LOG2E * cxy, -0.5 * LOG2E * cyy
    constant = a * u * u + b2 * u * v + c2 * v * v + LOG2E * log_op
    coefs = [
        jnp.where(live > 0.0, constant, -1e5),
        jnp.where(live > 0.0, -2.0 * a * u - b2 * v, 0.0),
        jnp.where(live > 0.0, -2.0 * c2 * v - b2 * u, 0.0),
        jnp.where(live > 0.0, a, 0.0),
        jnp.where(live > 0.0, b2, 0.0),
        jnp.where(live > 0.0, c2, 0.0),
    ] + [tile3[q, 0:4] for q in range(6, 9)]
    for c in range(9):
        coef3[c, 0:4] = coefs[c]
    for c in range(9, 16):
        coef3[c, 0:4] = jnp.zeros((4, 512), F32)
    grad3[...] = jnp.zeros(grad3.shape, F32)
    power = monomials(iota((256, 48), 0), iota((256, 48), 1) % 16)
    moment = monomials(iota((16, 256), 1), iota((16, 256), 0))
    lower = tri[...]

    for n in range(8):
        pair = slice(128 * (n // 2), 128 * (n // 2) + 128)
        mine = jnp.concatenate([coef3[:, b, pair] for b in range(4)], axis=1)
        sorted_parts = nn(jnp.concatenate(pieces(mine, 3), axis=0), sort[n])
        front = fold(sorted_parts, 3)
        q2 = nn(power, sorted_parts.astype(BF16))
        alpha = jnp.exp2(q2)
        log_keep = jnp.log(1.0 - alpha)
        hi, lo = pieces(log_keep, 2)
        before = jnp.exp(nn(hi, lower) + nn(lo, lower))
        weight = before * alpha
        w_hi, w_lo = pieces(weight, 2)
        colour = jnp.where(iota((8, 256), 0) < 3, pltpu.roll(front, 10, 0)[0:8], 0.0)
        c_all = jnp.concatenate(pieces(colour, 2), axis=0)
        rendered = fold(nt(c_all, w_hi), 2) + fold(nt(c_all, w_lo), 2)
        wanted = jnp.concatenate([target_ref[n:n + 1, 256 * ch:256 * (ch + 1)] for ch in range(3)] + [jnp.zeros((5, 256), F32)], axis=0)
        residual = rendered - wanted
        down = jnp.transpose(jnp.concatenate([residual, jnp.zeros((120, 256), F32)], axis=0))
        gain = down[:, 0:1] * colour[0:1] + down[:, 1:2] * colour[1:2] + down[:, 2:3] * colour[2:3]
        passed = weight * gain
        hi, lo = pieces(passed, 2)
        behind = nt(hi, lower) + nt(lo, lower)
        change = passed - behind * (alpha * jnp.exp(-log_keep))
        moments = nn(moment, pieces(change, 3)[0]) + nn(moment, pieces(change, 3)[1]) + nn(moment, pieces(change, 3)[2])
        r_all = jnp.concatenate(pieces(residual, 2), axis=0)
        shade = fold(nn(r_all, w_hi), 2) + fold(nn(r_all, w_lo), 2)
        back = jnp.concatenate([moments[0:8], shade], axis=0)
        spread = fold(nt(jnp.concatenate(pieces(back, 3), axis=0), sort[n]), 3)
        for b in range(4):
            grad3[:, b, pair] += spread[:, 128 * b:128 * (b + 1)]

    m0, mx, my, mxx, mxy, myy = (grad3[t, 0:4] for t in range(6))
    u, v, cxx, cxy, cyy, _ = geometry()
    hx, hy = mx - u * m0, my - v * m0
    hxx = mxx - 2.0 * u * mx + u * u * m0
    hxy = mxy - u * my - v * mx + u * v * m0
    hyy = myy - 2.0 * v * my + v * v * m0
    results = [cxx * hx + cxy * hy, cxy * hx + cyy * hy, -0.5 * hxx, -hxy, -0.5 * hyy, m0]
    results += [grad3[8 + ch, 0:4] for ch in range(3)]
    for q in range(9):
        tile3[q, 0:4] = results[q]
    for q in range(9, 16):
        tile3[q, 0:4] = jnp.zeros((4, 512), F32)
    rows = jnp.concatenate([tile3[:, b, :] for b in range(4)], axis=0)
    out = fold(nt(jnp.concatenate(pieces(rows, 3), axis=0), listed[...]), 3)
    put(jnp.transpose(jnp.concatenate([out, jnp.zeros((64, 512), F32)], axis=0)))


def rate_column():
    row = iota((59, 1), 0)
    rate = jnp.full((59, 1), 0.000125, F32)
    for end, value in ((14, 0.0025), (11, 0.05), (10, 0.001), (6, 0.005), (3, 0.00016)):
        rate = jnp.where(row < end, value, rate)
    return rate


def adam(grad3, params_ref, first_ref, second_ref, new_params, new_first, new_second):
    rate = rate_column()
    for g in range(8):
        at = slice(256 * g, 256 * (g + 1))
        gradient = grad3[:, g, :]
        first = 0.9 * first_ref[:, at] + 0.1 * gradient
        second = 0.999 * second_ref[:, at] + 0.001 * gradient * gradient
        new_first[:, at] = first
        new_second[:, at] = second
        new_params[:, at] = params_ref[:, at] - rate * first / (jnp.sqrt(second) + 1e-15)


OWNER_SCRATCH = [
    pltpu.VMEM((2048, 512), BF16),
    pltpu.VMEM((8, 256), F32),
    pltpu.VMEM((59, 8, 256), F32),
    pltpu.VMEM((16, 8, 256), F32),
]
RENDER_SCRATCH = [
    pltpu.VMEM((512, 512), BF16),
    pltpu.VMEM((8, 512, 256), BF16),
    pltpu.VMEM((3, 8, 512), F32),
    pltpu.VMEM((256, 256), BF16),
    pltpu.VMEM((16, 8, 512), F32),
    pltpu.VMEM((16, 8, 512), F32),
    pltpu.VMEM((16, 8, 512), F32),
]


def landed(ref, sem):
    pltpu.make_async_copy(ref, ref, sem).wait()


def step(
    send_ref, params_ref, lists_ref, order_ref, where_ref, live_ref, target_ref, camera_ref, out_ref,
    pick, image_of, par3, shown3, owner3, listed, sort, place, tri, tile3, coef3, grad3,
    cam_row, cams, shown_out, shown_mid, shown_in, back_out, back_mid, back_in, send_sems, recv_sems, own_sem,
):
    i = lax.axis_index("img")
    j = lax.axis_index("dev")
    mesh_ids = pl.DeviceIdType.MESH

    barrier = pltpu.get_barrier_semaphore()
    for s in range(1, 8):
        pl.semaphore_signal(barrier, inc=1, device_id=(lax.rem(i + s, 8), j), device_id_type=mesh_ids)

    @pl.loop(1, 64)
    def _(s):
        pl.semaphore_signal(barrier, inc=1, device_id=(i, lax.rem(j + s, 64)), device_id_type=mesh_ids)

    cam_row[...] = jnp.zeros((8, 128), F32)
    cam_row[0:1, 0:12] = camera_ref[...]
    owner_tables(send_ref, params_ref, pick, image_of, par3)
    pl.semaphore_wait(barrier, 70)

    def to_img(source, target, phase):
        for s in range(1, 8):
            t = lax.rem(i + s, 8)
            pltpu.make_async_remote_copy(
                src_ref=source(t),
                dst_ref=target,
                send_sem=send_sems.at[phase],
                recv_sem=recv_sems.at[phase],
                device_id=(t, j),
                device_id_type=mesh_ids,
            ).start()
        own = pltpu.make_async_copy(source(i), target, own_sem)
        own.start()
        own.wait()

    def to_dev(source, target, phase):
        def one(s, carry):
            t = lax.rem(j + s, 64)
            pltpu.make_async_remote_copy(
                src_ref=source.at[:, t, :],
                dst_ref=target.at[:, j, :],
                send_sem=send_sems.at[phase],
                recv_sem=recv_sems.at[phase],
                device_id=(i, t),
                device_id_type=mesh_ids,
            ).start()
            return carry

        lax.fori_loop(1, 64, one, 0)
        own = pltpu.make_async_copy(source.at[:, j, :], target.at[:, j, :], own_sem)
        own.start()
        own.wait()

    to_img(lambda t: cam_row.at[pl.ds(0, 1)], cams.at[pl.ds(i, 1)], 0)
    landed(cams.at[pl.ds(0, 7)], recv_sems.at[0])

    def put_shown(x):
        shown_out[...] = x.reshape(8, 64, 128)

    owner_forward(cams, pick, image_of, par3, shown3, put_shown)
    to_img(lambda t: shown_out.at[t], shown_mid.at[i], 1)
    renderer_tables(lists_ref, order_ref, where_ref, live_ref, listed, sort, place, tri)
    landed(shown_mid.at[pl.ds(0, 7)], recv_sems.at[1])
    to_dev(shown_mid, shown_in, 2)
    landed(shown_in.at[:, pl.ds(0, 63), :], recv_sems.at[2])

    def put_back(x):
        back_out[...] = x.reshape(8, 64, 128)

    render(shown_in[...].reshape(512, 128), listed, sort, place, tri, target_ref, tile3, coef3, grad3, put_back)
    to_dev(back_out, back_mid, 3)
    landed(back_mid.at[:, pl.ds(0, 63), :], recv_sems.at[3])
    to_img(lambda t: back_mid.at[t], back_in.at[i], 4)
    landed(back_in.at[pl.ds(0, 7)], recv_sems.at[4])
    owner_gradient(back_in[...].reshape(512, 128), cams, pick, image_of, par3, shown3, owner3)
    for g in range(8):
        out_ref[:, 256 * g:256 * (g + 1)] = owner3[:, g, :]
    landed(cams.at[pl.ds(0, 7)], send_sems.at[0])
    landed(shown_out.at[pl.ds(0, 7)], send_sems.at[1])
    landed(shown_mid.at[:, pl.ds(0, 63), :], send_sems.at[2])
    landed(back_out.at[:, pl.ds(0, 63), :], send_sems.at[3])
    landed(back_mid.at[pl.ds(0, 7)], send_sems.at[4])


def local(
    params, first_moment, second_moment, send_blocks, tile_blocks, tile_live, depth_order, tile_where, target, camera
):
    vmem = pl.BlockSpec(memory_space=pltpu.VMEM)
    smem = pl.BlockSpec(memory_space=pltpu.SMEM)
    block = pltpu.VMEM((8, 64, 128), F32)
    gradient = pl.pallas_call(
        step,
        out_shape=jax.ShapeDtypeStruct((59, 2048), F32),
        in_specs=[vmem, vmem, vmem, vmem, smem, smem, vmem, vmem],
        out_specs=vmem,
        scratch_shapes=OWNER_SCRATCH
        + [pltpu.VMEM((59, 8, 256), F32)]
        + RENDER_SCRATCH
        + [pltpu.VMEM((8, 128), F32)] * 2
        + [block] * 6
        + [pltpu.SemaphoreType.DMA((5,)), pltpu.SemaphoreType.DMA((5,)), pltpu.SemaphoreType.DMA],
        compiler_params=pltpu.CompilerParams(collective_id=0, has_side_effects=True, vmem_limit_bytes=40 << 20),
    )(
        send_blocks,
        params,
        tile_blocks.reshape(1, 512),
        depth_order.reshape(8, 256),
        tile_where,
        tile_live,
        target.reshape(8, 768),
        camera,
    )
    new_first = 0.9 * first_moment + 0.1 * gradient
    new_second = 0.999 * second_moment + 0.001 * gradient * gradient
    new_params = params - rate_column() * new_first / (jnp.sqrt(new_second) + 1e-15)
    return new_params, new_first, new_second


def solution(mesh):
    return jax.shard_map(
        local,
        mesh=mesh,
        in_specs=(
            P(None, ("img", "dev")),
            P(None, ("img", "dev")),
            P(None, ("img", "dev")),
            P(("img", "dev"), None),
            P("img", "dev", None),
            P("img", "dev"),
            P("img", "dev", None),
            P("img", "dev"),
            P("img", "dev", None),
            P("img", None),
        ),
        out_specs=(P(None, ("img", "dev")), P(None, ("img", "dev")), P(None, ("img", "dev"))),
        check_vma=False,
    )
```

```python
import functools

import jax
import jax.numpy as jnp
from jax import lax
from jax.experimental import pallas as pl
from jax.experimental.pallas import tpu as pltpu
from jax.sharding import PartitionSpec as P

F32, BF16 = jnp.float32, jnp.bfloat16
LOG2E = 1.4426950408889634
FOCAL = 1024.0
CENTRE_U, CENTRE_V = 256.0, 128.0

HARMONIC_ZERO = 0.28209479177387814
HARMONIC_ONE = 0.4886025119029199
HARMONIC_TWO = (
    1.0925484305920792,
    -1.0925484305920792,
    0.31539156525252005,
    -1.0925484305920792,
    0.5462742152960396,
)
HARMONIC_THREE = (
    -0.5900435899266435,
    2.890611442640554,
    -0.4570457994644658,
    0.3731763325901154,
    -0.4570457994644658,
    1.445305721320277,
    -0.5900435899266435,
)


def harmonics(dir_x, dir_y, dir_z):
    square_x = dir_x * dir_x
    square_y = dir_y * dir_y
    square_z = dir_z * dir_z
    return [
        -HARMONIC_ONE * dir_y,
        HARMONIC_ONE * dir_z,
        -HARMONIC_ONE * dir_x,
        HARMONIC_TWO[0] * dir_x * dir_y,
        HARMONIC_TWO[1] * dir_y * dir_z,
        HARMONIC_TWO[2] * (2.0 * square_z - square_x - square_y),
        HARMONIC_TWO[3] * dir_x * dir_z,
        HARMONIC_TWO[4] * (square_x - square_y),
        HARMONIC_THREE[0] * dir_y * (3.0 * square_x - square_y),
        HARMONIC_THREE[1] * dir_x * dir_y * dir_z,
        HARMONIC_THREE[2] * dir_y * (4.0 * square_z - square_x - square_y),
        HARMONIC_THREE[3] * dir_z * (2.0 * square_z - 3.0 * square_x - 3.0 * square_y),
        HARMONIC_THREE[4] * dir_x * (4.0 * square_z - square_x - square_y),
        HARMONIC_THREE[5] * dir_z * (square_x - square_y),
        HARMONIC_THREE[6] * dir_x * (square_x - 3.0 * square_y),
    ]


def project(values, cam):
    m = [[cam[3 * r + c] for c in range(3)] for r in range(3)]
    viewed = [m[r][0] * values[0] + m[r][1] * values[1] + m[r][2] * values[2] + cam[9 + r] for r in range(3)]
    inverse_z = 1.0 / viewed[2]
    centre_u = FOCAL * viewed[0] * inverse_z + CENTRE_U
    centre_v = FOCAL * viewed[1] * inverse_z + CENTRE_V
    scales = [jnp.exp(values[3 + c]) for c in range(3)]
    norm = jnp.sqrt(values[6] * values[6] + values[7] * values[7] + values[8] * values[8] + values[9] * values[9])
    inverse_norm = 1.0 / norm
    w, x, y, z = (values[6 + c] * inverse_norm for c in range(4))
    rot = [
        [1.0 - 2.0 * (y * y + z * z), 2.0 * (x * y - w * z), 2.0 * (x * z + w * y)],
        [2.0 * (x * y + w * z), 1.0 - 2.0 * (x * x + z * z), 2.0 * (y * z - w * x)],
        [2.0 * (x * z - w * y), 2.0 * (y * z + w * x), 1.0 - 2.0 * (x * x + y * y)],
    ]
    focal_z = FOCAL * inverse_z
    jac = [[focal_z * (m[r][c] - viewed[r] * inverse_z * m[2][c]) for c in range(3)] for r in range(2)]
    proj = [
        [(jac[r][0] * rot[0][c] + jac[r][1] * rot[1][c] + jac[r][2] * rot[2][c]) * scales[c] for c in range(3)]
        for r in range(2)
    ]
    cov_xx = proj[0][0] * proj[0][0] + proj[0][1] * proj[0][1] + proj[0][2] * proj[0][2] + 0.3
    cov_xy = proj[0][0] * proj[1][0] + proj[0][1] * proj[1][1] + proj[0][2] * proj[1][2]
    cov_yy = proj[1][0] * proj[1][0] + proj[1][1] * proj[1][1] + proj[1][2] * proj[1][2] + 0.3
    inverse_det = 1.0 / (cov_xx * cov_yy - cov_xy * cov_xy)
    log_opacity = -jnp.log(1.0 + jnp.exp(-values[10]))
    inverse_distance = 1.0 / jnp.sqrt(viewed[0] * viewed[0] + viewed[1] * viewed[1] + viewed[2] * viewed[2])
    terms = harmonics(*[viewed[c] * inverse_distance for c in range(3)])
    colour = []
    for ch in range(3):
        total = 0.5 + HARMONIC_ZERO * values[11 + ch]
        for k in range(1, 16):
            total = total + terms[k - 1] * values[11 + 3 * k + ch]
        colour.append(jnp.maximum(total, 0.0))
    return [centre_u, centre_v, cov_yy * inverse_det, -cov_xy * inverse_det, cov_xx * inverse_det, log_opacity] + colour


def iota(shape, dim):
    return lax.broadcasted_iota(jnp.int32, shape, dim)


def one_hot(truth):
    return jnp.where(truth, 1.0, 0.0).astype(BF16)


def pieces(x, count):
    out = []
    for _ in range(count - 1):
        part = x.astype(BF16)
        out.append(part)
        x = x - part.astype(F32)
    out.append(x.astype(BF16))
    return out


def nn(a, b):
    return lax.dot_general(a, b, (((1,), (0,)), ((), ())), preferred_element_type=F32)


def nt(a, b):
    return lax.dot_general(a, b, (((1,), (1,)), ((), ())), preferred_element_type=F32)


def fold(x, count):
    rows = x.shape[0] // count
    total = x[:rows]
    for c in range(1, count):
        total = total + x[c * rows:(c + 1) * rows]
    return total


def owner_tables(send_ref, pick, image_of):
    send = send_ref[...]

    def chunk(g, carry):
        lanes = pl.ds(pl.multiple_of(g * 256, 256), 256)
        pick[lanes, :] = one_hot(iota((256, 512), 0) // 4 + g * 64 == send)
        return carry

    lax.fori_loop(0, 8, chunk, 0)
    image_row = jnp.broadcast_to((iota((8, 512), 1) // 64).astype(F32), (8, 512)).astype(BF16)
    images = nt(image_row, pick[...])
    for g in range(8):
        image_of[g:g + 1, :] = images[0:1, 256 * g:256 * (g + 1)]


def cameras_of(cam_ref, image_of):
    image = image_of[...]
    masks = [image == float(i) for i in range(8)]
    cams = cam_ref[...]
    out = []
    for t in range(12):
        value = jnp.zeros((8, 256), F32)
        for i in range(8):
            value = jnp.where(masks[i], cams[i:i + 1, t:t + 1], value)
        out.append(value)
    return out


def owner_forward(cam_ref, pick, image_of, par3, shown3, put):
    shown = project([par3[c] for c in range(59)], cameras_of(cam_ref, image_of))
    for q in range(9):
        shown3[q] = shown[q]
    for q in range(9, 16):
        shown3[q] = jnp.zeros((8, 256), F32)
    within = iota((16, 256), 1) % 4
    total = jnp.zeros((192, 512), F32)
    for g in range(8):
        rows = []
        for b in range(4):
            rows.append(jnp.where(within == b, shown3[:, g, :], 0.0))
        rows = jnp.concatenate(rows, axis=0)
        total = total + nn(jnp.concatenate(pieces(rows, 3), axis=0), pick[256 * g:256 * (g + 1), :])
    sums = fold(total, 3)
    put(jnp.transpose(jnp.concatenate([sums, jnp.zeros((64, 512), F32)], axis=0)))


def owner_gradient(got, cam_ref, pick, image_of, par3, shown3, grad3):
    rows = jnp.transpose(got)[0:64]
    parts = jnp.concatenate(pieces(rows, 3), axis=0)
    within = iota((16, 256), 1) % 4
    for g in range(8):
        spread = fold(nt(parts, pick[256 * g:256 * (g + 1), :]), 3)
        total = jnp.zeros((16, 256), F32)
        for b in range(4):
            total = total + jnp.where(within == b, spread[16 * b:16 * (b + 1)], 0.0)
        shown3[:, g, :] = total
    values = [par3[c] for c in range(59)]
    cams = cameras_of(cam_ref, image_of)
    _, pullback = jax.vjp(lambda v: project(v, cams), values)
    (grads,) = pullback([shown3[q] for q in range(9)])
    for c in range(59):
        grad3[c] = grads[c]


def renderer_tables(lists_ref, order_ref, where_ref, live_ref, target_ref, listed, sort, place, tri, wanted):
    listed[...] = one_hot(iota((512, 512), 0) == lists_ref[...])

    def one_tile(n, carry):
        order = order_ref[pl.ds(n, 1), :]
        key = (order % 4) * 128 + (n % 2) * 64 + order // 4
        sort[n] = one_hot(iota((512, 256), 0) == key)
        return carry

    lax.fori_loop(0, 8, one_tile, 0)
    lane = iota((8, 512), 1)
    tile = lane // 64
    where = jnp.zeros((8, 512), jnp.int32)
    live = jnp.zeros((8, 512), jnp.int32)
    for n in range(8):
        where = jnp.where(tile == n, where_ref[0:1, n:n + 1], where)
        live = jnp.where(tile == n, live_ref[0:1, n:n + 1], live)
    place[0] = (where % 32 * 16 + 8).astype(F32)
    place[1] = (where // 32 * 16 + 8).astype(F32)
    place[2] = jnp.where(lane % 64 < live, 1.0, 0.0)
    tri[0] = one_hot(iota((256, 256), 0) < iota((256, 256), 1))
    tri[1] = one_hot(iota((256, 256), 0) > iota((256, 256), 1))
    for n in range(8):
        rows = [target_ref[n:n + 1, 256 * ch:256 * (ch + 1)] for ch in range(3)]
        wanted[n] = jnp.transpose(jnp.concatenate(rows + [jnp.zeros((125, 256), F32)], axis=0))[:, 0:8]


def monomials(pixel, term):
    x = (pixel % 16).astype(F32) - 7.5
    y = (pixel // 16).astype(F32) - 7.5
    out = jnp.zeros(pixel.shape, F32)
    for t, value in enumerate((jnp.ones_like(x), x, y, x * x, x * y, y * y)):
        out = jnp.where(term == t, value, out)
    return out.astype(BF16)


def render(got, listed, sort, place, tri, wanted, tile3, coef3, grad3, front3, alpha3, weight3, high3, low3, put):
    rows = jnp.transpose(got)[0:64]
    tiles = fold(nn(jnp.concatenate(pieces(rows, 3), axis=0), listed[...]), 3)
    for b in range(4):
        tile3[:, b, :] = tiles[16 * b:16 * (b + 1)]
    centre_x, centre_y, live = place[0, 0:4], place[1, 0:4], place[2, 0:4]

    def geometry():
        u, v, cxx, cxy, cyy, log_op = (tile3[q, 0:4] for q in range(6))
        return u - centre_x, v - centre_y, cxx, cxy, cyy, log_op

    u, v, cxx, cxy, cyy, log_op = geometry()
    a, b2, c2 = -0.5 * LOG2E * cxx, -LOG2E * cxy, -0.5 * LOG2E * cyy
    constant = a * u * u + b2 * u * v + c2 * v * v + LOG2E * log_op
    coefs = [
        jnp.where(live > 0.0, constant, -1e5),
        jnp.where(live > 0.0, -2.0 * a * u - b2 * v, 0.0),
        jnp.where(live > 0.0, -2.0 * c2 * v - b2 * u, 0.0),
        jnp.where(live > 0.0, a, 0.0),
        jnp.where(live > 0.0, b2, 0.0),
        jnp.where(live > 0.0, c2, 0.0),
    ] + [tile3[q, 0:4] for q in range(6, 9)]
    for c in range(9):
        coef3[c, 0:4] = coefs[c]
    for c in range(9, 16):
        coef3[c, 0:4] = jnp.zeros((4, 512), F32)
    grad3[...] = jnp.zeros(grad3.shape, F32)
    power = monomials(iota((256, 48), 0), iota((256, 48), 1) % 16)
    column = iota((16, 256), 0).astype(F32) - 7.5
    zero8 = jnp.zeros((8, 256), F32)

    for n in range(8):
        pair = slice(128 * (n // 2), 128 * (n // 2) + 128)
        mine = jnp.concatenate([coef3[:, b, pair] for b in range(4)], axis=1)
        sorted_parts = nn(jnp.concatenate(pieces(mine, 3), axis=0), sort[n])
        front = fold(sorted_parts, 3)
        front3[n] = jnp.where(iota((8, 256), 0) < 3, pltpu.roll(front, 10, 0)[0:8], 0.0)
        alpha = jnp.exp2(nn(power, sorted_parts.astype(BF16)))
        alpha3[n] = alpha
        high3[n], low3[n] = pieces(jnp.log(1.0 - alpha), 2)
    for n in range(8):
        weight = jnp.exp(nn(high3[n], tri[0]) + nn(low3[n], tri[0])) * alpha3[n]
        weight3[n] = weight
        high3[n], low3[n] = pieces(weight, 2)
    for n in range(8):
        colour = front3[n]
        c_all = jnp.concatenate(pieces(colour, 2), axis=0)
        both = nt(high3[n], c_all) + nt(low3[n], c_all)
        residual = both[:, 0:8] + both[:, 8:16] - wanted[n]
        weight = weight3[n]
        gain = jnp.zeros((256, 256), F32)
        shades = []
        for ch in range(3):
            gain = gain + residual[:, ch:ch + 1] * colour[ch:ch + 1]
            shades.append(jnp.sum(residual[:, ch:ch + 1] * weight, axis=0, keepdims=True))
        passed = weight * gain
        weight3[n] = passed
        high3[n], low3[n] = pieces(passed, 2)
        front3[n] = jnp.concatenate(shades + [zero8[0:5]], axis=0)
    for n in range(8):
        alpha = alpha3[n]
        keep = 1.0 - alpha
        guess = pl.reciprocal(keep, approx=True)
        inverse = guess * (2.0 - keep * guess)
        behind = nn(high3[n], tri[1]) + nn(low3[n], tri[1])
        change = (weight3[n] - behind * (alpha * inverse)).reshape(16, 16, 256)
        s0, s1, s2 = change[0], -7.5 * change[0], 56.25 * change[0]
        for y in range(1, 16):
            s0 = s0 + change[y]
            s1 = s1 + (y - 7.5) * change[y]
            s2 = s2 + (y - 7.5) * (y - 7.5) * change[y]
        moments = [s0, s0 * column, s1, s0 * column * column, s1 * column, s2]
        back = jnp.concatenate([jnp.sum(m, axis=0, keepdims=True) for m in moments] + [zero8[0:2], front3[n]], axis=0)
        pair = slice(128 * (n // 2), 128 * (n // 2) + 128)
        spread = fold(nt(jnp.concatenate(pieces(back, 3), axis=0), sort[n]), 3)
        for b in range(4):
            grad3[:, b, pair] += spread[:, 128 * b:128 * (b + 1)]

    m0, mx, my, mxx, mxy, myy = (grad3[t, 0:4] for t in range(6))
    u, v, cxx, cxy, cyy, _ = geometry()
    hx, hy = mx - u * m0, my - v * m0
    hxx = mxx - 2.0 * u * mx + u * u * m0
    hxy = mxy - u * my - v * mx + u * v * m0
    hyy = myy - 2.0 * v * my + v * v * m0
    results = [cxx * hx + cxy * hy, cxy * hx + cyy * hy, -0.5 * hxx, -hxy, -0.5 * hyy, m0]
    results += [grad3[8 + ch, 0:4] for ch in range(3)]
    for q in range(9):
        tile3[q, 0:4] = results[q]
    for q in range(9, 16):
        tile3[q, 0:4] = jnp.zeros((4, 512), F32)
    rows = jnp.concatenate([tile3[:, b, :] for b in range(4)], axis=0)
    out = fold(nt(jnp.concatenate(pieces(rows, 3), axis=0), listed[...]), 3)
    put(jnp.transpose(jnp.concatenate([out, jnp.zeros((64, 512), F32)], axis=0)))


def rate_column():
    row = iota((59, 1), 0)
    rate = jnp.full((59, 1), 0.000125, F32)
    for end, value in ((14, 0.0025), (11, 0.05), (10, 0.001), (6, 0.005), (3, 0.00016)):
        rate = jnp.where(row < end, value, rate)
    return rate


def adam(grad3, params_ref, first_ref, second_ref, new_params, new_first, new_second):
    rate = rate_column()
    for g in range(8):
        at = slice(256 * g, 256 * (g + 1))
        gradient = grad3[:, g, :]
        first = 0.9 * first_ref[:, at] + 0.1 * gradient
        second = 0.999 * second_ref[:, at] + 0.001 * gradient * gradient
        new_first[:, at] = first
        new_second[:, at] = second
        new_params[:, at] = params_ref[:, at] - rate * first / (jnp.sqrt(second) + 1e-15)


OWNER_SCRATCH = [
    pltpu.VMEM((2048, 512), BF16),
    pltpu.VMEM((8, 256), F32),
    pltpu.VMEM((59, 8, 256), F32),
    pltpu.VMEM((16, 8, 256), F32),
]
RENDER_SCRATCH = [
    pltpu.VMEM((512, 512), BF16),
    pltpu.VMEM((8, 512, 256), BF16),
    pltpu.VMEM((3, 8, 512), F32),
    pltpu.VMEM((2, 256, 256), BF16),
    pltpu.VMEM((8, 256, 8), F32),
    pltpu.VMEM((16, 8, 512), F32),
    pltpu.VMEM((16, 8, 512), F32),
    pltpu.VMEM((16, 8, 512), F32),
    pltpu.VMEM((8, 8, 256), F32),
    pltpu.VMEM((8, 256, 256), F32),
    pltpu.VMEM((8, 256, 256), F32),
    pltpu.VMEM((8, 256, 256), BF16),
    pltpu.VMEM((8, 256, 256), BF16),
]


def landed(ref, sem):
    pltpu.make_async_copy(ref, ref, sem).wait()


def step(
    params_hbm, send_hbm, lists_hbm, order_hbm, where_hbm, live_hbm, target_hbm, camera_hbm, out_ref,
    send_ref, lists_ref, order_ref, where_ref, live_ref, target_ref, camera_ref, in_sems,
    pick, image_of, par3, shown3, owner3,
    listed, sort, place, tri, wanted, tile3, coef3, grad3, front3, alpha3, weight3, high3, low3,
    cam_row, cams, shown_out, shown_mid, shown_in, back_out, back_mid, back_in, send_sems, recv_sems, own_sem,
):
    i = lax.axis_index("img")
    j = lax.axis_index("dev")
    mesh_ids = pl.DeviceIdType.MESH

    loads = [
        pltpu.make_async_copy(source, target, in_sems.at[c])
        for c, (source, target) in enumerate(
            [(camera_hbm, camera_ref), (send_hbm, send_ref)]
            + [(params_hbm.at[:, pl.ds(256 * g, 256)], par3.at[:, g, :]) for g in range(8)]
            + [(lists_hbm, lists_ref), (order_hbm, order_ref), (where_hbm, where_ref), (live_hbm, live_ref)]
            + [(target_hbm, target_ref)]
        )
    ]
    for load in loads:
        load.start()

    barrier = pltpu.get_barrier_semaphore()
    for s in range(1, 8):
        pl.semaphore_signal(barrier, inc=1, device_id=(lax.rem(i + s, 8), j), device_id_type=mesh_ids)

    @pl.loop(1, 64)
    def _(s):
        pl.semaphore_signal(barrier, inc=1, device_id=(i, lax.rem(j + s, 64)), device_id_type=mesh_ids)

    cam_row[...] = jnp.zeros((8, 128), F32)
    loads[0].wait()
    cam_row[0:1, 0:12] = camera_ref[...]
    loads[1].wait()
    owner_tables(send_ref, pick, image_of)
    pl.semaphore_wait(barrier, 70)

    def to_img(source, target, phase):
        for s in range(1, 8):
            t = lax.rem(i + s, 8)
            pltpu.make_async_remote_copy(
                src_ref=source(t),
                dst_ref=target,
                send_sem=send_sems.at[phase],
                recv_sem=recv_sems.at[phase],
                device_id=(t, j),
                device_id_type=mesh_ids,
            ).start()
        own = pltpu.make_async_copy(source(i), target, own_sem)
        own.start()
        own.wait()

    def to_dev(source, target, phase):
        def one(s, carry):
            t = lax.rem(j + s, 64)
            pltpu.make_async_remote_copy(
                src_ref=source.at[:, t, :],
                dst_ref=target.at[:, j, :],
                send_sem=send_sems.at[phase],
                recv_sem=recv_sems.at[phase],
                device_id=(i, t),
                device_id_type=mesh_ids,
            ).start()
            return carry

        lax.fori_loop(1, 64, one, 0)
        own = pltpu.make_async_copy(source.at[:, j, :], target.at[:, j, :], own_sem)
        own.start()
        own.wait()

    to_img(lambda t: cam_row.at[pl.ds(0, 1)], cams.at[pl.ds(i, 1)], 0)
    landed(cams.at[pl.ds(0, 7)], recv_sems.at[0])

    def put_shown(x):
        shown_out[...] = x.reshape(8, 64, 128)

    for load in loads[2:10]:
        load.wait()
    owner_forward(cams, pick, image_of, par3, shown3, put_shown)
    to_img(lambda t: shown_out.at[t], shown_mid.at[i], 1)
    for load in loads[10:]:
        load.wait()
    renderer_tables(lists_ref, order_ref, where_ref, live_ref, target_ref, listed, sort, place, tri, wanted)
    landed(shown_mid.at[pl.ds(0, 7)], recv_sems.at[1])
    to_dev(shown_mid, shown_in, 2)
    landed(shown_in.at[:, pl.ds(0, 63), :], recv_sems.at[2])

    def put_back(x):
        back_out[...] = x.reshape(8, 64, 128)

    render(
        shown_in[...].reshape(512, 128),
        listed, sort, place, tri, wanted, tile3, coef3, grad3, front3, alpha3, weight3, high3, low3,
        put_back,
    )
    to_dev(back_out, back_mid, 3)
    landed(back_mid.at[:, pl.ds(0, 63), :], recv_sems.at[3])
    to_img(lambda t: back_mid.at[t], back_in.at[i], 4)
    landed(back_in.at[pl.ds(0, 7)], recv_sems.at[4])
    owner_gradient(back_in[...].reshape(512, 128), cams, pick, image_of, par3, shown3, owner3)
    for g in range(8):
        out_ref[:, 256 * g:256 * (g + 1)] = owner3[:, g, :]
    landed(cams.at[pl.ds(0, 7)], send_sems.at[0])
    landed(shown_out.at[pl.ds(0, 7)], send_sems.at[1])
    landed(shown_mid.at[:, pl.ds(0, 63), :], send_sems.at[2])
    landed(back_out.at[:, pl.ds(0, 63), :], send_sems.at[3])
    landed(back_mid.at[pl.ds(0, 7)], send_sems.at[4])


def local(
    params, first_moment, second_moment, send_blocks, tile_blocks, tile_live, depth_order, tile_where, target, camera
):
    vmem = pl.BlockSpec(memory_space=pltpu.VMEM)
    whole = pl.BlockSpec(memory_space=pl.ANY)
    integer = jnp.int32
    block = pltpu.VMEM((8, 64, 128), F32)
    gradient = pl.pallas_call(
        step,
        out_shape=jax.ShapeDtypeStruct((59, 2048), F32),
        in_specs=[whole] * 8,
        out_specs=vmem,
        scratch_shapes=[
            pltpu.VMEM((1, 512), integer),
            pltpu.VMEM((1, 512), integer),
            pltpu.VMEM((8, 256), integer),
            pltpu.VMEM((1, 8), integer),
            pltpu.VMEM((1, 8), integer),
            pltpu.VMEM((8, 768), F32),
            pltpu.VMEM((1, 12), F32),
            pltpu.SemaphoreType.DMA((15,)),
        ]
        + OWNER_SCRATCH
        + [pltpu.VMEM((59, 8, 256), F32)]
        + RENDER_SCRATCH
        + [pltpu.VMEM((8, 128), F32)] * 2
        + [block] * 6
        + [pltpu.SemaphoreType.DMA((5,)), pltpu.SemaphoreType.DMA((5,)), pltpu.SemaphoreType.DMA],
        compiler_params=pltpu.CompilerParams(collective_id=0, has_side_effects=True, vmem_limit_bytes=56 << 20),
    )(
        params,
        send_blocks,
        tile_blocks.reshape(1, 512),
        depth_order.reshape(8, 256),
        tile_where,
        tile_live,
        target.reshape(8, 768),
        camera,
    )
    new_first = 0.9 * first_moment + 0.1 * gradient
    new_second = 0.999 * second_moment + 0.001 * gradient * gradient
    new_params = params - rate_column() * new_first / (jnp.sqrt(new_second) + 1e-15)
    return new_params, new_first, new_second


def solution(mesh):
    return jax.shard_map(
        local,
        mesh=mesh,
        in_specs=(
            P(None, ("img", "dev")),
            P(None, ("img", "dev")),
            P(None, ("img", "dev")),
            P(("img", "dev"), None),
            P("img", "dev", None),
            P("img", "dev"),
            P("img", "dev", None),
            P("img", "dev"),
            P("img", "dev", None),
            P("img", None),
        ),
        out_specs=(P(None, ("img", "dev")), P(None, ("img", "dev")), P(None, ("img", "dev"))),
        check_vma=False,
    )
```

```python
import functools

import jax
import jax.numpy as jnp
from jax import lax
from jax.experimental import pallas as pl
from jax.experimental.pallas import tpu as pltpu
from jax.sharding import PartitionSpec as P

F32, BF16 = jnp.float32, jnp.bfloat16
LOG2E = 1.4426950408889634
FOCAL = 1024.0
CENTRE_U, CENTRE_V = 256.0, 128.0

HARMONIC_ZERO = 0.28209479177387814
HARMONIC_ONE = 0.4886025119029199
HARMONIC_TWO = (
    1.0925484305920792,
    -1.0925484305920792,
    0.31539156525252005,
    -1.0925484305920792,
    0.5462742152960396,
)
HARMONIC_THREE = (
    -0.5900435899266435,
    2.890611442640554,
    -0.4570457994644658,
    0.3731763325901154,
    -0.4570457994644658,
    1.445305721320277,
    -0.5900435899266435,
)


def harmonics(dir_x, dir_y, dir_z):
    square_x = dir_x * dir_x
    square_y = dir_y * dir_y
    square_z = dir_z * dir_z
    return [
        -HARMONIC_ONE * dir_y,
        HARMONIC_ONE * dir_z,
        -HARMONIC_ONE * dir_x,
        HARMONIC_TWO[0] * dir_x * dir_y,
        HARMONIC_TWO[1] * dir_y * dir_z,
        HARMONIC_TWO[2] * (2.0 * square_z - square_x - square_y),
        HARMONIC_TWO[3] * dir_x * dir_z,
        HARMONIC_TWO[4] * (square_x - square_y),
        HARMONIC_THREE[0] * dir_y * (3.0 * square_x - square_y),
        HARMONIC_THREE[1] * dir_x * dir_y * dir_z,
        HARMONIC_THREE[2] * dir_y * (4.0 * square_z - square_x - square_y),
        HARMONIC_THREE[3] * dir_z * (2.0 * square_z - 3.0 * square_x - 3.0 * square_y),
        HARMONIC_THREE[4] * dir_x * (4.0 * square_z - square_x - square_y),
        HARMONIC_THREE[5] * dir_z * (square_x - square_y),
        HARMONIC_THREE[6] * dir_x * (square_x - 3.0 * square_y),
    ]


def project(values, cam):
    m = [[cam[3 * r + c] for c in range(3)] for r in range(3)]
    viewed = [m[r][0] * values[0] + m[r][1] * values[1] + m[r][2] * values[2] + cam[9 + r] for r in range(3)]
    inverse_z = 1.0 / viewed[2]
    centre_u = FOCAL * viewed[0] * inverse_z + CENTRE_U
    centre_v = FOCAL * viewed[1] * inverse_z + CENTRE_V
    scales = [jnp.exp(values[3 + c]) for c in range(3)]
    norm = jnp.sqrt(values[6] * values[6] + values[7] * values[7] + values[8] * values[8] + values[9] * values[9])
    inverse_norm = 1.0 / norm
    w, x, y, z = (values[6 + c] * inverse_norm for c in range(4))
    rot = [
        [1.0 - 2.0 * (y * y + z * z), 2.0 * (x * y - w * z), 2.0 * (x * z + w * y)],
        [2.0 * (x * y + w * z), 1.0 - 2.0 * (x * x + z * z), 2.0 * (y * z - w * x)],
        [2.0 * (x * z - w * y), 2.0 * (y * z + w * x), 1.0 - 2.0 * (x * x + y * y)],
    ]
    focal_z = FOCAL * inverse_z
    jac = [[focal_z * (m[r][c] - viewed[r] * inverse_z * m[2][c]) for c in range(3)] for r in range(2)]
    proj = [
        [(jac[r][0] * rot[0][c] + jac[r][1] * rot[1][c] + jac[r][2] * rot[2][c]) * scales[c] for c in range(3)]
        for r in range(2)
    ]
    cov_xx = proj[0][0] * proj[0][0] + proj[0][1] * proj[0][1] + proj[0][2] * proj[0][2] + 0.3
    cov_xy = proj[0][0] * proj[1][0] + proj[0][1] * proj[1][1] + proj[0][2] * proj[1][2]
    cov_yy = proj[1][0] * proj[1][0] + proj[1][1] * proj[1][1] + proj[1][2] * proj[1][2] + 0.3
    inverse_det = 1.0 / (cov_xx * cov_yy - cov_xy * cov_xy)
    log_opacity = -jnp.log(1.0 + jnp.exp(-values[10]))
    inverse_distance = 1.0 / jnp.sqrt(viewed[0] * viewed[0] + viewed[1] * viewed[1] + viewed[2] * viewed[2])
    terms = harmonics(*[viewed[c] * inverse_distance for c in range(3)])
    colour = []
    for ch in range(3):
        total = 0.5 + HARMONIC_ZERO * values[11 + ch]
        for k in range(1, 16):
            total = total + terms[k - 1] * values[11 + 3 * k + ch]
        colour.append(jnp.maximum(total, 0.0))
    return [centre_u, centre_v, cov_yy * inverse_det, -cov_xy * inverse_det, cov_xx * inverse_det, log_opacity] + colour


def iota(shape, dim):
    return lax.broadcasted_iota(jnp.int32, shape, dim)


def one_hot(truth):
    return jnp.where(truth, 1.0, 0.0).astype(BF16)


def pieces(x, count):
    out = []
    for _ in range(count - 1):
        part = x.astype(BF16)
        out.append(part)
        x = x - part.astype(F32)
    out.append(x.astype(BF16))
    return out


def nn(a, b):
    return lax.dot_general(a, b, (((1,), (0,)), ((), ())), preferred_element_type=F32)


def nt(a, b):
    return lax.dot_general(a, b, (((1,), (1,)), ((), ())), preferred_element_type=F32)


def paired_rows(x):
    return jnp.transpose(jnp.concatenate([x[:, 0:256], x[:, 256:512]], axis=0))


def unpaired(x):
    down = jnp.transpose(x)
    return jnp.concatenate([down[0:64], down[64:128]], axis=1)


def exchange_halves(a, b):
    first = iota(a.shape, len(a.shape) - 1) < 64
    turned_a, turned_b = pltpu.roll(a, 64, len(a.shape) - 1), pltpu.roll(b, 64, len(b.shape) - 1)
    return jnp.where(first, a, turned_b), jnp.where(first, turned_a, b)


def fold(x, count):
    rows = x.shape[0] // count
    total = x[:rows]
    for c in range(1, count):
        total = total + x[c * rows:(c + 1) * rows]
    return total


def owner_tables(send_ref, pick, image_of):
    send = send_ref[...]

    def chunk(g, carry):
        lanes = pl.ds(pl.multiple_of(g * 256, 256), 256)
        pick[lanes, :] = one_hot(iota((256, 512), 0) // 4 + g * 64 == send)
        return carry

    lax.fori_loop(0, 8, chunk, 0)
    image_row = jnp.broadcast_to((iota((8, 512), 1) // 64).astype(F32), (8, 512)).astype(BF16)
    images = nt(image_row, pick[...])
    for g in range(8):
        image_of[g:g + 1, :] = images[0:1, 256 * g:256 * (g + 1)]


def cameras_of(cam_ref, image_of):
    image = image_of[...]
    masks = [image == float(i) for i in range(8)]
    cams = cam_ref[...]
    out = []
    for t in range(12):
        value = jnp.zeros((8, 256), F32)
        for i in range(8):
            value = jnp.where(masks[i], cams[i:i + 1, t:t + 1], value)
        out.append(value)
    return out


def owner_forward(cam_ref, pick, image_of, par3, shown3, put):
    shown = project([par3[c] for c in range(59)], cameras_of(cam_ref, image_of))
    for q in range(9):
        shown3[q] = shown[q]
    for q in range(9, 16):
        shown3[q] = jnp.zeros((8, 256), F32)
    within = iota((16, 256), 1) % 4
    total = jnp.zeros((192, 512), F32)
    for g in range(8):
        rows = []
        for b in range(4):
            rows.append(jnp.where(within == b, shown3[:, g, :], 0.0))
        rows = jnp.concatenate(rows, axis=0)
        total = total + nn(jnp.concatenate(pieces(rows, 3), axis=0), pick[256 * g:256 * (g + 1), :])
    put(paired_rows(fold(total, 3)))


def owner_gradient(got, cam_ref, pick, image_of, par3, shown3, grad3):
    parts = jnp.concatenate(pieces(unpaired(got), 3), axis=0)
    within = iota((16, 256), 1) % 4
    for g in range(8):
        spread = fold(nt(parts, pick[256 * g:256 * (g + 1), :]), 3)
        total = jnp.zeros((16, 256), F32)
        for b in range(4):
            total = total + jnp.where(within == b, spread[16 * b:16 * (b + 1)], 0.0)
        shown3[:, g, :] = total
    values = [par3[c] for c in range(59)]
    cams = cameras_of(cam_ref, image_of)
    _, pullback = jax.vjp(lambda v: project(v, cams), values)
    (grads,) = pullback([shown3[q] for q in range(9)])
    for c in range(59):
        grad3[c] = grads[c]


def renderer_tables(lists_ref, order_ref, where_ref, live_ref, target_ref, listed, sort, place, tri, wanted):
    spot = iota((512, 512), 0)
    listed[...] = one_hot(spot // 32 % 8 * 64 + spot // 256 * 32 + spot % 32 == lists_ref[...])

    def one_tile(n, carry):
        order = order_ref[pl.ds(n, 1), :]
        key = (order % 4) * 128 + (n % 2) * 64 + order // 4
        sort[n] = one_hot(iota((512, 256), 0) == key)
        return carry

    lax.fori_loop(0, 8, one_tile, 0)
    lane = iota((8, 512), 1)
    tile = lane // 64
    where = jnp.zeros((8, 512), jnp.int32)
    live = jnp.zeros((8, 512), jnp.int32)
    for n in range(8):
        where = jnp.where(tile == n, where_ref[0:1, n:n + 1], where)
        live = jnp.where(tile == n, live_ref[0:1, n:n + 1], live)
    place[0] = (where % 32 * 16 + 8).astype(F32)
    place[1] = (where // 32 * 16 + 8).astype(F32)
    place[2] = jnp.where(lane % 64 < live, 1.0, 0.0)
    tri[0] = one_hot(iota((256, 256), 0) < iota((256, 256), 1))
    tri[1] = one_hot(iota((256, 256), 0) > iota((256, 256), 1))
    for n in range(8):
        rows = [target_ref[n:n + 1, 256 * ch:256 * (ch + 1)] for ch in range(3)]
        wanted[n] = jnp.transpose(jnp.concatenate(rows + [jnp.zeros((125, 256), F32)], axis=0))[:, 0:8]


def monomials(pixel, term):
    x = (pixel % 16).astype(F32) - 7.5
    y = (pixel // 16).astype(F32) - 7.5
    out = jnp.zeros(pixel.shape, F32)
    for t, value in enumerate((jnp.ones_like(x), x, y, x * x, x * y, y * y)):
        out = jnp.where(term == t, value, out)
    return out.astype(BF16)


def render(got, listed, sort, place, tri, wanted, tile3, coef3, grad3, front3, alpha3, weight3, high3, low3, put):
    rows = unpaired(got)
    tiles = fold(nn(jnp.concatenate(pieces(rows, 3), axis=0), listed[...]), 3)
    for b in range(4):
        tile3[:, b, :] = tiles[16 * b:16 * (b + 1)]
    centre_x, centre_y, live = place[0, 0:4], place[1, 0:4], place[2, 0:4]

    def geometry():
        u, v, cxx, cxy, cyy, log_op = (tile3[q, 0:4] for q in range(6))
        return u - centre_x, v - centre_y, cxx, cxy, cyy, log_op

    u, v, cxx, cxy, cyy, log_op = geometry()
    a, b2, c2 = -0.5 * LOG2E * cxx, -LOG2E * cxy, -0.5 * LOG2E * cyy
    constant = a * u * u + b2 * u * v + c2 * v * v + LOG2E * log_op
    coefs = [
        jnp.where(live > 0.0, constant, -1e5),
        jnp.where(live > 0.0, -2.0 * a * u - b2 * v, 0.0),
        jnp.where(live > 0.0, -2.0 * c2 * v - b2 * u, 0.0),
        jnp.where(live > 0.0, a, 0.0),
        jnp.where(live > 0.0, b2, 0.0),
        jnp.where(live > 0.0, c2, 0.0),
    ] + [tile3[q, 0:4] for q in range(6, 9)]
    for c in range(9):
        coef3[c, 0:4] = coefs[c]
    for c in range(9, 16):
        coef3[c, 0:4] = jnp.zeros((4, 512), F32)
    grad3[...] = jnp.zeros(grad3.shape, F32)
    power = monomials(iota((256, 48), 0), iota((256, 48), 1) % 16)
    column = iota((16, 256), 0).astype(F32) - 7.5
    zero8 = jnp.zeros((8, 256), F32)

    for n in range(8):
        pair = slice(128 * (n // 2), 128 * (n // 2) + 128)
        mine = jnp.concatenate([coef3[:, b, pair] for b in range(4)], axis=1)
        sorted_parts = nn(jnp.concatenate(pieces(mine, 3), axis=0), sort[n])
        front = fold(sorted_parts, 3)
        front3[n] = jnp.where(iota((8, 256), 0) < 3, pltpu.roll(front, 10, 0)[0:8], 0.0)
        alpha = jnp.exp2(nn(power, sorted_parts.astype(BF16)))
        alpha3[n] = alpha
        high3[n], low3[n] = pieces(jnp.log(1.0 - alpha), 2)
    for n in range(8):
        weight = jnp.exp(nn(high3[n], tri[0]) + nn(low3[n], tri[0])) * alpha3[n]
        weight3[n] = weight
        high3[n], low3[n] = pieces(weight, 2)
    for n in range(8):
        colour = front3[n]
        c_all = jnp.concatenate(pieces(colour, 2), axis=0)
        both = nt(high3[n], c_all) + nt(low3[n], c_all)
        residual = both[:, 0:8] + both[:, 8:16] - wanted[n]
        weight = weight3[n]
        gain = jnp.zeros((256, 256), F32)
        shades = []
        for ch in range(3):
            gain = gain + residual[:, ch:ch + 1] * colour[ch:ch + 1]
            shades.append(jnp.sum(residual[:, ch:ch + 1] * weight, axis=0, keepdims=True))
        passed = weight * gain
        weight3[n] = passed
        high3[n], low3[n] = pieces(passed, 2)
        front3[n] = jnp.concatenate(shades + [zero8[0:5]], axis=0)
    for n in range(8):
        alpha = alpha3[n]
        keep = 1.0 - alpha
        guess = pl.reciprocal(keep, approx=True)
        inverse = guess * (2.0 - keep * guess)
        behind = nn(high3[n], tri[1]) + nn(low3[n], tri[1])
        change = (weight3[n] - behind * (alpha * inverse)).reshape(16, 16, 256)
        s0, s1, s2 = change[0], -7.5 * change[0], 56.25 * change[0]
        for y in range(1, 16):
            s0 = s0 + change[y]
            s1 = s1 + (y - 7.5) * change[y]
            s2 = s2 + (y - 7.5) * (y - 7.5) * change[y]
        moments = [s0, s0 * column, s1, s0 * column * column, s1 * column, s2]
        back = jnp.concatenate([jnp.sum(m, axis=0, keepdims=True) for m in moments] + [zero8[0:2], front3[n]], axis=0)
        pair = slice(128 * (n // 2), 128 * (n // 2) + 128)
        spread = fold(nt(jnp.concatenate(pieces(back, 3), axis=0), sort[n]), 3)
        for b in range(4):
            grad3[:, b, pair] += spread[:, 128 * b:128 * (b + 1)]

    m0, mx, my, mxx, mxy, myy = (grad3[t, 0:4] for t in range(6))
    u, v, cxx, cxy, cyy, _ = geometry()
    hx, hy = mx - u * m0, my - v * m0
    hxx = mxx - 2.0 * u * mx + u * u * m0
    hxy = mxy - u * my - v * mx + u * v * m0
    hyy = myy - 2.0 * v * my + v * v * m0
    results = [cxx * hx + cxy * hy, cxy * hx + cyy * hy, -0.5 * hxx, -hxy, -0.5 * hyy, m0]
    results += [grad3[8 + ch, 0:4] for ch in range(3)]
    for q in range(9):
        tile3[q, 0:4] = results[q]
    for q in range(9, 16):
        tile3[q, 0:4] = jnp.zeros((4, 512), F32)
    rows = jnp.concatenate([tile3[:, b, :] for b in range(4)], axis=0)
    put(paired_rows(fold(nt(jnp.concatenate(pieces(rows, 3), axis=0), listed[...]), 3)))


def rate_column():
    row = iota((59, 1), 0)
    rate = jnp.full((59, 1), 0.000125, F32)
    for end, value in ((14, 0.0025), (11, 0.05), (10, 0.001), (6, 0.005), (3, 0.00016)):
        rate = jnp.where(row < end, value, rate)
    return rate


def adam(grad3, params_ref, first_ref, second_ref, new_params, new_first, new_second):
    rate = rate_column()
    for g in range(8):
        at = slice(256 * g, 256 * (g + 1))
        gradient = grad3[:, g, :]
        first = 0.9 * first_ref[:, at] + 0.1 * gradient
        second = 0.999 * second_ref[:, at] + 0.001 * gradient * gradient
        new_first[:, at] = first
        new_second[:, at] = second
        new_params[:, at] = params_ref[:, at] - rate * first / (jnp.sqrt(second) + 1e-15)


OWNER_SCRATCH = [
    pltpu.VMEM((2048, 512), BF16),
    pltpu.VMEM((8, 256), F32),
    pltpu.VMEM((59, 8, 256), F32),
    pltpu.VMEM((16, 8, 256), F32),
]
RENDER_SCRATCH = [
    pltpu.VMEM((512, 512), BF16),
    pltpu.VMEM((8, 512, 256), BF16),
    pltpu.VMEM((3, 8, 512), F32),
    pltpu.VMEM((2, 256, 256), BF16),
    pltpu.VMEM((8, 256, 8), F32),
    pltpu.VMEM((16, 8, 512), F32),
    pltpu.VMEM((16, 8, 512), F32),
    pltpu.VMEM((16, 8, 512), F32),
    pltpu.VMEM((8, 8, 256), F32),
    pltpu.VMEM((8, 256, 256), F32),
    pltpu.VMEM((8, 256, 256), F32),
    pltpu.VMEM((8, 256, 256), BF16),
    pltpu.VMEM((8, 256, 256), BF16),
]


def landed(ref, sem):
    pltpu.make_async_copy(ref, ref, sem).wait()


def step(
    params_hbm, send_hbm, lists_hbm, order_hbm, where_hbm, live_hbm, target_hbm, camera_hbm, out_ref,
    send_ref, lists_ref, order_ref, where_ref, live_ref, target_ref, camera_ref, in_sems,
    pick, image_of, par3, shown3, owner3,
    listed, sort, place, tri, wanted, tile3, coef3, grad3, front3, alpha3, weight3, high3, low3,
    cam_row, cams, shown_out, shown_mid, back_send, back_in, shown_send, shown_in, back_out, back_mid, send_sems, recv_sems, own_sem,
):
    i = lax.axis_index("img")
    j = lax.axis_index("dev")
    mesh_ids = pl.DeviceIdType.MESH

    barrier = pltpu.get_barrier_semaphore()
    for s in range(1, 8):
        pl.semaphore_signal(barrier, inc=1, device_id=(lax.rem(i + s, 8), j), device_id_type=mesh_ids)

    @pl.loop(1, 64)
    def _(s):
        pl.semaphore_signal(barrier, inc=1, device_id=(i, lax.rem(j + s, 64)), device_id_type=mesh_ids)

    loads = [
        pltpu.make_async_copy(source, target, in_sems.at[c])
        for c, (source, target) in enumerate(
            [(camera_hbm, camera_ref), (send_hbm, send_ref)]
            + [(params_hbm.at[:, pl.ds(256 * g, 256)], par3.at[:, g, :]) for g in range(8)]
            + [(lists_hbm, lists_ref), (order_hbm, order_ref), (where_hbm, where_ref), (live_hbm, live_ref)]
            + [(target_hbm, target_ref)]
        )
    ]
    for load in loads:
        load.start()
    cam_row[...] = jnp.zeros((8, 128), F32)
    loads[0].wait()
    cam_row[0:1, 0:12] = camera_ref[...]
    pl.semaphore_wait(barrier, 70)

    def to_img(source, target, phase):
        for s in range(1, 8):
            t = lax.rem(i + s, 8)
            pltpu.make_async_remote_copy(
                src_ref=source(t),
                dst_ref=target,
                send_sem=send_sems.at[phase],
                recv_sem=recv_sems.at[phase],
                device_id=(t, j),
                device_id_type=mesh_ids,
            ).start()
        own = pltpu.make_async_copy(source(i), target, own_sem)
        own.start()
        own.wait()

    def to_dev(source, target, phase):
        def one(s, carry):
            t = lax.rem(j + s, 64)
            pltpu.make_async_remote_copy(
                src_ref=source.at[t],
                dst_ref=target.at[j],
                send_sem=send_sems.at[phase],
                recv_sem=recv_sems.at[phase],
                device_id=(i, t),
                device_id_type=mesh_ids,
            ).start()
            return carry

        lax.fori_loop(1, 64, one, 0)
        own = pltpu.make_async_copy(source.at[j], target.at[j], own_sem)
        own.start()
        own.wait()

    to_img(lambda t: cam_row.at[pl.ds(0, 1)], cams.at[pl.ds(i, 1)], 0)
    loads[1].wait()
    owner_tables(send_ref, pick, image_of)
    landed(cams.at[pl.ds(0, 7)], recv_sems.at[0])

    def put_shown(x):
        for p in range(4):
            shown_out[:, p, :] = x[64 * p:64 * (p + 1)]

    for load in loads[2:10]:
        load.wait()
    owner_forward(cams, pick, image_of, par3, shown3, put_shown)
    to_dev(shown_out, shown_mid, 1)
    for load in loads[10:]:
        load.wait()
    renderer_tables(lists_ref, order_ref, where_ref, live_ref, target_ref, listed, sort, place, tri, wanted)
    landed(shown_mid.at[pl.ds(0, 63)], recv_sems.at[1])
    for p in range(4):
        low_half, high_half = exchange_halves(shown_mid[0:32, p, :], shown_mid[32:64, p, :])
        shown_send[p] = low_half
        shown_send[p + 4] = high_half
    to_img(lambda t: shown_send.at[t], shown_in.at[i], 2)
    landed(shown_in.at[pl.ds(0, 7)], recv_sems.at[2])

    def put_back(x):
        back_out[...] = x.reshape(8, 32, 128)

    render(
        shown_in[...].reshape(256, 128),
        listed, sort, place, tri, wanted, tile3, coef3, grad3, front3, alpha3, weight3, high3, low3,
        put_back,
    )
    to_img(lambda t: back_out.at[t], back_mid.at[i], 3)
    landed(back_mid.at[pl.ds(0, 7)], recv_sems.at[3])
    for p in range(4):
        low_half, high_half = exchange_halves(back_mid[p], back_mid[p + 4])
        back_send[0:32, p, :] = low_half
        back_send[32:64, p, :] = high_half
    to_dev(back_send, back_in, 4)
    landed(back_in.at[pl.ds(0, 63)], recv_sems.at[4])
    got = jnp.concatenate([back_in[:, p, :] for p in range(4)], axis=0)
    owner_gradient(got, cams, pick, image_of, par3, shown3, owner3)
    for g in range(8):
        out_ref[:, 256 * g:256 * (g + 1)] = owner3[:, g, :]
    landed(cams.at[pl.ds(0, 7)], send_sems.at[0])
    landed(shown_out.at[pl.ds(0, 63)], send_sems.at[1])
    landed(shown_send.at[pl.ds(0, 7)], send_sems.at[2])
    landed(back_out.at[pl.ds(0, 7)], send_sems.at[3])
    landed(back_send.at[pl.ds(0, 63)], send_sems.at[4])


def local(
    params, first_moment, second_moment, send_blocks, tile_blocks, tile_live, depth_order, tile_where, target, camera
):
    vmem = pl.BlockSpec(memory_space=pltpu.VMEM)
    whole = pl.BlockSpec(memory_space=pltpu.HBM)
    integer = jnp.int32
    by_dev = pltpu.VMEM((64, 4, 128), F32)
    by_img = pltpu.VMEM((8, 32, 128), F32)
    operands = (
        params,
        send_blocks,
        tile_blocks.reshape(1, 512),
        depth_order.reshape(8, 256),
        tile_where,
        tile_live,
        target.reshape(8, 768),
        camera,
    )
    gradient = pl.pallas_call(
        step,
        out_shape=jax.ShapeDtypeStruct((59, 2048), F32),
        in_specs=[whole] * 8,
        out_specs=vmem,
        scratch_shapes=[
            pltpu.VMEM((1, 512), integer),
            pltpu.VMEM((1, 512), integer),
            pltpu.VMEM((8, 256), integer),
            pltpu.VMEM((1, 8), integer),
            pltpu.VMEM((1, 8), integer),
            pltpu.VMEM((8, 768), F32),
            pltpu.VMEM((1, 12), F32),
            pltpu.SemaphoreType.DMA((15,)),
        ]
        + OWNER_SCRATCH
        + [pltpu.VMEM((59, 8, 256), F32)]
        + RENDER_SCRATCH
        + [pltpu.VMEM((8, 128), F32)] * 2
        + [by_dev] * 4
        + [by_img] * 4
        + [pltpu.SemaphoreType.DMA((5,)), pltpu.SemaphoreType.DMA((5,)), pltpu.SemaphoreType.DMA],
        compiler_params=pltpu.CompilerParams(collective_id=0, has_side_effects=True, vmem_limit_bytes=24 << 20),
    )(*[pltpu.with_memory_space_constraint(operand, pltpu.HBM) for operand in operands])
    new_first = 0.9 * first_moment + 0.1 * gradient
    new_second = 0.999 * second_moment + 0.001 * gradient * gradient
    new_params = params - rate_column() * new_first / (jnp.sqrt(new_second) + 1e-15)
    return new_params, new_first, new_second


def solution(mesh):
    return jax.shard_map(
        local,
        mesh=mesh,
        in_specs=(
            P(None, ("img", "dev")),
            P(None, ("img", "dev")),
            P(None, ("img", "dev")),
            P(("img", "dev"), None),
            P("img", "dev", None),
            P("img", "dev"),
            P("img", "dev", None),
            P("img", "dev"),
            P("img", "dev", None),
            P("img", None),
        ),
        out_specs=(P(None, ("img", "dev")), P(None, ("img", "dev")), P(None, ("img", "dev"))),
        check_vma=False,
    )
```

```python
import functools

import jax
import jax.numpy as jnp
from jax import lax
from jax.experimental import pallas as pl
from jax.experimental.pallas import tpu as pltpu
from jax.sharding import PartitionSpec as P

F32, BF16 = jnp.float32, jnp.bfloat16
LOG2E = 1.4426950408889634
FOCAL = 1024.0
CENTRE_U, CENTRE_V = 256.0, 128.0

HARMONIC_ZERO = 0.28209479177387814
HARMONIC_ONE = 0.4886025119029199
HARMONIC_TWO = (
    1.0925484305920792,
    -1.0925484305920792,
    0.31539156525252005,
    -1.0925484305920792,
    0.5462742152960396,
)
HARMONIC_THREE = (
    -0.5900435899266435,
    2.890611442640554,
    -0.4570457994644658,
    0.3731763325901154,
    -0.4570457994644658,
    1.445305721320277,
    -0.5900435899266435,
)


def harmonics(dir_x, dir_y, dir_z):
    square_x = dir_x * dir_x
    square_y = dir_y * dir_y
    square_z = dir_z * dir_z
    return [
        -HARMONIC_ONE * dir_y,
        HARMONIC_ONE * dir_z,
        -HARMONIC_ONE * dir_x,
        HARMONIC_TWO[0] * dir_x * dir_y,
        HARMONIC_TWO[1] * dir_y * dir_z,
        HARMONIC_TWO[2] * (2.0 * square_z - square_x - square_y),
        HARMONIC_TWO[3] * dir_x * dir_z,
        HARMONIC_TWO[4] * (square_x - square_y),
        HARMONIC_THREE[0] * dir_y * (3.0 * square_x - square_y),
        HARMONIC_THREE[1] * dir_x * dir_y * dir_z,
        HARMONIC_THREE[2] * dir_y * (4.0 * square_z - square_x - square_y),
        HARMONIC_THREE[3] * dir_z * (2.0 * square_z - 3.0 * square_x - 3.0 * square_y),
        HARMONIC_THREE[4] * dir_x * (4.0 * square_z - square_x - square_y),
        HARMONIC_THREE[5] * dir_z * (square_x - square_y),
        HARMONIC_THREE[6] * dir_x * (square_x - 3.0 * square_y),
    ]


def project(values, cam):
    m = [[cam[3 * r + c] for c in range(3)] for r in range(3)]
    viewed = [m[r][0] * values[0] + m[r][1] * values[1] + m[r][2] * values[2] + cam[9 + r] for r in range(3)]
    inverse_z = 1.0 / viewed[2]
    centre_u = FOCAL * viewed[0] * inverse_z + CENTRE_U
    centre_v = FOCAL * viewed[1] * inverse_z + CENTRE_V
    scales = [jnp.exp(values[3 + c]) for c in range(3)]
    norm = jnp.sqrt(values[6] * values[6] + values[7] * values[7] + values[8] * values[8] + values[9] * values[9])
    inverse_norm = 1.0 / norm
    w, x, y, z = (values[6 + c] * inverse_norm for c in range(4))
    rot = [
        [1.0 - 2.0 * (y * y + z * z), 2.0 * (x * y - w * z), 2.0 * (x * z + w * y)],
        [2.0 * (x * y + w * z), 1.0 - 2.0 * (x * x + z * z), 2.0 * (y * z - w * x)],
        [2.0 * (x * z - w * y), 2.0 * (y * z + w * x), 1.0 - 2.0 * (x * x + y * y)],
    ]
    focal_z = FOCAL * inverse_z
    jac = [[focal_z * (m[r][c] - viewed[r] * inverse_z * m[2][c]) for c in range(3)] for r in range(2)]
    proj = [
        [(jac[r][0] * rot[0][c] + jac[r][1] * rot[1][c] + jac[r][2] * rot[2][c]) * scales[c] for c in range(3)]
        for r in range(2)
    ]
    cov_xx = proj[0][0] * proj[0][0] + proj[0][1] * proj[0][1] + proj[0][2] * proj[0][2] + 0.3
    cov_xy = proj[0][0] * proj[1][0] + proj[0][1] * proj[1][1] + proj[0][2] * proj[1][2]
    cov_yy = proj[1][0] * proj[1][0] + proj[1][1] * proj[1][1] + proj[1][2] * proj[1][2] + 0.3
    inverse_det = 1.0 / (cov_xx * cov_yy - cov_xy * cov_xy)
    log_opacity = -jnp.log(1.0 + jnp.exp(-values[10]))
    inverse_distance = 1.0 / jnp.sqrt(viewed[0] * viewed[0] + viewed[1] * viewed[1] + viewed[2] * viewed[2])
    terms = harmonics(*[viewed[c] * inverse_distance for c in range(3)])
    colour = []
    for ch in range(3):
        total = 0.5 + HARMONIC_ZERO * values[11 + ch]
        for k in range(1, 16):
            total = total + terms[k - 1] * values[11 + 3 * k + ch]
        colour.append(jnp.maximum(total, 0.0))
    return [centre_u, centre_v, cov_yy * inverse_det, -cov_xy * inverse_det, cov_xx * inverse_det, log_opacity] + colour


def iota(shape, dim):
    return lax.broadcasted_iota(jnp.int32, shape, dim)


def one_hot(truth):
    return jnp.where(truth, 1.0, 0.0).astype(BF16)


def pieces(x, count):
    out = []
    for _ in range(count - 1):
        part = x.astype(BF16)
        out.append(part)
        x = x - part.astype(F32)
    out.append(x.astype(BF16))
    return out


def nn(a, b):
    return lax.dot_general(a, b, (((1,), (0,)), ((), ())), preferred_element_type=F32)


def nt(a, b):
    return lax.dot_general(a, b, (((1,), (1,)), ((), ())), preferred_element_type=F32)


def paired_rows(x):
    return jnp.transpose(jnp.concatenate([x[:, 0:256], x[:, 256:512]], axis=0))


def unpaired(x):
    down = jnp.transpose(x)
    return jnp.concatenate([down[0:64], down[64:128]], axis=1)


def exchange_halves(a, b):
    first = iota(a.shape, len(a.shape) - 1) < 64
    turned_a, turned_b = pltpu.roll(a, 64, len(a.shape) - 1), pltpu.roll(b, 64, len(b.shape) - 1)
    return jnp.where(first, a, turned_b), jnp.where(first, turned_a, b)


def fold(x, count):
    rows = x.shape[0] // count
    total = x[:rows]
    for c in range(1, count):
        total = total + x[c * rows:(c + 1) * rows]
    return total


def owner_tables(send_ref, pick, image_of):
    send = send_ref[...]

    def chunk(g, carry):
        lanes = pl.ds(pl.multiple_of(g * 256, 256), 256)
        pick[lanes, :] = one_hot(iota((256, 512), 0) // 4 + g * 64 == send)
        return carry

    lax.fori_loop(0, 8, chunk, 0)
    image_row = jnp.broadcast_to((iota((8, 512), 1) // 64).astype(F32), (8, 512)).astype(BF16)
    images = nt(image_row, pick[...])
    for g in range(8):
        image_of[g:g + 1, :] = images[0:1, 256 * g:256 * (g + 1)]


def as_column(row):
    row = row.astype(F32)
    row = jnp.concatenate([row, jnp.zeros((128 - row.shape[0], row.shape[1]), F32)], axis=0)
    return jnp.transpose(row)


def owner_tables_back(send_ref, pick_back):
    send = as_column(send_ref[...])[:, 0:1].astype(jnp.int32)

    def chunk(g, carry):
        pick_back[g] = one_hot(iota((512, 256), 1) // 4 + g * 64 == send)
        return carry

    lax.fori_loop(0, 8, chunk, 0)


def cameras_of(cam_ref, image_of):
    image = image_of[...]
    masks = [image == float(i) for i in range(8)]
    cams = cam_ref[...]
    out = []
    for t in range(12):
        value = jnp.zeros((8, 256), F32)
        for i in range(8):
            value = jnp.where(masks[i], cams[i:i + 1, t:t + 1], value)
        out.append(value)
    return out


def owner_forward(cam_ref, pick, image_of, par3, shown3, put):
    shown = project([par3[c] for c in range(59)], cameras_of(cam_ref, image_of))
    for q in range(9):
        shown3[q] = shown[q]
    for q in range(9, 16):
        shown3[q] = jnp.zeros((8, 256), F32)
    within = iota((16, 256), 1) % 4
    total = jnp.zeros((192, 512), F32)
    for g in range(8):
        rows = []
        for b in range(4):
            rows.append(jnp.where(within == b, shown3[:, g, :], 0.0))
        rows = jnp.concatenate(rows, axis=0)
        total = total + nn(jnp.concatenate(pieces(rows, 3), axis=0), pick[256 * g:256 * (g + 1), :])
    put(paired_rows(fold(total, 3)))


def owner_gradient(got, cam_ref, pick_back, image_of, par3, shown3, grad3):
    parts = jnp.concatenate(pieces(unpaired(got), 2), axis=0)
    within = iota((16, 256), 1) % 4
    for g in range(8):
        spread = fold(nn(parts, pick_back[g]), 2)
        total = jnp.zeros((16, 256), F32)
        for b in range(4):
            total = total + jnp.where(within == b, spread[16 * b:16 * (b + 1)], 0.0)
        shown3[:, g, :] = total
    values = [par3[c] for c in range(59)]
    cams = cameras_of(cam_ref, image_of)
    _, pullback = jax.vjp(lambda v: project(v, cams), values)
    (grads,) = pullback([shown3[q] for q in range(9)])
    for c in range(59):
        grad3[c] = grads[c]


def renderer_tables(
    lists_ref, order_ref, where_ref, live_ref, target_ref, listed, sort, place, tri, wanted, listed_back, sort_back
):
    spot = iota((512, 512), 0)
    listed[...] = one_hot(spot // 32 % 8 * 64 + spot // 256 * 32 + spot % 32 == lists_ref[...])

    def one_tile(n, carry):
        order = order_ref[pl.ds(n, 1), :]
        key = (order % 4) * 128 + (n % 2) * 64 + order // 4
        sort[n] = one_hot(iota((512, 256), 0) == key)
        return carry

    lax.fori_loop(0, 8, one_tile, 0)
    spot = iota((512, 512), 1)
    column = as_column(lists_ref[...])[:, 0:1].astype(jnp.int32)
    listed_back[...] = one_hot(spot // 32 % 8 * 64 + spot // 256 * 32 + spot % 32 == column)
    order = order_ref[...]
    column = as_column((order % 4) * 128 + (iota((8, 256), 0) % 2) * 64 + order // 4)
    for n in range(8):
        sort_back[n] = one_hot(iota((256, 512), 1) == column[:, n:n + 1].astype(jnp.int32))
    lane = iota((8, 512), 1)
    tile = lane // 64
    where = jnp.zeros((8, 512), jnp.int32)
    live = jnp.zeros((8, 512), jnp.int32)
    for n in range(8):
        where = jnp.where(tile == n, where_ref[0:1, n:n + 1], where)
        live = jnp.where(tile == n, live_ref[0:1, n:n + 1], live)
    place[0] = (where % 32 * 16 + 8).astype(F32)
    place[1] = (where // 32 * 16 + 8).astype(F32)
    place[2] = jnp.where(lane % 64 < live, 1.0, 0.0)
    tri[0] = one_hot(iota((256, 256), 0) < iota((256, 256), 1))
    tri[1] = one_hot(iota((256, 256), 0) > iota((256, 256), 1))
    for n in range(8):
        rows = [target_ref[n:n + 1, 256 * ch:256 * (ch + 1)] for ch in range(3)]
        wanted[n] = jnp.transpose(jnp.concatenate(rows + [jnp.zeros((125, 256), F32)], axis=0))[:, 0:8]


def monomials(pixel, term):
    x = (pixel % 16).astype(F32) - 7.5
    y = (pixel // 16).astype(F32) - 7.5
    out = jnp.zeros(pixel.shape, F32)
    for t, value in enumerate((jnp.ones_like(x), x, y, x * x, x * y, y * y)):
        out = jnp.where(term == t, value, out)
    return out.astype(BF16)


def render(
    got, listed, sort, place, tri, wanted, listed_back, sort_back, tile3, coef3, grad3, front3, alpha3, weight3, high3, low3, put
):
    rows = unpaired(got)
    tiles = fold(nn(jnp.concatenate(pieces(rows, 3), axis=0), listed[...]), 3)
    for b in range(4):
        tile3[:, b, :] = tiles[16 * b:16 * (b + 1)]
    centre_x, centre_y, live = place[0, 0:4], place[1, 0:4], place[2, 0:4]

    def geometry():
        u, v, cxx, cxy, cyy, log_op = (tile3[q, 0:4] for q in range(6))
        return u - centre_x, v - centre_y, cxx, cxy, cyy, log_op

    u, v, cxx, cxy, cyy, log_op = geometry()
    a, b2, c2 = -0.5 * LOG2E * cxx, -LOG2E * cxy, -0.5 * LOG2E * cyy
    constant = a * u * u + b2 * u * v + c2 * v * v + LOG2E * log_op
    coefs = [
        jnp.where(live > 0.0, constant, -1e5),
        jnp.where(live > 0.0, -2.0 * a * u - b2 * v, 0.0),
        jnp.where(live > 0.0, -2.0 * c2 * v - b2 * u, 0.0),
        jnp.where(live > 0.0, a, 0.0),
        jnp.where(live > 0.0, b2, 0.0),
        jnp.where(live > 0.0, c2, 0.0),
    ] + [tile3[q, 0:4] for q in range(6, 9)]
    for c in range(9):
        coef3[c, 0:4] = coefs[c]
    for c in range(9, 16):
        coef3[c, 0:4] = jnp.zeros((4, 512), F32)
    grad3[...] = jnp.zeros(grad3.shape, F32)
    power = monomials(iota((256, 48), 0), iota((256, 48), 1) % 16)
    column = iota((16, 256), 0).astype(F32) - 7.5
    zero8 = jnp.zeros((8, 256), F32)

    for n in range(8):
        pair = slice(128 * (n // 2), 128 * (n // 2) + 128)
        mine = jnp.concatenate([coef3[:, b, pair] for b in range(4)], axis=1)
        sorted_parts = nn(jnp.concatenate(pieces(mine, 3), axis=0), sort[n])
        front = fold(sorted_parts, 3)
        front3[n] = jnp.where(iota((8, 256), 0) < 3, pltpu.roll(front, 10, 0)[0:8], 0.0)
        alpha = jnp.exp2(nn(power, sorted_parts.astype(BF16)))
        alpha3[n] = alpha
        high3[n], low3[n] = pieces(jnp.log(1.0 - alpha), 2)
    for n in range(8):
        weight = jnp.exp(nn(high3[n], tri[0]) + nn(low3[n], tri[0])) * alpha3[n]
        weight3[n] = weight
        high3[n], low3[n] = pieces(weight, 2)
    for n in range(8):
        colour = front3[n]
        c_all = jnp.concatenate(pieces(colour, 2), axis=0)
        both = nt(high3[n], c_all) + nt(low3[n], c_all)
        residual = both[:, 0:8] + both[:, 8:16] - wanted[n]
        weight = weight3[n]
        gain = jnp.zeros((256, 256), F32)
        shades = []
        for ch in range(3):
            gain = gain + residual[:, ch:ch + 1] * colour[ch:ch + 1]
            shades.append(jnp.sum(residual[:, ch:ch + 1] * weight, axis=0, keepdims=True))
        passed = weight * gain
        weight3[n] = passed
        high3[n], low3[n] = pieces(passed, 2)
        front3[n] = jnp.concatenate(shades + [zero8[0:5]], axis=0)
    for n in range(8):
        alpha = alpha3[n]
        keep = 1.0 - alpha
        guess = pl.reciprocal(keep, approx=True)
        inverse = guess * (2.0 - keep * guess)
        behind = nn(high3[n], tri[1]) + nn(low3[n], tri[1])
        change = (weight3[n] - behind * (alpha * inverse)).reshape(16, 16, 256)
        s0, s1, s2 = change[0], -7.5 * change[0], 56.25 * change[0]
        for y in range(1, 16):
            s0 = s0 + change[y]
            s1 = s1 + (y - 7.5) * change[y]
            s2 = s2 + (y - 7.5) * (y - 7.5) * change[y]
        moments = [s0, s0 * column, s1, s0 * column * column, s1 * column, s2]
        back = jnp.concatenate([jnp.sum(m, axis=0, keepdims=True) for m in moments] + [zero8[0:2], front3[n]], axis=0)
        pair = slice(128 * (n // 2), 128 * (n // 2) + 128)
        spread = fold(nn(jnp.concatenate(pieces(back, 3), axis=0), sort_back[n]), 3)
        for b in range(4):
            grad3[:, b, pair] += spread[:, 128 * b:128 * (b + 1)]

    m0, mx, my, mxx, mxy, myy = (grad3[t, 0:4] for t in range(6))
    u, v, cxx, cxy, cyy, _ = geometry()
    hx, hy = mx - u * m0, my - v * m0
    hxx = mxx - 2.0 * u * mx + u * u * m0
    hxy = mxy - u * my - v * mx + u * v * m0
    hyy = myy - 2.0 * v * my + v * v * m0
    results = [cxx * hx + cxy * hy, cxy * hx + cyy * hy, -0.5 * hxx, -hxy, -0.5 * hyy, m0]
    results += [grad3[8 + ch, 0:4] for ch in range(3)]
    for q in range(9):
        tile3[q, 0:4] = results[q]
    for q in range(9, 16):
        tile3[q, 0:4] = jnp.zeros((4, 512), F32)
    rows = jnp.concatenate([tile3[:, b, :] for b in range(4)], axis=0)
    put(paired_rows(fold(nn(jnp.concatenate(pieces(rows, 2), axis=0), listed_back[...]), 2)))


def rate_column():
    row = iota((59, 1), 0)
    rate = jnp.full((59, 1), 0.000125, F32)
    for end, value in ((14, 0.0025), (11, 0.05), (10, 0.001), (6, 0.005), (3, 0.00016)):
        rate = jnp.where(row < end, value, rate)
    return rate


def adam(grad3, params_ref, first_ref, second_ref, new_params, new_first, new_second):
    rate = rate_column()
    for g in range(8):
        at = slice(256 * g, 256 * (g + 1))
        gradient = grad3[:, g, :]
        first = 0.9 * first_ref[:, at] + 0.1 * gradient
        second = 0.999 * second_ref[:, at] + 0.001 * gradient * gradient
        new_first[:, at] = first
        new_second[:, at] = second
        new_params[:, at] = params_ref[:, at] - rate * first / (jnp.sqrt(second) + 1e-15)


OWNER_SCRATCH = [
    pltpu.VMEM((2048, 512), BF16),
    pltpu.VMEM((8, 256), F32),
    pltpu.VMEM((59, 8, 256), F32),
    pltpu.VMEM((16, 8, 256), F32),
    pltpu.VMEM((8, 512, 256), BF16),
]
RENDER_SCRATCH = [
    pltpu.VMEM((512, 512), BF16),
    pltpu.VMEM((8, 512, 256), BF16),
    pltpu.VMEM((3, 8, 512), F32),
    pltpu.VMEM((2, 256, 256), BF16),
    pltpu.VMEM((8, 256, 8), F32),
    pltpu.VMEM((512, 512), BF16),
    pltpu.VMEM((8, 256, 512), BF16),
    pltpu.VMEM((16, 8, 512), F32),
    pltpu.VMEM((16, 8, 512), F32),
    pltpu.VMEM((16, 8, 512), F32),
    pltpu.VMEM((8, 8, 256), F32),
    pltpu.VMEM((8, 256, 256), F32),
    pltpu.VMEM((8, 256, 256), F32),
    pltpu.VMEM((8, 256, 256), BF16),
    pltpu.VMEM((8, 256, 256), BF16),
]


def landed(ref, sem):
    pltpu.make_async_copy(ref, ref, sem).wait()


def step(
    params_hbm, send_hbm, lists_hbm, order_hbm, where_hbm, live_hbm, target_hbm, camera_hbm, first_hbm, second_hbm,
    new_params, new_first, new_second,
    send_ref, lists_ref, order_ref, where_ref, live_ref, target_ref, camera_ref, in_sems,
    pick, image_of, par3, shown3, pick_back, owner3, params_ref, first_ref, second_ref,
    listed, sort, place, tri, wanted, listed_back, sort_back, tile3, coef3, grad3, front3, alpha3, weight3, high3, low3,
    cam_row, cams, shown_out, shown_mid, back_send, back_in, shown_send, shown_in, back_out, back_mid, send_sems, recv_sems, own_sem,
):
    i = lax.axis_index("img")
    j = lax.axis_index("dev")
    mesh_ids = pl.DeviceIdType.MESH

    barrier = pltpu.get_barrier_semaphore()
    for s in range(1, 8):
        pl.semaphore_signal(barrier, inc=1, device_id=(lax.rem(i + s, 8), j), device_id_type=mesh_ids)

    @pl.loop(1, 64)
    def _(s):
        pl.semaphore_signal(barrier, inc=1, device_id=(i, lax.rem(j + s, 64)), device_id_type=mesh_ids)

    loads = [
        pltpu.make_async_copy(source, target, in_sems.at[c])
        for c, (source, target) in enumerate(
            [(camera_hbm, camera_ref), (send_hbm, send_ref)]
            + [(params_hbm.at[:, pl.ds(256 * g, 256)], par3.at[:, g, :]) for g in range(8)]
            + [(lists_hbm, lists_ref), (order_hbm, order_ref), (where_hbm, where_ref), (live_hbm, live_ref)]
            + [(target_hbm, target_ref), (params_hbm, params_ref), (first_hbm, first_ref), (second_hbm, second_ref)]
        )
    ]
    for load in loads:
        load.start()
    cam_row[...] = jnp.zeros((8, 128), F32)
    loads[0].wait()
    cam_row[0:1, 0:12] = camera_ref[...]
    pl.semaphore_wait(barrier, 70)

    def to_img(source, target, phase):
        for s in range(1, 8):
            t = lax.rem(i + s, 8)
            pltpu.make_async_remote_copy(
                src_ref=source(t),
                dst_ref=target,
                send_sem=send_sems.at[phase],
                recv_sem=recv_sems.at[phase],
                device_id=(t, j),
                device_id_type=mesh_ids,
            ).start()
        own = pltpu.make_async_copy(source(i), target, own_sem)
        own.start()
        own.wait()

    def to_dev(source, target, phase):
        def one(s, carry):
            t = lax.rem(j + s, 64)
            pltpu.make_async_remote_copy(
                src_ref=source.at[t],
                dst_ref=target.at[j],
                send_sem=send_sems.at[phase],
                recv_sem=recv_sems.at[phase],
                device_id=(i, t),
                device_id_type=mesh_ids,
            ).start()
            return carry

        lax.fori_loop(1, 64, one, 0)
        own = pltpu.make_async_copy(source.at[j], target.at[j], own_sem)
        own.start()
        own.wait()

    to_img(lambda t: cam_row.at[pl.ds(0, 1)], cams.at[pl.ds(i, 1)], 0)
    loads[1].wait()
    owner_tables(send_ref, pick, image_of)
    landed(cams.at[pl.ds(0, 7)], recv_sems.at[0])

    def put_shown(x):
        for p in range(4):
            shown_out[:, p, :] = x[64 * p:64 * (p + 1)]

    for load in loads[2:10]:
        load.wait()
    owner_forward(cams, pick, image_of, par3, shown3, put_shown)
    to_dev(shown_out, shown_mid, 1)
    for load in loads[10:]:
        load.wait()
    renderer_tables(
        lists_ref, order_ref, where_ref, live_ref, target_ref, listed, sort, place, tri, wanted, listed_back, sort_back
    )
    landed(shown_mid.at[pl.ds(0, 63)], recv_sems.at[1])
    for p in range(4):
        low_half, high_half = exchange_halves(shown_mid[0:32, p, :], shown_mid[32:64, p, :])
        shown_send[p] = low_half
        shown_send[p + 4] = high_half
    to_img(lambda t: shown_send.at[t], shown_in.at[i], 2)
    owner_tables_back(send_ref, pick_back)
    landed(shown_in.at[pl.ds(0, 7)], recv_sems.at[2])

    def put_back(x):
        back_out[...] = x.reshape(8, 32, 128)

    render(
        shown_in[...].reshape(256, 128),
        listed, sort, place, tri, wanted, listed_back, sort_back, tile3, coef3, grad3, front3, alpha3, weight3, high3, low3,
        put_back,
    )
    to_img(lambda t: back_out.at[t], back_mid.at[i], 3)
    landed(back_mid.at[pl.ds(0, 7)], recv_sems.at[3])
    for p in range(4):
        low_half, high_half = exchange_halves(back_mid[p], back_mid[p + 4])
        back_send[0:32, p, :] = low_half
        back_send[32:64, p, :] = high_half
    to_dev(back_send, back_in, 4)
    landed(back_in.at[pl.ds(0, 63)], recv_sems.at[4])
    got = jnp.concatenate([back_in[:, p, :] for p in range(4)], axis=0)
    owner_gradient(got, cams, pick_back, image_of, par3, shown3, owner3)
    adam(owner3, params_ref, first_ref, second_ref, new_params, new_first, new_second)
    landed(cams.at[pl.ds(0, 7)], send_sems.at[0])
    landed(shown_out.at[pl.ds(0, 63)], send_sems.at[1])
    landed(shown_send.at[pl.ds(0, 7)], send_sems.at[2])
    landed(back_out.at[pl.ds(0, 7)], send_sems.at[3])
    landed(back_send.at[pl.ds(0, 63)], send_sems.at[4])


def write_out(*refs):
    copies = [pltpu.make_async_copy(refs[c], refs[3 + c], refs[6].at[c]) for c in range(3)]
    for copy in copies:
        copy.start()
    for copy in copies:
        copy.wait()


def local(
    params, first_moment, second_moment, send_blocks, tile_blocks, tile_live, depth_order, tile_where, target, camera
):
    vmem = pl.BlockSpec(memory_space=pltpu.VMEM)
    whole = pl.BlockSpec(memory_space=pltpu.HBM)
    integer = jnp.int32
    by_dev = pltpu.VMEM((64, 4, 128), F32)
    by_img = pltpu.VMEM((8, 32, 128), F32)
    operands = (
        params,
        send_blocks,
        tile_blocks.reshape(1, 512),
        depth_order.reshape(8, 256),
        tile_where,
        tile_live,
        target.reshape(8, 768),
        camera,
        first_moment,
        second_moment,
    )
    shape = jax.ShapeDtypeStruct((59, 2048), F32)
    updated = pl.pallas_call(
        step,
        out_shape=(shape, shape, shape),
        in_specs=[whole] * 10,
        out_specs=(vmem, vmem, vmem),
        scratch_shapes=[
            pltpu.VMEM((1, 512), integer),
            pltpu.VMEM((1, 512), integer),
            pltpu.VMEM((8, 256), integer),
            pltpu.VMEM((1, 8), integer),
            pltpu.VMEM((1, 8), integer),
            pltpu.VMEM((8, 768), F32),
            pltpu.VMEM((1, 12), F32),
            pltpu.SemaphoreType.DMA((18,)),
        ]
        + OWNER_SCRATCH
        + [pltpu.VMEM((59, 8, 256), F32)]
        + [pltpu.VMEM((59, 2048), F32)] * 3
        + RENDER_SCRATCH
        + [pltpu.VMEM((8, 128), F32)] * 2
        + [by_dev] * 4
        + [by_img] * 4
        + [pltpu.SemaphoreType.DMA((5,)), pltpu.SemaphoreType.DMA((5,)), pltpu.SemaphoreType.DMA],
        compiler_params=pltpu.CompilerParams(collective_id=0, has_side_effects=True, vmem_limit_bytes=36 << 20),
    )(*[pltpu.with_memory_space_constraint(operand, pltpu.HBM) for operand in operands])
    return pl.pallas_call(
        write_out,
        out_shape=(shape, shape, shape),
        in_specs=[vmem] * 3,
        out_specs=(whole, whole, whole),
        scratch_shapes=[pltpu.SemaphoreType.DMA((3,))],
    )(*updated)


def solution(mesh):
    return jax.shard_map(
        local,
        mesh=mesh,
        in_specs=(
            P(None, ("img", "dev")),
            P(None, ("img", "dev")),
            P(None, ("img", "dev")),
            P(("img", "dev"), None),
            P("img", "dev", None),
            P("img", "dev"),
            P("img", "dev", None),
            P("img", "dev"),
            P("img", "dev", None),
            P("img", None),
        ),
        out_specs=(P(None, ("img", "dev")), P(None, ("img", "dev")), P(None, ("img", "dev"))),
        check_vma=False,
    )
```

```python
import functools

import jax
import jax.numpy as jnp
from jax import lax
from jax.experimental import pallas as pl
from jax.experimental.pallas import tpu as pltpu
from jax.sharding import PartitionSpec as P

F32, BF16 = jnp.float32, jnp.bfloat16
LOG2E = 1.4426950408889634
FOCAL = 1024.0
CENTRE_U, CENTRE_V = 256.0, 128.0

HARMONIC_ZERO = 0.28209479177387814
HARMONIC_ONE = 0.4886025119029199
HARMONIC_TWO = (
    1.0925484305920792,
    -1.0925484305920792,
    0.31539156525252005,
    -1.0925484305920792,
    0.5462742152960396,
)
HARMONIC_THREE = (
    -0.5900435899266435,
    2.890611442640554,
    -0.4570457994644658,
    0.3731763325901154,
    -0.4570457994644658,
    1.445305721320277,
    -0.5900435899266435,
)


def harmonics(dir_x, dir_y, dir_z):
    square_x = dir_x * dir_x
    square_y = dir_y * dir_y
    square_z = dir_z * dir_z
    return [
        -HARMONIC_ONE * dir_y,
        HARMONIC_ONE * dir_z,
        -HARMONIC_ONE * dir_x,
        HARMONIC_TWO[0] * dir_x * dir_y,
        HARMONIC_TWO[1] * dir_y * dir_z,
        HARMONIC_TWO[2] * (2.0 * square_z - square_x - square_y),
        HARMONIC_TWO[3] * dir_x * dir_z,
        HARMONIC_TWO[4] * (square_x - square_y),
        HARMONIC_THREE[0] * dir_y * (3.0 * square_x - square_y),
        HARMONIC_THREE[1] * dir_x * dir_y * dir_z,
        HARMONIC_THREE[2] * dir_y * (4.0 * square_z - square_x - square_y),
        HARMONIC_THREE[3] * dir_z * (2.0 * square_z - 3.0 * square_x - 3.0 * square_y),
        HARMONIC_THREE[4] * dir_x * (4.0 * square_z - square_x - square_y),
        HARMONIC_THREE[5] * dir_z * (square_x - square_y),
        HARMONIC_THREE[6] * dir_x * (square_x - 3.0 * square_y),
    ]


def project(values, cam):
    m = [[cam[3 * r + c] for c in range(3)] for r in range(3)]
    viewed = [m[r][0] * values[0] + m[r][1] * values[1] + m[r][2] * values[2] + cam[9 + r] for r in range(3)]
    inverse_z = 1.0 / viewed[2]
    centre_u = FOCAL * viewed[0] * inverse_z + CENTRE_U
    centre_v = FOCAL * viewed[1] * inverse_z + CENTRE_V
    scales = [jnp.exp(values[3 + c]) for c in range(3)]
    norm = jnp.sqrt(values[6] * values[6] + values[7] * values[7] + values[8] * values[8] + values[9] * values[9])
    inverse_norm = 1.0 / norm
    w, x, y, z = (values[6 + c] * inverse_norm for c in range(4))
    rot = [
        [1.0 - 2.0 * (y * y + z * z), 2.0 * (x * y - w * z), 2.0 * (x * z + w * y)],
        [2.0 * (x * y + w * z), 1.0 - 2.0 * (x * x + z * z), 2.0 * (y * z - w * x)],
        [2.0 * (x * z - w * y), 2.0 * (y * z + w * x), 1.0 - 2.0 * (x * x + y * y)],
    ]
    focal_z = FOCAL * inverse_z
    jac = [[focal_z * (m[r][c] - viewed[r] * inverse_z * m[2][c]) for c in range(3)] for r in range(2)]
    proj = [
        [(jac[r][0] * rot[0][c] + jac[r][1] * rot[1][c] + jac[r][2] * rot[2][c]) * scales[c] for c in range(3)]
        for r in range(2)
    ]
    cov_xx = proj[0][0] * proj[0][0] + proj[0][1] * proj[0][1] + proj[0][2] * proj[0][2] + 0.3
    cov_xy = proj[0][0] * proj[1][0] + proj[0][1] * proj[1][1] + proj[0][2] * proj[1][2]
    cov_yy = proj[1][0] * proj[1][0] + proj[1][1] * proj[1][1] + proj[1][2] * proj[1][2] + 0.3
    inverse_det = 1.0 / (cov_xx * cov_yy - cov_xy * cov_xy)
    log_opacity = -jnp.log(1.0 + jnp.exp(-values[10]))
    inverse_distance = 1.0 / jnp.sqrt(viewed[0] * viewed[0] + viewed[1] * viewed[1] + viewed[2] * viewed[2])
    terms = harmonics(*[viewed[c] * inverse_distance for c in range(3)])
    colour = []
    for ch in range(3):
        total = 0.5 + HARMONIC_ZERO * values[11 + ch]
        for k in range(1, 16):
            total = total + terms[k - 1] * values[11 + 3 * k + ch]
        colour.append(jnp.maximum(total, 0.0))
    return [centre_u, centre_v, cov_yy * inverse_det, -cov_xy * inverse_det, cov_xx * inverse_det, log_opacity] + colour


def iota(shape, dim):
    return lax.broadcasted_iota(jnp.int32, shape, dim)


def one_hot(truth):
    return jnp.where(truth, 1.0, 0.0).astype(BF16)


def pieces(x, count):
    out = []
    for _ in range(count - 1):
        part = x.astype(BF16)
        out.append(part)
        x = x - part.astype(F32)
    out.append(x.astype(BF16))
    return out


def nn(a, b):
    return lax.dot_general(a, b, (((1,), (0,)), ((), ())), preferred_element_type=F32)


def nt(a, b):
    return lax.dot_general(a, b, (((1,), (1,)), ((), ())), preferred_element_type=F32)


def paired_rows(x):
    return jnp.transpose(jnp.concatenate([x[:, 0:256], x[:, 256:512]], axis=0))


def unpaired(x):
    down = jnp.transpose(x)
    return jnp.concatenate([down[0:64], down[64:128]], axis=1)


def exchange_halves(a, b):
    first = iota(a.shape, len(a.shape) - 1) < 64
    turned_a, turned_b = pltpu.roll(a, 64, len(a.shape) - 1), pltpu.roll(b, 64, len(b.shape) - 1)
    return jnp.where(first, a, turned_b), jnp.where(first, turned_a, b)


def fold(x, count):
    rows = x.shape[0] // count
    total = x[:rows]
    for c in range(1, count):
        total = total + x[c * rows:(c + 1) * rows]
    return total


def owner_tables(send_ref, pick, image_of):
    send = send_ref[...]

    def chunk(g, carry):
        lanes = pl.ds(pl.multiple_of(g * 256, 256), 256)
        pick[lanes, :] = one_hot(iota((256, 512), 0) // 4 + g * 64 == send)
        return carry

    lax.fori_loop(0, 8, chunk, 0)
    image_row = jnp.broadcast_to((iota((8, 512), 1) // 64).astype(F32), (8, 512)).astype(BF16)
    images = nt(image_row, pick[...])
    for g in range(8):
        image_of[g:g + 1, :] = images[0:1, 256 * g:256 * (g + 1)]


def as_column(row):
    row = row.astype(F32)
    row = jnp.concatenate([row, jnp.zeros((128 - row.shape[0], row.shape[1]), F32)], axis=0)
    return jnp.transpose(row)


def owner_tables_back(send_ref, pick_back):
    send = as_column(send_ref[...])[:, 0:1].astype(jnp.int32)

    def chunk(g, carry):
        pick_back[g] = one_hot(iota((512, 256), 1) // 4 + g * 64 == send)
        return carry

    lax.fori_loop(0, 8, chunk, 0)


def cameras_of(cam_ref, image_of):
    image = image_of[...]
    masks = [image == float(i) for i in range(8)]
    cams = cam_ref[...]
    out = []
    for t in range(12):
        value = jnp.zeros((8, 256), F32)
        for i in range(8):
            value = jnp.where(masks[i], cams[i:i + 1, t:t + 1], value)
        out.append(value)
    return out


def owner_forward(cam_ref, pick, image_of, par3, shown3, put):
    shown = project([par3[c] for c in range(59)], cameras_of(cam_ref, image_of))
    for q in range(9):
        shown3[q] = shown[q]
    for q in range(9, 16):
        shown3[q] = jnp.zeros((8, 256), F32)
    within = iota((16, 256), 1) % 4
    total = jnp.zeros((192, 512), F32)
    for g in range(8):
        rows = []
        for b in range(4):
            rows.append(jnp.where(within == b, shown3[:, g, :], 0.0))
        rows = jnp.concatenate(rows, axis=0)
        total = total + nn(jnp.concatenate(pieces(rows, 3), axis=0), pick[256 * g:256 * (g + 1), :])
    put(paired_rows(fold(total, 3)))


def owner_gradient(got, cam_ref, pick_back, image_of, par3, shown3, grad3):
    parts = jnp.concatenate(pieces(unpaired(got), 2), axis=0)
    within = iota((16, 256), 1) % 4
    for g in range(8):
        spread = fold(nn(parts, pick_back[g]), 2)
        total = jnp.zeros((16, 256), F32)
        for b in range(4):
            total = total + jnp.where(within == b, spread[16 * b:16 * (b + 1)], 0.0)
        shown3[:, g, :] = total
    values = [par3[c] for c in range(59)]
    cams = cameras_of(cam_ref, image_of)
    _, pullback = jax.vjp(lambda v: project(v, cams), values)
    (grads,) = pullback([shown3[q] for q in range(9)])
    for c in range(59):
        grad3[c] = grads[c]


def renderer_tables(
    lists_ref, order_ref, where_ref, live_ref, target_ref, listed, sort, place, tri, wanted, listed_back, sort_back
):
    spot = iota((512, 512), 0)
    listed[...] = one_hot(spot // 32 % 8 * 64 + spot // 256 * 32 + spot % 32 == lists_ref[...])

    def one_tile(n, carry):
        order = order_ref[pl.ds(n, 1), :]
        key = (order % 4) * 128 + (n % 2) * 64 + order // 4
        sort[n] = one_hot(iota((512, 256), 0) == key)
        return carry

    lax.fori_loop(0, 8, one_tile, 0)
    spot = iota((512, 512), 1)
    column = as_column(lists_ref[...])[:, 0:1].astype(jnp.int32)
    listed_back[...] = one_hot(spot // 32 % 8 * 64 + spot // 256 * 32 + spot % 32 == column)
    order = order_ref[...]
    column = as_column((order % 4) * 128 + (iota((8, 256), 0) % 2) * 64 + order // 4)
    for n in range(8):
        sort_back[n] = one_hot(iota((256, 512), 1) == column[:, n:n + 1].astype(jnp.int32))
    lane = iota((8, 512), 1)
    tile = lane // 64
    where = jnp.zeros((8, 512), jnp.int32)
    live = jnp.zeros((8, 512), jnp.int32)
    for n in range(8):
        where = jnp.where(tile == n, where_ref[0:1, n:n + 1], where)
        live = jnp.where(tile == n, live_ref[0:1, n:n + 1], live)
    place[0] = (where % 32 * 16 + 8).astype(F32)
    place[1] = (where // 32 * 16 + 8).astype(F32)
    place[2] = jnp.where(lane % 64 < live, 1.0, 0.0)
    tri[0] = one_hot(iota((256, 256), 0) < iota((256, 256), 1))
    tri[1] = one_hot(iota((256, 256), 0) > iota((256, 256), 1))
    for n in range(8):
        rows = [target_ref[n:n + 1, 256 * ch:256 * (ch + 1)] for ch in range(3)]
        wanted[n] = jnp.transpose(jnp.concatenate(rows + [jnp.zeros((125, 256), F32)], axis=0))[:, 0:8]


def monomials(pixel, term):
    x = (pixel % 16).astype(F32) - 7.5
    y = (pixel // 16).astype(F32) - 7.5
    out = jnp.zeros(pixel.shape, F32)
    for t, value in enumerate((jnp.ones_like(x), x, y, x * x, x * y, y * y)):
        out = jnp.where(term == t, value, out)
    return out.astype(BF16)


def render(
    got, listed, sort, place, tri, wanted, listed_back, sort_back, tile3, coef3, grad3, front3, alpha3, weight3, high3, low3, put
):
    rows = unpaired(got)
    tiles = fold(nn(jnp.concatenate(pieces(rows, 3), axis=0), listed[...]), 3)
    for b in range(4):
        tile3[:, b, :] = tiles[16 * b:16 * (b + 1)]
    centre_x, centre_y, live = place[0, 0:4], place[1, 0:4], place[2, 0:4]

    def geometry():
        u, v, cxx, cxy, cyy, log_op = (tile3[q, 0:4] for q in range(6))
        return u - centre_x, v - centre_y, cxx, cxy, cyy, log_op

    u, v, cxx, cxy, cyy, log_op = geometry()
    a, b2, c2 = -0.5 * LOG2E * cxx, -LOG2E * cxy, -0.5 * LOG2E * cyy
    constant = a * u * u + b2 * u * v + c2 * v * v + LOG2E * log_op
    coefs = [
        jnp.where(live > 0.0, constant, -1e5),
        jnp.where(live > 0.0, -2.0 * a * u - b2 * v, 0.0),
        jnp.where(live > 0.0, -2.0 * c2 * v - b2 * u, 0.0),
        jnp.where(live > 0.0, a, 0.0),
        jnp.where(live > 0.0, b2, 0.0),
        jnp.where(live > 0.0, c2, 0.0),
    ] + [tile3[q, 0:4] for q in range(6, 9)]
    for c in range(9):
        coef3[c, 0:4] = coefs[c]
    for c in range(9, 16):
        coef3[c, 0:4] = jnp.zeros((4, 512), F32)
    grad3[...] = jnp.zeros(grad3.shape, F32)
    power = monomials(iota((256, 48), 0), iota((256, 48), 1) % 16)
    column = iota((16, 256), 0).astype(F32) - 7.5
    zero8 = jnp.zeros((8, 256), F32)

    for n in range(8):
        pair = slice(128 * (n // 2), 128 * (n // 2) + 128)
        mine = jnp.concatenate([coef3[:, b, pair] for b in range(4)], axis=1)
        sorted_parts = nn(jnp.concatenate(pieces(mine, 3), axis=0), sort[n])
        front = fold(sorted_parts, 3)
        front3[n] = jnp.where(iota((8, 256), 0) < 3, pltpu.roll(front, 10, 0)[0:8], 0.0)
        alpha = jnp.exp2(nn(power, sorted_parts.astype(BF16)))
        alpha3[n] = alpha
        high3[n], low3[n] = pieces(jnp.log(1.0 - alpha), 2)
    for n in range(8):
        weight = jnp.exp(nn(high3[n], tri[0]) + nn(low3[n], tri[0])) * alpha3[n]
        weight3[n] = weight
        high3[n], low3[n] = pieces(weight, 2)
    for n in range(8):
        colour = front3[n]
        c_all = jnp.concatenate(pieces(colour, 2), axis=0)
        both = nt(high3[n], c_all) + nt(low3[n], c_all)
        residual = both[:, 0:8] + both[:, 8:16] - wanted[n]
        weight = weight3[n]
        gain = jnp.zeros((256, 256), F32)
        shades = []
        for ch in range(3):
            gain = gain + residual[:, ch:ch + 1] * colour[ch:ch + 1]
            shades.append(jnp.sum(residual[:, ch:ch + 1] * weight, axis=0, keepdims=True))
        passed = weight * gain
        weight3[n] = passed
        high3[n], low3[n] = pieces(passed, 2)
        front3[n] = jnp.concatenate(shades + [zero8[0:5]], axis=0)
    for n in range(8):
        alpha = alpha3[n]
        keep = 1.0 - alpha
        guess = pl.reciprocal(keep, approx=True)
        inverse = guess * (2.0 - keep * guess)
        behind = nn(high3[n], tri[1]) + nn(low3[n], tri[1])
        change = (weight3[n] - behind * (alpha * inverse)).reshape(16, 16, 256)
        s0, s1, s2 = change[0], -7.5 * change[0], 56.25 * change[0]
        for y in range(1, 16):
            s0 = s0 + change[y]
            s1 = s1 + (y - 7.5) * change[y]
            s2 = s2 + (y - 7.5) * (y - 7.5) * change[y]
        moments = [s0, s0 * column, s1, s0 * column * column, s1 * column, s2]
        back = jnp.concatenate([jnp.sum(m, axis=0, keepdims=True) for m in moments] + [zero8[0:2], front3[n]], axis=0)
        pair = slice(128 * (n // 2), 128 * (n // 2) + 128)
        spread = fold(nn(jnp.concatenate(pieces(back, 3), axis=0), sort_back[n]), 3)
        for b in range(4):
            grad3[:, b, pair] += spread[:, 128 * b:128 * (b + 1)]

    m0, mx, my, mxx, mxy, myy = (grad3[t, 0:4] for t in range(6))
    u, v, cxx, cxy, cyy, _ = geometry()
    hx, hy = mx - u * m0, my - v * m0
    hxx = mxx - 2.0 * u * mx + u * u * m0
    hxy = mxy - u * my - v * mx + u * v * m0
    hyy = myy - 2.0 * v * my + v * v * m0
    results = [cxx * hx + cxy * hy, cxy * hx + cyy * hy, -0.5 * hxx, -hxy, -0.5 * hyy, m0]
    results += [grad3[8 + ch, 0:4] for ch in range(3)]
    for q in range(9):
        tile3[q, 0:4] = results[q]
    for q in range(9, 16):
        tile3[q, 0:4] = jnp.zeros((4, 512), F32)
    rows = jnp.concatenate([tile3[:, b, :] for b in range(4)], axis=0)
    put(paired_rows(fold(nn(jnp.concatenate(pieces(rows, 2), axis=0), listed_back[...]), 2)))


def rate_column():
    row = iota((59, 1), 0)
    rate = jnp.full((59, 1), 0.000125, F32)
    for end, value in ((14, 0.0025), (11, 0.05), (10, 0.001), (6, 0.005), (3, 0.00016)):
        rate = jnp.where(row < end, value, rate)
    return rate


def adam(both_ref, params_ref, first_ref, out_params, out_first, out_second, held_p, held_f, held_s, sems):
    rate = rate_column()
    copies = []
    for c in range(8):
        at = slice(8 * c, min(8 * c + 8, 59))
        gradient = both_ref[0, at, :]
        first = 0.9 * first_ref[at, :] + 0.1 * gradient
        second = 0.999 * both_ref[1, at, :] + 0.001 * gradient * gradient
        held_f[at, :] = first
        held_s[at, :] = second
        held_p[at, :] = params_ref[at, :] - rate[at] * first / (jnp.sqrt(second) + 1e-15)
        for part, (held, out) in enumerate(((held_p, out_params), (held_f, out_first), (held_s, out_second))):
            copy = pltpu.make_async_copy(held.at[at, :], out.at[at, :], sems.at[3 * c + part])
            copy.start()
            copies.append(copy)
    for copy in copies:
        copy.wait()


OWNER_SCRATCH = [
    pltpu.VMEM((2048, 512), BF16),
    pltpu.VMEM((8, 256), F32),
    pltpu.VMEM((59, 8, 256), F32),
    pltpu.VMEM((16, 8, 256), F32),
    pltpu.VMEM((8, 512, 256), BF16),
]
RENDER_SCRATCH = [
    pltpu.VMEM((512, 512), BF16),
    pltpu.VMEM((8, 512, 256), BF16),
    pltpu.VMEM((3, 8, 512), F32),
    pltpu.VMEM((2, 256, 256), BF16),
    pltpu.VMEM((8, 256, 8), F32),
    pltpu.VMEM((512, 512), BF16),
    pltpu.VMEM((8, 256, 512), BF16),
    pltpu.VMEM((16, 8, 512), F32),
    pltpu.VMEM((16, 8, 512), F32),
    pltpu.VMEM((16, 8, 512), F32),
    pltpu.VMEM((8, 8, 256), F32),
    pltpu.VMEM((8, 256, 256), F32),
    pltpu.VMEM((8, 256, 256), F32),
    pltpu.VMEM((8, 256, 256), BF16),
    pltpu.VMEM((8, 256, 256), BF16),
]


def landed(ref, sem):
    pltpu.make_async_copy(ref, ref, sem).wait()


def step(
    params_hbm, send_hbm, lists_hbm, order_hbm, where_hbm, live_hbm, target_hbm, camera_hbm, second_hbm, out_ref,
    send_ref, lists_ref, order_ref, where_ref, live_ref, target_ref, camera_ref, in_sems,
    pick, image_of, par3, shown3, pick_back, owner3,
    listed, sort, place, tri, wanted, listed_back, sort_back, tile3, coef3, grad3, front3, alpha3, weight3, high3, low3,
    cam_row, cams, shown_out, shown_mid, back_send, back_in, shown_send, shown_in, back_out, back_mid, send_sems, recv_sems, own_sem,
):
    i = lax.axis_index("img")
    j = lax.axis_index("dev")
    mesh_ids = pl.DeviceIdType.MESH

    barrier = pltpu.get_barrier_semaphore()
    for s in range(1, 8):
        pl.semaphore_signal(barrier, inc=1, device_id=(lax.rem(i + s, 8), j), device_id_type=mesh_ids)

    @pl.loop(1, 64)
    def _(s):
        pl.semaphore_signal(barrier, inc=1, device_id=(i, lax.rem(j + s, 64)), device_id_type=mesh_ids)

    loads = [
        pltpu.make_async_copy(source, target, in_sems.at[c])
        for c, (source, target) in enumerate(
            [(camera_hbm, camera_ref), (send_hbm, send_ref)]
            + [(params_hbm.at[:, pl.ds(256 * g, 256)], par3.at[:, g, :]) for g in range(8)]
            + [(lists_hbm, lists_ref), (order_hbm, order_ref), (where_hbm, where_ref), (live_hbm, live_ref)]
            + [(target_hbm, target_ref), (second_hbm, out_ref.at[1])]
        )
    ]
    for load in loads:
        load.start()
    cam_row[...] = jnp.zeros((8, 128), F32)
    loads[0].wait()
    cam_row[0:1, 0:12] = camera_ref[...]
    pl.semaphore_wait(barrier, 70)

    def to_img(source, target, phase):
        for s in range(1, 8):
            t = lax.rem(i + s, 8)
            pltpu.make_async_remote_copy(
                src_ref=source(t),
                dst_ref=target,
                send_sem=send_sems.at[phase],
                recv_sem=recv_sems.at[phase],
                device_id=(t, j),
                device_id_type=mesh_ids,
            ).start()
        own = pltpu.make_async_copy(source(i), target, own_sem)
        own.start()
        own.wait()

    def to_dev(source, target, phase):
        def one(s, carry):
            t = lax.rem(j + s, 64)
            pltpu.make_async_remote_copy(
                src_ref=source.at[t],
                dst_ref=target.at[j],
                send_sem=send_sems.at[phase],
                recv_sem=recv_sems.at[phase],
                device_id=(i, t),
                device_id_type=mesh_ids,
            ).start()
            return carry

        lax.fori_loop(1, 64, one, 0)
        own = pltpu.make_async_copy(source.at[j], target.at[j], own_sem)
        own.start()
        own.wait()

    to_img(lambda t: cam_row.at[pl.ds(0, 1)], cams.at[pl.ds(i, 1)], 0)
    loads[1].wait()
    owner_tables(send_ref, pick, image_of)
    landed(cams.at[pl.ds(0, 7)], recv_sems.at[0])

    def put_shown(x):
        for p in range(4):
            shown_out[:, p, :] = x[64 * p:64 * (p + 1)]

    for load in loads[2:10]:
        load.wait()
    owner_forward(cams, pick, image_of, par3, shown3, put_shown)
    to_dev(shown_out, shown_mid, 1)
    for load in loads[10:]:
        load.wait()
    renderer_tables(
        lists_ref, order_ref, where_ref, live_ref, target_ref, listed, sort, place, tri, wanted, listed_back, sort_back
    )
    landed(shown_mid.at[pl.ds(0, 63)], recv_sems.at[1])
    for p in range(4):
        low_half, high_half = exchange_halves(shown_mid[0:32, p, :], shown_mid[32:64, p, :])
        shown_send[p] = low_half
        shown_send[p + 4] = high_half
    to_img(lambda t: shown_send.at[t], shown_in.at[i], 2)
    owner_tables_back(send_ref, pick_back)
    landed(shown_in.at[pl.ds(0, 7)], recv_sems.at[2])

    def put_back(x):
        back_out[...] = x.reshape(8, 32, 128)

    render(
        shown_in[...].reshape(256, 128),
        listed, sort, place, tri, wanted, listed_back, sort_back, tile3, coef3, grad3, front3, alpha3, weight3, high3, low3,
        put_back,
    )
    to_img(lambda t: back_out.at[t], back_mid.at[i], 3)
    landed(back_mid.at[pl.ds(0, 7)], recv_sems.at[3])
    for p in range(4):
        low_half, high_half = exchange_halves(back_mid[p], back_mid[p + 4])
        back_send[0:32, p, :] = low_half
        back_send[32:64, p, :] = high_half
    to_dev(back_send, back_in, 4)
    landed(back_in.at[pl.ds(0, 63)], recv_sems.at[4])
    got = jnp.concatenate([back_in[:, p, :] for p in range(4)], axis=0)
    owner_gradient(got, cams, pick_back, image_of, par3, shown3, owner3)
    for g in range(8):
        out_ref[0, :, 256 * g:256 * (g + 1)] = owner3[:, g, :]
    landed(cams.at[pl.ds(0, 7)], send_sems.at[0])
    landed(shown_out.at[pl.ds(0, 63)], send_sems.at[1])
    landed(shown_send.at[pl.ds(0, 7)], send_sems.at[2])
    landed(back_out.at[pl.ds(0, 7)], send_sems.at[3])
    landed(back_send.at[pl.ds(0, 63)], send_sems.at[4])


def local(
    params, first_moment, second_moment, send_blocks, tile_blocks, tile_live, depth_order, tile_where, target, camera
):
    vmem = pl.BlockSpec(memory_space=pltpu.VMEM)
    whole = pl.BlockSpec(memory_space=pltpu.HBM)
    integer = jnp.int32
    by_dev = pltpu.VMEM((64, 4, 128), F32)
    by_img = pltpu.VMEM((8, 32, 128), F32)
    operands = (
        params,
        send_blocks,
        tile_blocks.reshape(1, 512),
        depth_order.reshape(8, 256),
        tile_where,
        tile_live,
        target.reshape(8, 768),
        camera,
        second_moment,
    )
    shape = jax.ShapeDtypeStruct((59, 2048), F32)
    gradient_second = pl.pallas_call(
        step,
        out_shape=jax.ShapeDtypeStruct((2, 59, 2048), F32),
        in_specs=[whole] * 9,
        out_specs=vmem,
        scratch_shapes=[
            pltpu.VMEM((1, 512), integer),
            pltpu.VMEM((1, 512), integer),
            pltpu.VMEM((8, 256), integer),
            pltpu.VMEM((1, 8), integer),
            pltpu.VMEM((1, 8), integer),
            pltpu.VMEM((8, 768), F32),
            pltpu.VMEM((1, 12), F32),
            pltpu.SemaphoreType.DMA((16,)),
        ]
        + OWNER_SCRATCH
        + [pltpu.VMEM((59, 8, 256), F32)]
        + RENDER_SCRATCH
        + [pltpu.VMEM((8, 128), F32)] * 2
        + [by_dev] * 4
        + [by_img] * 4
        + [pltpu.SemaphoreType.DMA((5,)), pltpu.SemaphoreType.DMA((5,)), pltpu.SemaphoreType.DMA],
        compiler_params=pltpu.CompilerParams(collective_id=0, has_side_effects=True, vmem_limit_bytes=24 << 20),
    )(*[pltpu.with_memory_space_constraint(operand, pltpu.HBM) for operand in operands])
    return pl.pallas_call(
        adam,
        out_shape=(shape, shape, shape),
        in_specs=[vmem] * 3,
        out_specs=(whole, whole, whole),
        scratch_shapes=[pltpu.VMEM((59, 2048), F32)] * 3 + [pltpu.SemaphoreType.DMA((24,))],
        compiler_params=pltpu.CompilerParams(vmem_limit_bytes=16 << 20),
    )(gradient_second, params, first_moment)


def solution(mesh):
    return jax.shard_map(
        local,
        mesh=mesh,
        in_specs=(
            P(None, ("img", "dev")),
            P(None, ("img", "dev")),
            P(None, ("img", "dev")),
            P(("img", "dev"), None),
            P("img", "dev", None),
            P("img", "dev"),
            P("img", "dev", None),
            P("img", "dev"),
            P("img", "dev", None),
            P("img", None),
        ),
        out_specs=(P(None, ("img", "dev")), P(None, ("img", "dev")), P(None, ("img", "dev"))),
        check_vma=False,
    )
```

```python
import functools

import jax
import jax.numpy as jnp
from jax import lax
from jax.experimental import pallas as pl
from jax.experimental.pallas import tpu as pltpu
from jax.sharding import PartitionSpec as P

F32, BF16 = jnp.float32, jnp.bfloat16
LOG2E = 1.4426950408889634
FOCAL = 1024.0
CENTRE_U, CENTRE_V = 256.0, 128.0

HARMONIC_ZERO = 0.28209479177387814
HARMONIC_ONE = 0.4886025119029199
HARMONIC_TWO = (
    1.0925484305920792,
    -1.0925484305920792,
    0.31539156525252005,
    -1.0925484305920792,
    0.5462742152960396,
)
HARMONIC_THREE = (
    -0.5900435899266435,
    2.890611442640554,
    -0.4570457994644658,
    0.3731763325901154,
    -0.4570457994644658,
    1.445305721320277,
    -0.5900435899266435,
)


def harmonics(dir_x, dir_y, dir_z):
    square_x = dir_x * dir_x
    square_y = dir_y * dir_y
    square_z = dir_z * dir_z
    return [
        -HARMONIC_ONE * dir_y,
        HARMONIC_ONE * dir_z,
        -HARMONIC_ONE * dir_x,
        HARMONIC_TWO[0] * dir_x * dir_y,
        HARMONIC_TWO[1] * dir_y * dir_z,
        HARMONIC_TWO[2] * (2.0 * square_z - square_x - square_y),
        HARMONIC_TWO[3] * dir_x * dir_z,
        HARMONIC_TWO[4] * (square_x - square_y),
        HARMONIC_THREE[0] * dir_y * (3.0 * square_x - square_y),
        HARMONIC_THREE[1] * dir_x * dir_y * dir_z,
        HARMONIC_THREE[2] * dir_y * (4.0 * square_z - square_x - square_y),
        HARMONIC_THREE[3] * dir_z * (2.0 * square_z - 3.0 * square_x - 3.0 * square_y),
        HARMONIC_THREE[4] * dir_x * (4.0 * square_z - square_x - square_y),
        HARMONIC_THREE[5] * dir_z * (square_x - square_y),
        HARMONIC_THREE[6] * dir_x * (square_x - 3.0 * square_y),
    ]


def project(values, cam):
    m = [[cam[3 * r + c] for c in range(3)] for r in range(3)]
    viewed = [m[r][0] * values[0] + m[r][1] * values[1] + m[r][2] * values[2] + cam[9 + r] for r in range(3)]
    inverse_z = 1.0 / viewed[2]
    centre_u = FOCAL * viewed[0] * inverse_z + CENTRE_U
    centre_v = FOCAL * viewed[1] * inverse_z + CENTRE_V
    scales = [jnp.exp(values[3 + c]) for c in range(3)]
    norm = jnp.sqrt(values[6] * values[6] + values[7] * values[7] + values[8] * values[8] + values[9] * values[9])
    inverse_norm = 1.0 / norm
    w, x, y, z = (values[6 + c] * inverse_norm for c in range(4))
    rot = [
        [1.0 - 2.0 * (y * y + z * z), 2.0 * (x * y - w * z), 2.0 * (x * z + w * y)],
        [2.0 * (x * y + w * z), 1.0 - 2.0 * (x * x + z * z), 2.0 * (y * z - w * x)],
        [2.0 * (x * z - w * y), 2.0 * (y * z + w * x), 1.0 - 2.0 * (x * x + y * y)],
    ]
    focal_z = FOCAL * inverse_z
    jac = [[focal_z * (m[r][c] - viewed[r] * inverse_z * m[2][c]) for c in range(3)] for r in range(2)]
    proj = [
        [(jac[r][0] * rot[0][c] + jac[r][1] * rot[1][c] + jac[r][2] * rot[2][c]) * scales[c] for c in range(3)]
        for r in range(2)
    ]
    cov_xx = proj[0][0] * proj[0][0] + proj[0][1] * proj[0][1] + proj[0][2] * proj[0][2] + 0.3
    cov_xy = proj[0][0] * proj[1][0] + proj[0][1] * proj[1][1] + proj[0][2] * proj[1][2]
    cov_yy = proj[1][0] * proj[1][0] + proj[1][1] * proj[1][1] + proj[1][2] * proj[1][2] + 0.3
    inverse_det = 1.0 / (cov_xx * cov_yy - cov_xy * cov_xy)
    log_opacity = -jnp.log(1.0 + jnp.exp(-values[10]))
    inverse_distance = 1.0 / jnp.sqrt(viewed[0] * viewed[0] + viewed[1] * viewed[1] + viewed[2] * viewed[2])
    terms = harmonics(*[viewed[c] * inverse_distance for c in range(3)])
    colour = []
    for ch in range(3):
        total = 0.5 + HARMONIC_ZERO * values[11 + ch]
        for k in range(1, 16):
            total = total + terms[k - 1] * values[11 + 3 * k + ch]
        colour.append(jnp.maximum(total, 0.0))
    return [centre_u, centre_v, cov_yy * inverse_det, -cov_xy * inverse_det, cov_xx * inverse_det, log_opacity] + colour


def iota(shape, dim):
    return lax.broadcasted_iota(jnp.int32, shape, dim)


def one_hot(truth):
    return jnp.where(truth, 1.0, 0.0).astype(BF16)


def pieces(x, count):
    out = []
    for _ in range(count - 1):
        part = x.astype(BF16)
        out.append(part)
        x = x - part.astype(F32)
    out.append(x.astype(BF16))
    return out


def nn(a, b):
    return lax.dot_general(a, b, (((1,), (0,)), ((), ())), preferred_element_type=F32)


def nt(a, b):
    return lax.dot_general(a, b, (((1,), (1,)), ((), ())), preferred_element_type=F32)


def paired_rows(x):
    return jnp.transpose(jnp.concatenate([x[:, 0:256], x[:, 256:512]], axis=0))


def unpaired(x):
    down = jnp.transpose(x)
    return jnp.concatenate([down[0:64], down[64:128]], axis=1)


def exchange_halves(a, b):
    first = iota(a.shape, len(a.shape) - 1) < 64
    turned_a, turned_b = pltpu.roll(a, 64, len(a.shape) - 1), pltpu.roll(b, 64, len(b.shape) - 1)
    return jnp.where(first, a, turned_b), jnp.where(first, turned_a, b)


def fold(x, count):
    rows = x.shape[0] // count
    total = x[:rows]
    for c in range(1, count):
        total = total + x[c * rows:(c + 1) * rows]
    return total


def owner_tables(send_ref, pick, image_of, weave):
    pick[...] = one_hot(iota((512, 512), 0) == send_ref[...])
    row, column = iota((256, 256), 0), iota((256, 256), 1)
    weave[0] = one_hot(row == column % 64 * 4 + column // 64)
    weave[1] = one_hot(column == row % 64 * 4 + row // 64)
    images = nt((iota((8, 512), 1) // 64).astype(F32).astype(BF16), pick[...])
    own = jnp.where(iota((8, 512), 1) // 64 == iota((8, 512), 0), images, 0.0).astype(BF16)
    image_of[...] = nn(own, one_hot(iota((512, 256), 0) % 64 == iota((512, 256), 1) // 4))


def as_column(row):
    row = row.astype(F32)
    row = jnp.concatenate([row, jnp.zeros((128 - row.shape[0], row.shape[1]), F32)], axis=0)
    return jnp.transpose(row)


def owner_tables_back(send_ref, pick_back):
    pick_back[...] = one_hot(iota((512, 512), 1) == as_column(send_ref[...])[:, 0:1].astype(jnp.int32))


def cameras_of(cam_ref, image_of):
    image = image_of[...]
    masks = [image == float(i) for i in range(8)]
    cams = cam_ref[...]
    out = []
    for t in range(12):
        value = jnp.zeros((8, 256), F32)
        for i in range(8):
            value = jnp.where(masks[i], cams[i:i + 1, t:t + 1], value)
        out.append(value)
    return out


def owner_forward(cam_ref, pick, image_of, weave, par3, shown3, put):
    shown = project([par3[c] for c in range(59)], cameras_of(cam_ref, image_of))
    for q in range(9):
        shown3[q] = shown[q]
    for q in range(9, 16):
        shown3[q] = jnp.zeros((8, 256), F32)
    flat = shown3[0:10].reshape(80, 256)
    shown3[0:10] = fold(nn(jnp.concatenate(pieces(flat, 3), axis=0), weave[0]), 3).reshape(10, 8, 256)
    rows = [[], [], [], []]
    for p in range(2):
        at = slice(128 * p, 128 * (p + 1))
        for t in range(4):
            even, odd = exchange_halves(shown3[:, 2 * t, at], shown3[:, 2 * t + 1, at])
            rows[2 * p].append(even)
            rows[2 * p + 1].append(odd)
    rows = jnp.concatenate([jnp.concatenate(row, axis=1) for row in rows], axis=0)
    put(paired_rows(fold(nn(jnp.concatenate(pieces(rows, 3), axis=0), pick[...]), 3)))


def owner_pullback(cam_ref, image_of, par3):
    cams = cameras_of(cam_ref, image_of)
    return jax.vjp(lambda v: project(v, cams), [par3[c] for c in range(59)])[1]


def owner_gradient(got, pullback, pick_back, weave, shown3, grad3):
    spread = fold(nn(jnp.concatenate(pieces(unpaired(got), 2), axis=0), pick_back[...]), 2)
    for p in range(2):
        at = slice(128 * p, 128 * (p + 1))
        for t in range(4):
            lanes = slice(128 * t, 128 * (t + 1))
            even, odd = exchange_halves(spread[32 * p:32 * p + 16, lanes], spread[32 * p + 16:32 * p + 32, lanes])
            shown3[:, 2 * t, at] = even
            shown3[:, 2 * t + 1, at] = odd
    flat = shown3[0:10].reshape(80, 256)
    slopes = fold(nn(jnp.concatenate(pieces(flat, 2), axis=0), weave[1]), 2).reshape(10, 8, 256)
    (grads,) = pullback([slopes[q] for q in range(9)])
    for c in range(59):
        grad3[c] = grads[c]


def renderer_tables(
    lists_ref, order_ref, where_ref, live_ref, target_ref, listed, sort, place, tri, wanted, listed_back, sort_back, power,
    tile3, coef3, grad3,
):
    spot = iota((512, 512), 0)
    listed[...] = one_hot(spot // 32 % 8 * 64 + spot // 256 * 32 + spot % 32 == lists_ref[...])

    def one_tile(n, carry):
        order = order_ref[pl.ds(n, 1), :]
        key = (order % 4) * 128 + (n % 2) * 64 + order // 4
        sort[n] = one_hot(iota((512, 256), 0) == key)
        return carry

    lax.fori_loop(0, 8, one_tile, 0)
    spot = iota((512, 512), 1)
    column = as_column(lists_ref[...])[:, 0:1].astype(jnp.int32)
    listed_back[...] = one_hot(spot // 32 % 8 * 64 + spot // 256 * 32 + spot % 32 == column)
    order = order_ref[...]
    column = as_column((order % 4) * 128 + (iota((8, 256), 0) % 2) * 64 + order // 4)
    for n in range(8):
        sort_back[n] = one_hot(iota((256, 512), 1) == column[:, n:n + 1].astype(jnp.int32))
    lane = iota((8, 512), 1)
    tile = lane // 64
    where = jnp.zeros((8, 512), jnp.int32)
    live = jnp.zeros((8, 512), jnp.int32)
    for n in range(8):
        where = jnp.where(tile == n, where_ref[0:1, n:n + 1], where)
        live = jnp.where(tile == n, live_ref[0:1, n:n + 1], live)
    place[0] = (where % 32 * 16 + 8).astype(F32)
    place[1] = (where // 32 * 16 + 8).astype(F32)
    place[2] = jnp.where(lane % 64 < live, 1.0, 0.0)
    tri[0] = one_hot(iota((512, 256), 0) % 256 < iota((512, 256), 1))
    tri[1] = one_hot(iota((512, 256), 0) % 256 > iota((512, 256), 1))
    for n in range(8):
        rows = [target_ref[n:n + 1, 256 * ch:256 * (ch + 1)] for ch in range(3)]
        wanted[n] = jnp.transpose(jnp.concatenate(rows + [jnp.zeros((125, 256), F32)], axis=0))[:, 0:8]
    power[...] = monomials(iota((256, 48), 0), iota((256, 48), 1) % 16)
    for held in (tile3, coef3, grad3):
        held[...] = jnp.zeros(held.shape, F32)


def monomials(pixel, term):
    x = (pixel % 16).astype(F32) - 7.5
    y = (pixel // 16).astype(F32) - 7.5
    out = jnp.zeros(pixel.shape, F32)
    for t, value in enumerate((jnp.ones_like(x), x, y, x * x, x * y, y * y)):
        out = jnp.where(term == t, value, out)
    return out.astype(BF16)


def render(
    got, listed, sort, place, tri, wanted, listed_back, sort_back, power, tile3, coef3, grad3, front3, alpha3, weight3, split3, put
):
    rows = unpaired(got)
    tiles = fold(nn(jnp.concatenate(pieces(rows, 3), axis=0), listed[...]), 3)
    for b in range(4):
        tile3[:, b, :] = tiles[16 * b:16 * (b + 1)]
    centre_x, centre_y, live = place[0, 0:4], place[1, 0:4], place[2, 0:4]

    def geometry():
        u, v, cxx, cxy, cyy, log_op = (tile3[q, 0:4] for q in range(6))
        return u - centre_x, v - centre_y, cxx, cxy, cyy, log_op

    u, v, cxx, cxy, cyy, log_op = geometry()
    a, b2, c2 = -0.5 * LOG2E * cxx, -LOG2E * cxy, -0.5 * LOG2E * cyy
    constant = a * u * u + b2 * u * v + c2 * v * v + LOG2E * log_op
    coefs = [
        jnp.where(live > 0.0, constant, -1e5),
        jnp.where(live > 0.0, -2.0 * a * u - b2 * v, 0.0),
        jnp.where(live > 0.0, -2.0 * c2 * v - b2 * u, 0.0),
        jnp.where(live > 0.0, a, 0.0),
        jnp.where(live > 0.0, b2, 0.0),
        jnp.where(live > 0.0, c2, 0.0),
    ] + [tile3[q, 0:4] for q in range(6, 9)]
    for c in range(9):
        coef3[c, 0:4] = coefs[c]
    column = iota((16, 256), 0).astype(F32) - 7.5
    zero8 = jnp.zeros((8, 256), F32)

    for n in range(8):
        pair = slice(128 * (n // 2), 128 * (n // 2) + 128)
        mine = jnp.concatenate([coef3[:, b, pair] for b in range(4)], axis=1)
        sorted_parts = nn(jnp.concatenate(pieces(mine, 3), axis=0), sort[n])
        front = fold(sorted_parts, 3)
        front3[n] = jnp.where(iota((8, 256), 0) < 3, pltpu.roll(front, 10, 0)[0:8], 0.0)
        alpha = jnp.exp2(nn(power[...], sorted_parts.astype(BF16)))
        alpha3[n] = alpha
        split3[n] = jnp.concatenate(pieces(jnp.log(1.0 - alpha), 2), axis=1)
    for n in range(8):
        weight = jnp.exp(nn(split3[n], tri[0])) * alpha3[n]
        weight3[n] = weight
        split3[n] = jnp.concatenate(pieces(weight, 2), axis=1)
    for n in range(8):
        colour = front3[n]
        c_all = jnp.concatenate(pieces(colour, 2), axis=0)
        both = nt(split3[n], jnp.concatenate([c_all, c_all], axis=1))
        residual = both[:, 0:8] + both[:, 8:16] - wanted[n]
        weight = weight3[n]
        gain = jnp.zeros((256, 256), F32)
        shades = []
        for ch in range(3):
            gain = gain + residual[:, ch:ch + 1] * colour[ch:ch + 1]
            shades.append(jnp.sum(residual[:, ch:ch + 1] * weight, axis=0, keepdims=True))
        passed = weight * gain
        weight3[n] = passed
        split3[n] = jnp.concatenate(pieces(passed, 2), axis=1)
        front3[n] = jnp.concatenate(shades + [zero8[0:5]], axis=0)
    for n in range(8):
        alpha = alpha3[n]
        keep = 1.0 - alpha
        guess = pl.reciprocal(keep, approx=True)
        inverse = guess * (2.0 - keep * guess)
        behind = nn(split3[n], tri[1])
        change = (weight3[n] - behind * (alpha * inverse)).reshape(16, 16, 256)
        s0, s1, s2 = change[0], -7.5 * change[0], 56.25 * change[0]
        for y in range(1, 16):
            s0 = s0 + change[y]
            s1 = s1 + (y - 7.5) * change[y]
            s2 = s2 + (y - 7.5) * (y - 7.5) * change[y]
        moments = [s0, s0 * column, s1, s0 * column * column, s1 * column, s2]
        back = jnp.concatenate([jnp.sum(m, axis=0, keepdims=True) for m in moments] + [zero8[0:2], front3[n]], axis=0)
        pair = slice(128 * (n // 2), 128 * (n // 2) + 128)
        spread = fold(nn(jnp.concatenate(pieces(back, 3), axis=0), sort_back[n]), 3)
        for b in range(4):
            grad3[:, b, pair] += spread[:, 128 * b:128 * (b + 1)]

    m0, mx, my, mxx, mxy, myy = (grad3[t, 0:4] for t in range(6))
    u, v, cxx, cxy, cyy, _ = geometry()
    hx, hy = mx - u * m0, my - v * m0
    hxx = mxx - 2.0 * u * mx + u * u * m0
    hxy = mxy - u * my - v * mx + u * v * m0
    hyy = myy - 2.0 * v * my + v * v * m0
    results = [cxx * hx + cxy * hy, cxy * hx + cyy * hy, -0.5 * hxx, -hxy, -0.5 * hyy, m0]
    results += [grad3[8 + ch, 0:4] for ch in range(3)]
    for q in range(9):
        tile3[q, 0:4] = results[q]
    for q in range(9, 16):
        tile3[q, 0:4] = jnp.zeros((4, 512), F32)
    rows = jnp.concatenate([tile3[:, b, :] for b in range(4)], axis=0)
    put(paired_rows(fold(nn(jnp.concatenate(pieces(rows, 2), axis=0), listed_back[...]), 2)))


def rate_column():
    row = iota((59, 1), 0)
    rate = jnp.full((59, 1), 0.000125, F32)
    for end, value in ((14, 0.0025), (11, 0.05), (10, 0.001), (6, 0.005), (3, 0.00016)):
        rate = jnp.where(row < end, value, rate)
    return rate


def adam(both_ref, params_ref, first_ref, out_params, out_first, out_second, held_p, held_f, held_s, sems):
    rate = rate_column()
    copies = []
    for c in range(8):
        at = slice(8 * c, min(8 * c + 8, 59))
        gradient = both_ref[0, at, :]
        first = 0.9 * first_ref[at, :] + 0.1 * gradient
        second = 0.999 * both_ref[1, at, :] + 0.001 * gradient * gradient
        held_f[at, :] = first
        held_s[at, :] = second
        held_p[at, :] = params_ref[at, :] - rate[at] * first / (jnp.sqrt(second) + 1e-15)
        for part, (held, out) in enumerate(((held_p, out_params), (held_f, out_first), (held_s, out_second))):
            copy = pltpu.make_async_copy(held.at[at, :], out.at[at, :], sems.at[3 * c + part])
            copy.start()
            copies.append(copy)
    for copy in copies:
        copy.wait()


OWNER_SCRATCH = [
    pltpu.VMEM((512, 512), BF16),
    pltpu.VMEM((8, 256), F32),
    pltpu.VMEM((2, 256, 256), BF16),
    pltpu.VMEM((59, 8, 256), F32),
    pltpu.VMEM((16, 8, 256), F32),
    pltpu.VMEM((512, 512), BF16),
]
RENDER_SCRATCH = [
    pltpu.VMEM((512, 512), BF16),
    pltpu.VMEM((8, 512, 256), BF16),
    pltpu.VMEM((3, 8, 512), F32),
    pltpu.VMEM((2, 512, 256), BF16),
    pltpu.VMEM((8, 256, 8), F32),
    pltpu.VMEM((512, 512), BF16),
    pltpu.VMEM((8, 256, 512), BF16),
    pltpu.VMEM((256, 48), BF16),
    pltpu.VMEM((16, 8, 512), F32),
    pltpu.VMEM((16, 8, 512), F32),
    pltpu.VMEM((16, 8, 512), F32),
    pltpu.VMEM((8, 8, 256), F32),
    pltpu.VMEM((8, 256, 256), F32),
    pltpu.VMEM((8, 256, 256), F32),
    pltpu.VMEM((8, 256, 512), BF16),
]


def landed(ref, sem):
    pltpu.make_async_copy(ref, ref, sem).wait()


def step(
    params_hbm, send_hbm, lists_hbm, order_hbm, where_hbm, live_hbm, target_hbm, camera_hbm, second_hbm, out_ref,
    send_ref, lists_ref, order_ref, where_ref, live_ref, target_ref, camera_ref, in_sems,
    pick, image_of, weave, par3, shown3, pick_back, owner3,
    listed, sort, place, tri, wanted, listed_back, sort_back, power, tile3, coef3, grad3, front3, alpha3, weight3, split3,
    cam_row, cams, shown_out, shown_mid, back_send, back_in, shown_send, shown_in, back_out, back_mid, send_sems, recv_sems, own_sem,
):
    i = lax.axis_index("img")
    j = lax.axis_index("dev")
    mesh_ids = pl.DeviceIdType.MESH

    barrier = pltpu.get_barrier_semaphore()
    for s in range(1, 8):
        pl.semaphore_signal(barrier, inc=1, device_id=(lax.rem(i + s, 8), j), device_id_type=mesh_ids)

    @pl.loop(1, 64)
    def _(s):
        pl.semaphore_signal(barrier, inc=1, device_id=(i, lax.rem(j + s, 64)), device_id_type=mesh_ids)

    loads = [
        pltpu.make_async_copy(source, target, in_sems.at[c])
        for c, (source, target) in enumerate(
            [(camera_hbm, camera_ref), (send_hbm, send_ref)]
            + [(params_hbm.at[:, pl.ds(256 * g, 256)], par3.at[:, g, :]) for g in range(8)]
            + [(lists_hbm, lists_ref), (order_hbm, order_ref), (where_hbm, where_ref), (live_hbm, live_ref)]
            + [(target_hbm, target_ref), (second_hbm, out_ref.at[1])]
        )
    ]
    for load in loads:
        load.start()
    cam_row[...] = jnp.zeros((8, 128), F32)
    loads[0].wait()
    cam_row[0:1, 0:12] = camera_ref[...]
    pl.semaphore_wait(barrier, 70)

    def to_img(source, target, phase):
        for s in (4, 3, 5, 2, 6, 1, 7):
            t = lax.rem(i + s, 8)
            pltpu.make_async_remote_copy(
                src_ref=source(t),
                dst_ref=target,
                send_sem=send_sems.at[phase],
                recv_sem=recv_sems.at[phase],
                device_id=(t, j),
                device_id_type=mesh_ids,
            ).start()
        own = pltpu.make_async_copy(source(i), target, own_sem)
        own.start()
        own.wait()

    def to_dev(source, target, phase):
        def one(s, carry):
            t = lax.rem(j + s, 64)
            pltpu.make_async_remote_copy(
                src_ref=source.at[t],
                dst_ref=target.at[j],
                send_sem=send_sems.at[phase],
                recv_sem=recv_sems.at[phase],
                device_id=(i, t),
                device_id_type=mesh_ids,
            ).start()
            return carry

        lax.fori_loop(1, 64, one, 0)
        own = pltpu.make_async_copy(source.at[j], target.at[j], own_sem)
        own.start()
        own.wait()

    to_img(lambda t: cam_row.at[pl.ds(0, 1)], cams.at[pl.ds(i, 1)], 0)
    loads[1].wait()
    owner_tables(send_ref, pick, image_of, weave)
    landed(cams.at[pl.ds(0, 7)], recv_sems.at[0])

    def put_shown(x):
        for p in range(4):
            shown_out[:, p, :] = x[64 * p:64 * (p + 1)]

    for load in loads[2:10]:
        load.wait()
    owner_forward(cams, pick, image_of, weave, par3, shown3, put_shown)
    to_dev(shown_out, shown_mid, 1)
    for load in loads[10:]:
        load.wait()
    renderer_tables(
        lists_ref, order_ref, where_ref, live_ref, target_ref,
        listed, sort, place, tri, wanted, listed_back, sort_back, power, tile3, coef3, grad3,
    )
    landed(shown_mid.at[pl.ds(0, 63)], recv_sems.at[1])
    for p in range(4):
        low_half, high_half = exchange_halves(shown_mid[0:32, p, :], shown_mid[32:64, p, :])
        shown_send[p] = low_half
        shown_send[p + 4] = high_half
    to_img(lambda t: shown_send.at[t], shown_in.at[i], 2)
    owner_tables_back(send_ref, pick_back)
    landed(shown_in.at[pl.ds(0, 7)], recv_sems.at[2])

    def put_back(x):
        back_out[...] = x.reshape(8, 32, 128)

    render(
        shown_in[...].reshape(256, 128),
        listed, sort, place, tri, wanted, listed_back, sort_back, power, tile3, coef3, grad3, front3, alpha3, weight3, split3,
        put_back,
    )
    to_img(lambda t: back_out.at[t], back_mid.at[i], 3)
    landed(back_mid.at[pl.ds(0, 7)], recv_sems.at[3])
    for p in range(4):
        low_half, high_half = exchange_halves(back_mid[p], back_mid[p + 4])
        back_send[0:32, p, :] = low_half
        back_send[32:64, p, :] = high_half
    to_dev(back_send, back_in, 4)
    pullback = owner_pullback(cams, image_of, par3)
    landed(back_in.at[pl.ds(0, 63)], recv_sems.at[4])
    got = jnp.concatenate([back_in[:, p, :] for p in range(4)], axis=0)
    owner_gradient(got, pullback, pick_back, weave, shown3, owner3)
    for g in range(8):
        out_ref[0, :, 256 * g:256 * (g + 1)] = owner3[:, g, :]
    landed(cams.at[pl.ds(0, 7)], send_sems.at[0])
    landed(shown_out.at[pl.ds(0, 63)], send_sems.at[1])
    landed(shown_send.at[pl.ds(0, 7)], send_sems.at[2])
    landed(back_out.at[pl.ds(0, 7)], send_sems.at[3])
    landed(back_send.at[pl.ds(0, 63)], send_sems.at[4])


def local(
    params, first_moment, second_moment, send_blocks, tile_blocks, tile_live, depth_order, tile_where, target, camera
):
    vmem = pl.BlockSpec(memory_space=pltpu.VMEM)
    whole = pl.BlockSpec(memory_space=pltpu.HBM)
    integer = jnp.int32
    by_dev = pltpu.VMEM((64, 4, 128), F32)
    by_img = pltpu.VMEM((8, 32, 128), F32)
    operands = (
        params,
        send_blocks,
        tile_blocks.reshape(1, 512),
        depth_order.reshape(8, 256),
        tile_where,
        tile_live,
        target.reshape(8, 768),
        camera,
        second_moment,
    )
    shape = jax.ShapeDtypeStruct((59, 2048), F32)
    gradient_second = pl.pallas_call(
        step,
        out_shape=jax.ShapeDtypeStruct((2, 59, 2048), F32),
        in_specs=[whole] * 9,
        out_specs=vmem,
        scratch_shapes=[
            pltpu.VMEM((1, 512), integer),
            pltpu.VMEM((1, 512), integer),
            pltpu.VMEM((8, 256), integer),
            pltpu.VMEM((1, 8), integer),
            pltpu.VMEM((1, 8), integer),
            pltpu.VMEM((8, 768), F32),
            pltpu.VMEM((1, 12), F32),
            pltpu.SemaphoreType.DMA((16,)),
        ]
        + OWNER_SCRATCH
        + [pltpu.VMEM((59, 8, 256), F32)]
        + RENDER_SCRATCH
        + [pltpu.VMEM((8, 128), F32)] * 2
        + [by_dev] * 4
        + [by_img] * 4
        + [pltpu.SemaphoreType.DMA((5,)), pltpu.SemaphoreType.DMA((5,)), pltpu.SemaphoreType.DMA],
        compiler_params=pltpu.CompilerParams(collective_id=0, has_side_effects=True, vmem_limit_bytes=24 << 20),
    )(*[pltpu.with_memory_space_constraint(operand, pltpu.HBM) for operand in operands])
    return pl.pallas_call(
        adam,
        out_shape=(shape, shape, shape),
        in_specs=[vmem] * 3,
        out_specs=(whole, whole, whole),
        scratch_shapes=[pltpu.VMEM((59, 2048), F32)] * 3 + [pltpu.SemaphoreType.DMA((24,))],
        compiler_params=pltpu.CompilerParams(vmem_limit_bytes=16 << 20),
    )(gradient_second, params, first_moment)


def solution(mesh):
    return jax.shard_map(
        local,
        mesh=mesh,
        in_specs=(
            P(None, ("img", "dev")),
            P(None, ("img", "dev")),
            P(None, ("img", "dev")),
            P(("img", "dev"), None),
            P("img", "dev", None),
            P("img", "dev"),
            P("img", "dev", None),
            P("img", "dev"),
            P("img", "dev", None),
            P("img", None),
        ),
        out_specs=(P(None, ("img", "dev")), P(None, ("img", "dev")), P(None, ("img", "dev"))),
        check_vma=False,
    )
```

```python
import functools

import jax
import jax.numpy as jnp
from jax import lax
from jax.experimental import pallas as pl
from jax.experimental.pallas import tpu as pltpu
from jax.sharding import PartitionSpec as P

F32, BF16 = jnp.float32, jnp.bfloat16
LOG2E = 1.4426950408889634
FOCAL = 1024.0
CENTRE_U, CENTRE_V = 256.0, 128.0

HARMONIC_ZERO = 0.28209479177387814
HARMONIC_ONE = 0.4886025119029199
HARMONIC_TWO = (
    1.0925484305920792,
    -1.0925484305920792,
    0.31539156525252005,
    -1.0925484305920792,
    0.5462742152960396,
)
HARMONIC_THREE = (
    -0.5900435899266435,
    2.890611442640554,
    -0.4570457994644658,
    0.3731763325901154,
    -0.4570457994644658,
    1.445305721320277,
    -0.5900435899266435,
)


def harmonics(dir_x, dir_y, dir_z):
    square_x = dir_x * dir_x
    square_y = dir_y * dir_y
    square_z = dir_z * dir_z
    return [
        -HARMONIC_ONE * dir_y,
        HARMONIC_ONE * dir_z,
        -HARMONIC_ONE * dir_x,
        HARMONIC_TWO[0] * dir_x * dir_y,
        HARMONIC_TWO[1] * dir_y * dir_z,
        HARMONIC_TWO[2] * (2.0 * square_z - square_x - square_y),
        HARMONIC_TWO[3] * dir_x * dir_z,
        HARMONIC_TWO[4] * (square_x - square_y),
        HARMONIC_THREE[0] * dir_y * (3.0 * square_x - square_y),
        HARMONIC_THREE[1] * dir_x * dir_y * dir_z,
        HARMONIC_THREE[2] * dir_y * (4.0 * square_z - square_x - square_y),
        HARMONIC_THREE[3] * dir_z * (2.0 * square_z - 3.0 * square_x - 3.0 * square_y),
        HARMONIC_THREE[4] * dir_x * (4.0 * square_z - square_x - square_y),
        HARMONIC_THREE[5] * dir_z * (square_x - square_y),
        HARMONIC_THREE[6] * dir_x * (square_x - 3.0 * square_y),
    ]


def project(values, cam):
    m = [[cam[3 * r + c] for c in range(3)] for r in range(3)]
    viewed = [m[r][0] * values[0] + m[r][1] * values[1] + m[r][2] * values[2] + cam[9 + r] for r in range(3)]
    inverse_z = 1.0 / viewed[2]
    centre_u = FOCAL * viewed[0] * inverse_z + CENTRE_U
    centre_v = FOCAL * viewed[1] * inverse_z + CENTRE_V
    scales = [jnp.exp(values[3 + c]) for c in range(3)]
    norm = jnp.sqrt(values[6] * values[6] + values[7] * values[7] + values[8] * values[8] + values[9] * values[9])
    inverse_norm = 1.0 / norm
    w, x, y, z = (values[6 + c] * inverse_norm for c in range(4))
    rot = [
        [1.0 - 2.0 * (y * y + z * z), 2.0 * (x * y - w * z), 2.0 * (x * z + w * y)],
        [2.0 * (x * y + w * z), 1.0 - 2.0 * (x * x + z * z), 2.0 * (y * z - w * x)],
        [2.0 * (x * z - w * y), 2.0 * (y * z + w * x), 1.0 - 2.0 * (x * x + y * y)],
    ]
    focal_z = FOCAL * inverse_z
    jac = [[focal_z * (m[r][c] - viewed[r] * inverse_z * m[2][c]) for c in range(3)] for r in range(2)]
    proj = [
        [(jac[r][0] * rot[0][c] + jac[r][1] * rot[1][c] + jac[r][2] * rot[2][c]) * scales[c] for c in range(3)]
        for r in range(2)
    ]
    cov_xx = proj[0][0] * proj[0][0] + proj[0][1] * proj[0][1] + proj[0][2] * proj[0][2] + 0.3
    cov_xy = proj[0][0] * proj[1][0] + proj[0][1] * proj[1][1] + proj[0][2] * proj[1][2]
    cov_yy = proj[1][0] * proj[1][0] + proj[1][1] * proj[1][1] + proj[1][2] * proj[1][2] + 0.3
    inverse_det = 1.0 / (cov_xx * cov_yy - cov_xy * cov_xy)
    log_opacity = -jnp.log(1.0 + jnp.exp(-values[10]))
    inverse_distance = 1.0 / jnp.sqrt(viewed[0] * viewed[0] + viewed[1] * viewed[1] + viewed[2] * viewed[2])
    terms = harmonics(*[viewed[c] * inverse_distance for c in range(3)])
    colour = []
    for ch in range(3):
        total = 0.5 + HARMONIC_ZERO * values[11 + ch]
        for k in range(1, 16):
            total = total + terms[k - 1] * values[11 + 3 * k + ch]
        colour.append(jnp.maximum(total, 0.0))
    return [centre_u, centre_v, cov_yy * inverse_det, -cov_xy * inverse_det, cov_xx * inverse_det, log_opacity] + colour


def iota(shape, dim):
    return lax.broadcasted_iota(jnp.int32, shape, dim)


def one_hot(truth):
    return jnp.where(truth, 1.0, 0.0).astype(BF16)


def pieces(x, count):
    out = []
    for _ in range(count - 1):
        part = x.astype(BF16)
        out.append(part)
        x = x - part.astype(F32)
    out.append(x.astype(BF16))
    return out


def nn(a, b):
    return lax.dot_general(a, b, (((1,), (0,)), ((), ())), preferred_element_type=F32)


def nt(a, b):
    return lax.dot_general(a, b, (((1,), (1,)), ((), ())), preferred_element_type=F32)


def turned(x):
    rows, columns = x.shape
    side = -columns % 128
    if side:
        x = jnp.concatenate([x, jnp.zeros((rows, side), F32)], axis=1)
    return jnp.transpose(x)[0:columns]


def thirds(x):
    return turned(jnp.concatenate(list(x) + [jnp.zeros((8, 192), F32)], axis=0))


def by_image(x):
    x = jnp.concatenate([x[16 * b:16 * b + 10] for b in range(4)], axis=0)
    last = jnp.concatenate([x[:, 384:512], jnp.zeros((40, 64), F32)], axis=1)
    return thirds([x[:, 0:192], x[:, 192:384], last])


def from_images(x):
    down = turned(x)
    down = jnp.concatenate([down[0:40], down[40:80], down[80:120, 0:128]], axis=1)
    rest = jnp.zeros((6, 512), F32)
    return jnp.concatenate([part for b in range(4) for part in (down[10 * b:10 * b + 10], rest)], axis=0)


def regroup(rows, count, kept):
    lane = iota((count, 128), 1)
    total = jnp.zeros((count, 128), F32)
    for g, x in enumerate(rows):
        moved = x if g == kept else pltpu.roll(x, 40 * (g - kept) % 128, 1)
        total = jnp.where((lane >= 40 * g) & (lane < 40 * g + 40), moved, total)
    return total


def exchange_halves(a, b):
    first = iota(a.shape, len(a.shape) - 1) < 64
    turned_a, turned_b = pltpu.roll(a, 64, len(a.shape) - 1), pltpu.roll(b, 64, len(b.shape) - 1)
    return jnp.where(first, a, turned_b), jnp.where(first, turned_a, b)


def fold(x, count):
    rows = x.shape[0] // count
    total = x[:rows]
    for c in range(1, count):
        total = total + x[c * rows:(c + 1) * rows]
    return total


def owner_tables(send_ref, pick, image_of, weave):
    pick[...] = one_hot(iota((512, 512), 0) == send_ref[...])
    row, column = iota((256, 256), 0), iota((256, 256), 1)
    weave[0] = one_hot(row == column % 64 * 4 + column // 64)
    weave[1] = one_hot(column == row % 64 * 4 + row // 64)
    images = nt((iota((8, 512), 1) // 64).astype(F32).astype(BF16), pick[...])
    own = jnp.where(iota((8, 512), 1) // 64 == iota((8, 512), 0), images, 0.0).astype(BF16)
    image_of[...] = nn(own, one_hot(iota((512, 256), 0) % 64 == iota((512, 256), 1) // 4))


def as_column(row):
    row = row.astype(F32)
    row = jnp.concatenate([row, jnp.zeros((128 - row.shape[0], row.shape[1]), F32)], axis=0)
    return jnp.transpose(row)


def owner_tables_back(send_ref, pick_back):
    pick_back[...] = one_hot(iota((512, 512), 1) == as_column(send_ref[...])[:, 0:1].astype(jnp.int32))


def cameras_of(cam_ref, image_of):
    image = image_of[...]
    masks = [image == float(i) for i in range(8)]
    cams = cam_ref[...]
    out = []
    for t in range(12):
        value = jnp.zeros((8, 256), F32)
        for i in range(8):
            value = jnp.where(masks[i], cams[i:i + 1, t:t + 1], value)
        out.append(value)
    return out


def owner_forward(cam_ref, pick, image_of, weave, par3, shown3, put):
    shown = project([par3[c] for c in range(59)], cameras_of(cam_ref, image_of))
    for q in range(9):
        shown3[q] = shown[q]
    for q in range(9, 16):
        shown3[q] = jnp.zeros((8, 256), F32)
    flat = shown3[0:10].reshape(80, 256)
    shown3[0:10] = fold(nn(jnp.concatenate(pieces(flat, 3), axis=0), weave[0]), 3).reshape(10, 8, 256)
    rows = [[], [], [], []]
    for p in range(2):
        at = slice(128 * p, 128 * (p + 1))
        for t in range(4):
            even, odd = exchange_halves(shown3[:, 2 * t, at], shown3[:, 2 * t + 1, at])
            rows[2 * p].append(even)
            rows[2 * p + 1].append(odd)
    rows = jnp.concatenate([jnp.concatenate(row, axis=1) for row in rows], axis=0)
    put(by_image(fold(nn(jnp.concatenate(pieces(rows, 3), axis=0), pick[...]), 3)))


def owner_pullback(cam_ref, image_of, par3):
    cams = cameras_of(cam_ref, image_of)
    return jax.vjp(lambda v: project(v, cams), [par3[c] for c in range(59)])[1]


def owner_gradient(got, pullback, pick_back, weave, shown3, grad3):
    spread = fold(nn(jnp.concatenate(pieces(from_images(got), 2), axis=0), pick_back[...]), 2)
    for p in range(2):
        at = slice(128 * p, 128 * (p + 1))
        for t in range(4):
            lanes = slice(128 * t, 128 * (t + 1))
            even, odd = exchange_halves(spread[32 * p:32 * p + 16, lanes], spread[32 * p + 16:32 * p + 32, lanes])
            shown3[:, 2 * t, at] = even
            shown3[:, 2 * t + 1, at] = odd
    flat = shown3[0:10].reshape(80, 256)
    slopes = fold(nn(jnp.concatenate(pieces(flat, 2), axis=0), weave[1]), 2).reshape(10, 8, 256)
    (grads,) = pullback([slopes[q] for q in range(9)])
    for c in range(59):
        grad3[c] = grads[c]


def renderer_tables(
    lists_ref, order_ref, where_ref, live_ref, target_ref, listed, sort, place, tri, wanted, listed_back, sort_back, power,
    tile3, coef3, grad3,
):
    def owner_at(h, spot):
        column = 24 * h + spot % 24
        return jnp.where(column < 64, spot // 24 * 64 + column, -1)

    column = as_column(lists_ref[...])[:, 0:1].astype(jnp.int32)
    for h in range(3):
        listed[h] = one_hot(owner_at(h, iota((192, 512), 0)) == lists_ref[...])
        listed_back[h] = one_hot(owner_at(h, iota((512, 192), 1)) == column)

    def one_tile(n, carry):
        order = order_ref[pl.ds(n, 1), :]
        key = (order % 4) * 128 + (n % 2) * 64 + order // 4
        sort[n] = one_hot(iota((512, 256), 0) == key)
        return carry

    lax.fori_loop(0, 8, one_tile, 0)
    order = order_ref[...]
    column = as_column((order % 4) * 128 + (iota((8, 256), 0) % 2) * 64 + order // 4)
    for n in range(8):
        sort_back[n] = one_hot(iota((256, 512), 1) == column[:, n:n + 1].astype(jnp.int32))
    lane = iota((8, 512), 1)
    tile = lane // 64
    where = jnp.zeros((8, 512), jnp.int32)
    live = jnp.zeros((8, 512), jnp.int32)
    for n in range(8):
        where = jnp.where(tile == n, where_ref[0:1, n:n + 1], where)
        live = jnp.where(tile == n, live_ref[0:1, n:n + 1], live)
    place[0] = (where % 32 * 16 + 8).astype(F32)
    place[1] = (where // 32 * 16 + 8).astype(F32)
    place[2] = jnp.where(lane % 64 < live, 1.0, 0.0)
    tri[0] = one_hot(iota((512, 256), 0) % 256 < iota((512, 256), 1))
    tri[1] = one_hot(iota((512, 256), 0) % 256 > iota((512, 256), 1))
    for n in range(8):
        rows = [target_ref[n:n + 1, 256 * ch:256 * (ch + 1)] for ch in range(3)]
        wanted[n] = jnp.transpose(jnp.concatenate(rows + [jnp.zeros((125, 256), F32)], axis=0))[:, 0:8]
    power[...] = monomials(iota((256, 48), 0), iota((256, 48), 1) % 16)
    for held in (tile3, coef3, grad3):
        held[...] = jnp.zeros(held.shape, F32)


def monomials(pixel, term):
    x = (pixel % 16).astype(F32) - 7.5
    y = (pixel // 16).astype(F32) - 7.5
    out = jnp.zeros(pixel.shape, F32)
    for t, value in enumerate((jnp.ones_like(x), x, y, x * x, x * y, y * y)):
        out = jnp.where(term == t, value, out)
    return out.astype(BF16)


def render(
    got, listed, sort, place, tri, wanted, listed_back, sort_back, power, tile3, coef3, grad3, front3, alpha3, weight3, split3, put
):
    rows = turned(got)
    tiles = jnp.zeros((48, 512), F32)
    for h in range(3):
        third = jnp.concatenate([rows[40 * h:40 * h + 40], jnp.zeros((8, 192), F32)], axis=0)
        tiles = tiles + fold(nn(jnp.concatenate(pieces(third, 3), axis=0), listed[h]), 3)
    for b in range(4):
        tile3[0:10, b, :] = tiles[10 * b:10 * b + 10]
    centre_x, centre_y, live = place[0, 0:4], place[1, 0:4], place[2, 0:4]

    def geometry():
        u, v, cxx, cxy, cyy, log_op = (tile3[q, 0:4] for q in range(6))
        return u - centre_x, v - centre_y, cxx, cxy, cyy, log_op

    u, v, cxx, cxy, cyy, log_op = geometry()
    a, b2, c2 = -0.5 * LOG2E * cxx, -LOG2E * cxy, -0.5 * LOG2E * cyy
    constant = a * u * u + b2 * u * v + c2 * v * v + LOG2E * log_op
    coefs = [
        jnp.where(live > 0.0, constant, -1e5),
        jnp.where(live > 0.0, -2.0 * a * u - b2 * v, 0.0),
        jnp.where(live > 0.0, -2.0 * c2 * v - b2 * u, 0.0),
        jnp.where(live > 0.0, a, 0.0),
        jnp.where(live > 0.0, b2, 0.0),
        jnp.where(live > 0.0, c2, 0.0),
    ] + [tile3[q, 0:4] for q in range(6, 9)]
    for c in range(9):
        coef3[c, 0:4] = coefs[c]
    column = iota((16, 256), 0).astype(F32) - 7.5
    zero8 = jnp.zeros((8, 256), F32)

    for n in range(8):
        pair = slice(128 * (n // 2), 128 * (n // 2) + 128)
        mine = jnp.concatenate([coef3[:, b, pair] for b in range(4)], axis=1)
        sorted_parts = nn(jnp.concatenate(pieces(mine, 3), axis=0), sort[n])
        front = fold(sorted_parts, 3)
        front3[n] = jnp.where(iota((8, 256), 0) < 3, pltpu.roll(front, 10, 0)[0:8], 0.0)
        alpha = jnp.exp2(nn(power[...], sorted_parts.astype(BF16)))
        alpha3[n] = alpha
        split3[n] = jnp.concatenate(pieces(jnp.log(1.0 - alpha), 2), axis=1)
    for n in range(8):
        weight = jnp.exp(nn(split3[n], tri[0])) * alpha3[n]
        weight3[n] = weight
        split3[n] = jnp.concatenate(pieces(weight, 2), axis=1)
    for n in range(8):
        colour = front3[n]
        c_all = jnp.concatenate(pieces(colour, 2), axis=0)
        both = nt(split3[n], jnp.concatenate([c_all, c_all], axis=1))
        residual = both[:, 0:8] + both[:, 8:16] - wanted[n]
        weight = weight3[n]
        gain = jnp.zeros((256, 256), F32)
        shades = []
        for ch in range(3):
            gain = gain + residual[:, ch:ch + 1] * colour[ch:ch + 1]
            shades.append(jnp.sum(residual[:, ch:ch + 1] * weight, axis=0, keepdims=True))
        passed = weight * gain
        weight3[n] = passed
        split3[n] = jnp.concatenate(pieces(passed, 2), axis=1)
        front3[n] = jnp.concatenate(shades + [zero8[0:5]], axis=0)
    for n in range(8):
        alpha = alpha3[n]
        keep = 1.0 - alpha
        guess = pl.reciprocal(keep, approx=True)
        inverse = guess * (2.0 - keep * guess)
        behind = nn(split3[n], tri[1])
        change = (weight3[n] - behind * (alpha * inverse)).reshape(16, 16, 256)
        s0, s1, s2 = change[0], -7.5 * change[0], 56.25 * change[0]
        for y in range(1, 16):
            s0 = s0 + change[y]
            s1 = s1 + (y - 7.5) * change[y]
            s2 = s2 + (y - 7.5) * (y - 7.5) * change[y]
        moments = [s0, s0 * column, s1, s0 * column * column, s1 * column, s2]
        back = jnp.concatenate([jnp.sum(m, axis=0, keepdims=True) for m in moments] + [zero8[0:2], front3[n]], axis=0)
        pair = slice(128 * (n // 2), 128 * (n // 2) + 128)
        spread = fold(nn(jnp.concatenate(pieces(back, 3), axis=0), sort_back[n]), 3)
        for b in range(4):
            grad3[:, b, pair] += spread[:, 128 * b:128 * (b + 1)]

    m0, mx, my, mxx, mxy, myy = (grad3[t, 0:4] for t in range(6))
    u, v, cxx, cxy, cyy, _ = geometry()
    hx, hy = mx - u * m0, my - v * m0
    hxx = mxx - 2.0 * u * mx + u * u * m0
    hxy = mxy - u * my - v * mx + u * v * m0
    hyy = myy - 2.0 * v * my + v * v * m0
    results = [cxx * hx + cxy * hy, cxy * hx + cyy * hy, -0.5 * hxx, -hxy, -0.5 * hyy, m0]
    results += [grad3[8 + ch, 0:4] for ch in range(3)]
    for q in range(9):
        tile3[q, 0:4] = results[q]
    for q in range(9, 16):
        tile3[q, 0:4] = jnp.zeros((4, 512), F32)
    rows = jnp.concatenate([tile3[0:10, b, :] for b in range(4)] + [jnp.zeros((8, 512), F32)], axis=0)
    parts = jnp.concatenate(pieces(rows, 2), axis=0)
    put(thirds([fold(nn(parts, listed_back[h]), 2)[0:40] for h in range(3)]))


def rate_column():
    row = iota((59, 1), 0)
    rate = jnp.full((59, 1), 0.000125, F32)
    for end, value in ((14, 0.0025), (11, 0.05), (10, 0.001), (6, 0.005), (3, 0.00016)):
        rate = jnp.where(row < end, value, rate)
    return rate


def adam(both_ref, params_ref, first_ref, out_params, out_first, out_second, held_p, held_f, held_s, sems):
    rate = rate_column()
    copies = []
    for c in range(8):
        at = slice(8 * c, min(8 * c + 8, 59))
        gradient = both_ref[0, at, :]
        first = 0.9 * first_ref[at, :] + 0.1 * gradient
        second = 0.999 * both_ref[1, at, :] + 0.001 * gradient * gradient
        held_f[at, :] = first
        held_s[at, :] = second
        held_p[at, :] = params_ref[at, :] - rate[at] * first / (jnp.sqrt(second) + 1e-15)
        for part, (held, out) in enumerate(((held_p, out_params), (held_f, out_first), (held_s, out_second))):
            copy = pltpu.make_async_copy(held.at[at, :], out.at[at, :], sems.at[3 * c + part])
            copy.start()
            copies.append(copy)
    for copy in copies:
        copy.wait()


OWNER_SCRATCH = [
    pltpu.VMEM((512, 512), BF16),
    pltpu.VMEM((8, 256), F32),
    pltpu.VMEM((2, 256, 256), BF16),
    pltpu.VMEM((59, 8, 256), F32),
    pltpu.VMEM((16, 8, 256), F32),
    pltpu.VMEM((512, 512), BF16),
]
RENDER_SCRATCH = [
    pltpu.VMEM((3, 192, 512), BF16),
    pltpu.VMEM((8, 512, 256), BF16),
    pltpu.VMEM((3, 8, 512), F32),
    pltpu.VMEM((2, 512, 256), BF16),
    pltpu.VMEM((8, 256, 8), F32),
    pltpu.VMEM((3, 512, 192), BF16),
    pltpu.VMEM((8, 256, 512), BF16),
    pltpu.VMEM((256, 48), BF16),
    pltpu.VMEM((16, 8, 512), F32),
    pltpu.VMEM((16, 8, 512), F32),
    pltpu.VMEM((16, 8, 512), F32),
    pltpu.VMEM((8, 8, 256), F32),
    pltpu.VMEM((8, 256, 256), F32),
    pltpu.VMEM((8, 256, 256), F32),
    pltpu.VMEM((8, 256, 512), BF16),
]


def landed(ref, sem):
    pltpu.make_async_copy(ref, ref, sem).wait()


def step(
    params_hbm, send_hbm, lists_hbm, order_hbm, where_hbm, live_hbm, target_hbm, camera_hbm, second_hbm, out_ref,
    send_ref, lists_ref, order_ref, where_ref, live_ref, target_ref, camera_ref, in_sems,
    pick, image_of, weave, par3, shown3, pick_back, owner3,
    listed, sort, place, tri, wanted, listed_back, sort_back, power, tile3, coef3, grad3, front3, alpha3, weight3, split3,
    cam_row, cams, shown_out, shown_mid, back_send, back_in, shown_send, shown_in, back_out, back_mid, send_sems, recv_sems, own_sem,
):
    i = lax.axis_index("img")
    j = lax.axis_index("dev")
    mesh_ids = pl.DeviceIdType.MESH

    barrier = pltpu.get_barrier_semaphore()
    for s in range(1, 8):
        pl.semaphore_signal(barrier, inc=1, device_id=(lax.rem(i + s, 8), j), device_id_type=mesh_ids)

    @pl.loop(1, 64)
    def _(s):
        pl.semaphore_signal(barrier, inc=1, device_id=(i, lax.rem(j + s, 64)), device_id_type=mesh_ids)

    loads = [
        pltpu.make_async_copy(source, target, in_sems.at[c])
        for c, (source, target) in enumerate(
            [(camera_hbm, camera_ref), (send_hbm, send_ref)]
            + [(params_hbm.at[:, pl.ds(256 * g, 256)], par3.at[:, g, :]) for g in range(8)]
            + [(lists_hbm, lists_ref), (order_hbm, order_ref), (where_hbm, where_ref), (live_hbm, live_ref)]
            + [(target_hbm, target_ref), (second_hbm, out_ref.at[1])]
        )
    ]
    for load in loads:
        load.start()
    cam_row[...] = jnp.zeros((8, 128), F32)
    loads[0].wait()
    cam_row[0:1, 0:12] = camera_ref[...]
    pl.semaphore_wait(barrier, 70)

    def to_img(source, target, phase):
        for s in (4, 3, 5, 2, 6, 1, 7):
            t = lax.rem(i + s, 8)
            pltpu.make_async_remote_copy(
                src_ref=source(t),
                dst_ref=target,
                send_sem=send_sems.at[phase],
                recv_sem=recv_sems.at[phase],
                device_id=(t, j),
                device_id_type=mesh_ids,
            ).start()
        own = pltpu.make_async_copy(source(i), target, own_sem)
        own.start()
        own.wait()

    def to_dev(source, target, phase):
        def one(s, carry):
            t = lax.rem(j + s, 64)
            pltpu.make_async_remote_copy(
                src_ref=source.at[t],
                dst_ref=target.at[j],
                send_sem=send_sems.at[phase],
                recv_sem=recv_sems.at[phase],
                device_id=(i, t),
                device_id_type=mesh_ids,
            ).start()
            return carry

        lax.fori_loop(1, 64, one, 0)
        own = pltpu.make_async_copy(source.at[j], target.at[j], own_sem)
        own.start()
        own.wait()

    to_img(lambda t: cam_row.at[pl.ds(0, 1)], cams.at[pl.ds(i, 1)], 0)
    loads[1].wait()
    owner_tables(send_ref, pick, image_of, weave)
    landed(cams.at[pl.ds(0, 7)], recv_sems.at[0])

    def put_shown(x):
        for r in range(3):
            shown_out[:, r, :] = x[64 * r:64 * (r + 1)]

    for load in loads[2:10]:
        load.wait()
    owner_forward(cams, pick, image_of, weave, par3, shown3, put_shown)
    to_dev(shown_out, shown_mid, 1)
    for load in loads[10:]:
        load.wait()
    renderer_tables(
        lists_ref, order_ref, where_ref, live_ref, target_ref,
        listed, sort, place, tri, wanted, listed_back, sort_back, power, tile3, coef3, grad3,
    )
    landed(shown_mid.at[pl.ds(0, 63)], recv_sems.at[1])
    for r in range(3):
        rows = [shown_mid[0:24, r, :], shown_mid[24:48, r, :]]
        rows.append(jnp.concatenate([shown_mid[48:64, r, :], jnp.zeros((8, 128), F32)], axis=0))
        for g in range(3 if r < 2 else 2):
            shown_send[3 * g + r] = regroup(rows, 24, g)
    to_img(lambda t: shown_send.at[t], shown_in.at[i], 2)
    owner_tables_back(send_ref, pick_back)
    landed(shown_in.at[pl.ds(0, 7)], recv_sems.at[2])

    def put_back(x):
        back_out[...] = x.reshape(8, 24, 128)

    render(
        shown_in[...].reshape(192, 128),
        listed, sort, place, tri, wanted, listed_back, sort_back, power, tile3, coef3, grad3, front3, alpha3, weight3, split3,
        put_back,
    )
    to_img(lambda t: back_out.at[t], back_mid.at[i], 3)
    landed(back_mid.at[pl.ds(0, 7)], recv_sems.at[3])
    for r in range(3):
        for h in range(3):
            count = 24 if h < 2 else 16
            rows = [back_mid[3 * g + r, 0:count, :] for g in range(3 if r < 2 else 2)]
            back_send[24 * h:24 * h + count, r, :] = regroup(rows, count, h)
    to_dev(back_send, back_in, 4)
    pullback = owner_pullback(cams, image_of, par3)
    landed(back_in.at[pl.ds(0, 63)], recv_sems.at[4])
    got = jnp.concatenate([back_in[:, p, :] for p in range(3)], axis=0)
    owner_gradient(got, pullback, pick_back, weave, shown3, owner3)
    for g in range(8):
        out_ref[0, :, 256 * g:256 * (g + 1)] = owner3[:, g, :]
    landed(cams.at[pl.ds(0, 7)], send_sems.at[0])
    landed(shown_out.at[pl.ds(0, 63)], send_sems.at[1])
    landed(shown_send.at[pl.ds(0, 7)], send_sems.at[2])
    landed(back_out.at[pl.ds(0, 7)], send_sems.at[3])
    landed(back_send.at[pl.ds(0, 63)], send_sems.at[4])


def local(
    params, first_moment, second_moment, send_blocks, tile_blocks, tile_live, depth_order, tile_where, target, camera
):
    vmem = pl.BlockSpec(memory_space=pltpu.VMEM)
    whole = pl.BlockSpec(memory_space=pltpu.HBM)
    integer = jnp.int32
    by_dev = pltpu.VMEM((64, 3, 128), F32)
    by_img = pltpu.VMEM((8, 24, 128), F32)
    operands = (
        params,
        send_blocks,
        tile_blocks.reshape(1, 512),
        depth_order.reshape(8, 256),
        tile_where,
        tile_live,
        target.reshape(8, 768),
        camera,
        second_moment,
    )
    shape = jax.ShapeDtypeStruct((59, 2048), F32)
    gradient_second = pl.pallas_call(
        step,
        out_shape=jax.ShapeDtypeStruct((2, 59, 2048), F32),
        in_specs=[whole] * 9,
        out_specs=vmem,
        scratch_shapes=[
            pltpu.VMEM((1, 512), integer),
            pltpu.VMEM((1, 512), integer),
            pltpu.VMEM((8, 256), integer),
            pltpu.VMEM((1, 8), integer),
            pltpu.VMEM((1, 8), integer),
            pltpu.VMEM((8, 768), F32),
            pltpu.VMEM((1, 12), F32),
            pltpu.SemaphoreType.DMA((16,)),
        ]
        + OWNER_SCRATCH
        + [pltpu.VMEM((59, 8, 256), F32)]
        + RENDER_SCRATCH
        + [pltpu.VMEM((8, 128), F32)] * 2
        + [by_dev] * 4
        + [by_img] * 4
        + [pltpu.SemaphoreType.DMA((5,)), pltpu.SemaphoreType.DMA((5,)), pltpu.SemaphoreType.DMA],
        compiler_params=pltpu.CompilerParams(collective_id=0, has_side_effects=True, vmem_limit_bytes=24 << 20),
    )(*[pltpu.with_memory_space_constraint(operand, pltpu.HBM) for operand in operands])
    return pl.pallas_call(
        adam,
        out_shape=(shape, shape, shape),
        in_specs=[vmem] * 3,
        out_specs=(whole, whole, whole),
        scratch_shapes=[pltpu.VMEM((59, 2048), F32)] * 3 + [pltpu.SemaphoreType.DMA((24,))],
        compiler_params=pltpu.CompilerParams(vmem_limit_bytes=16 << 20),
    )(gradient_second, params, first_moment)


def solution(mesh):
    return jax.shard_map(
        local,
        mesh=mesh,
        in_specs=(
            P(None, ("img", "dev")),
            P(None, ("img", "dev")),
            P(None, ("img", "dev")),
            P(("img", "dev"), None),
            P("img", "dev", None),
            P("img", "dev"),
            P("img", "dev", None),
            P("img", "dev"),
            P("img", "dev", None),
            P("img", None),
        ),
        out_specs=(P(None, ("img", "dev")), P(None, ("img", "dev")), P(None, ("img", "dev"))),
        check_vma=False,
    )
```

```python
import functools

import jax
import jax.numpy as jnp
from jax import lax
from jax.experimental import pallas as pl
from jax.experimental.pallas import tpu as pltpu
from jax.sharding import PartitionSpec as P

F32, BF16 = jnp.float32, jnp.bfloat16
LOG2E = 1.4426950408889634
FOCAL = 1024.0
CENTRE_U, CENTRE_V = 256.0, 128.0

HARMONIC_ZERO = 0.28209479177387814
HARMONIC_ONE = 0.4886025119029199
HARMONIC_TWO = (
    1.0925484305920792,
    -1.0925484305920792,
    0.31539156525252005,
    -1.0925484305920792,
    0.5462742152960396,
)
HARMONIC_THREE = (
    -0.5900435899266435,
    2.890611442640554,
    -0.4570457994644658,
    0.3731763325901154,
    -0.4570457994644658,
    1.445305721320277,
    -0.5900435899266435,
)


def harmonics(dir_x, dir_y, dir_z):
    square_x = dir_x * dir_x
    square_y = dir_y * dir_y
    square_z = dir_z * dir_z
    return [
        -HARMONIC_ONE * dir_y,
        HARMONIC_ONE * dir_z,
        -HARMONIC_ONE * dir_x,
        HARMONIC_TWO[0] * dir_x * dir_y,
        HARMONIC_TWO[1] * dir_y * dir_z,
        HARMONIC_TWO[2] * (2.0 * square_z - square_x - square_y),
        HARMONIC_TWO[3] * dir_x * dir_z,
        HARMONIC_TWO[4] * (square_x - square_y),
        HARMONIC_THREE[0] * dir_y * (3.0 * square_x - square_y),
        HARMONIC_THREE[1] * dir_x * dir_y * dir_z,
        HARMONIC_THREE[2] * dir_y * (4.0 * square_z - square_x - square_y),
        HARMONIC_THREE[3] * dir_z * (2.0 * square_z - 3.0 * square_x - 3.0 * square_y),
        HARMONIC_THREE[4] * dir_x * (4.0 * square_z - square_x - square_y),
        HARMONIC_THREE[5] * dir_z * (square_x - square_y),
        HARMONIC_THREE[6] * dir_x * (square_x - 3.0 * square_y),
    ]


def shape_of(values):
    scales = [jnp.exp(values[3 + c]) for c in range(3)]
    norm = jnp.sqrt(values[6] * values[6] + values[7] * values[7] + values[8] * values[8] + values[9] * values[9])
    inverse_norm = 1.0 / norm
    w, x, y, z = (values[6 + c] * inverse_norm for c in range(4))
    rot = [
        [1.0 - 2.0 * (y * y + z * z), 2.0 * (x * y - w * z), 2.0 * (x * z + w * y)],
        [2.0 * (x * y + w * z), 1.0 - 2.0 * (x * x + z * z), 2.0 * (y * z - w * x)],
        [2.0 * (x * z - w * y), 2.0 * (y * z + w * x), 1.0 - 2.0 * (x * x + y * y)],
    ]
    return rot, scales, -jnp.log(1.0 + jnp.exp(-values[10]))


def project(values, cam, shape=None):
    rot, scales, log_opacity = shape_of(values) if shape is None else shape
    m = [[cam[3 * r + c] for c in range(3)] for r in range(3)]
    viewed = [m[r][0] * values[0] + m[r][1] * values[1] + m[r][2] * values[2] + cam[9 + r] for r in range(3)]
    inverse_z = 1.0 / viewed[2]
    centre_u = FOCAL * viewed[0] * inverse_z + CENTRE_U
    centre_v = FOCAL * viewed[1] * inverse_z + CENTRE_V
    focal_z = FOCAL * inverse_z
    jac = [[focal_z * (m[r][c] - viewed[r] * inverse_z * m[2][c]) for c in range(3)] for r in range(2)]
    proj = [
        [(jac[r][0] * rot[0][c] + jac[r][1] * rot[1][c] + jac[r][2] * rot[2][c]) * scales[c] for c in range(3)]
        for r in range(2)
    ]
    cov_xx = proj[0][0] * proj[0][0] + proj[0][1] * proj[0][1] + proj[0][2] * proj[0][2] + 0.3
    cov_xy = proj[0][0] * proj[1][0] + proj[0][1] * proj[1][1] + proj[0][2] * proj[1][2]
    cov_yy = proj[1][0] * proj[1][0] + proj[1][1] * proj[1][1] + proj[1][2] * proj[1][2] + 0.3
    inverse_det = 1.0 / (cov_xx * cov_yy - cov_xy * cov_xy)
    inverse_distance = 1.0 / jnp.sqrt(viewed[0] * viewed[0] + viewed[1] * viewed[1] + viewed[2] * viewed[2])
    terms = harmonics(*[viewed[c] * inverse_distance for c in range(3)])
    colour = []
    for ch in range(3):
        total = 0.5 + HARMONIC_ZERO * values[11 + ch]
        for k in range(1, 16):
            total = total + terms[k - 1] * values[11 + 3 * k + ch]
        colour.append(jnp.maximum(total, 0.0))
    return [centre_u, centre_v, cov_yy * inverse_det, -cov_xy * inverse_det, cov_xx * inverse_det, log_opacity] + colour


def iota(shape, dim):
    return lax.broadcasted_iota(jnp.int32, shape, dim)


def one_hot(truth):
    return jnp.where(truth, 1.0, 0.0).astype(BF16)


def pieces(x, count):
    out = []
    for _ in range(count - 1):
        part = x.astype(BF16)
        out.append(part)
        x = x - part.astype(F32)
    out.append(x.astype(BF16))
    return out


def nn(a, b):
    return lax.dot_general(a, b, (((1,), (0,)), ((), ())), preferred_element_type=F32)


def nt(a, b):
    return lax.dot_general(a, b, (((1,), (1,)), ((), ())), preferred_element_type=F32)


def turned(x):
    rows, columns = x.shape
    side = -columns % 128
    if side:
        x = jnp.concatenate([x, jnp.zeros((rows, side), F32)], axis=1)
    return jnp.transpose(x)[0:columns]


def thirds(x):
    return turned(jnp.concatenate(list(x) + [jnp.zeros((8, 192), F32)], axis=0))


def by_image(x):
    x = jnp.concatenate([x[16 * b:16 * b + 10] for b in range(4)], axis=0)
    last = jnp.concatenate([x[:, 384:512], jnp.zeros((40, 64), F32)], axis=1)
    return thirds([x[:, 0:192], x[:, 192:384], last])


def from_images(x):
    down = turned(x)
    down = jnp.concatenate([down[0:40], down[40:80], down[80:120, 0:128]], axis=1)
    rest = jnp.zeros((6, 512), F32)
    return jnp.concatenate([part for b in range(4) for part in (down[10 * b:10 * b + 10], rest)], axis=0)


def regroup(rows, count, kept):
    lane = iota((count, 128), 1)
    total = jnp.zeros((count, 128), F32)
    for g, x in enumerate(rows):
        moved = x if g == kept else pltpu.roll(x, 40 * (g - kept) % 128, 1)
        total = jnp.where((lane >= 40 * g) & (lane < 40 * g + 40), moved, total)
    return total


def exchange_halves(a, b):
    first = iota(a.shape, len(a.shape) - 1) < 64
    turned_a, turned_b = pltpu.roll(a, 64, len(a.shape) - 1), pltpu.roll(b, 64, len(b.shape) - 1)
    return jnp.where(first, a, turned_b), jnp.where(first, turned_a, b)


def fold(x, count):
    rows = x.shape[0] // count
    total = x[:rows]
    for c in range(1, count):
        total = total + x[c * rows:(c + 1) * rows]
    return total


def owner_tables(send_ref, pick, image_of, weave):
    pick[...] = one_hot(iota((512, 512), 0) == send_ref[...])
    row, column = iota((256, 256), 0), iota((256, 256), 1)
    weave[0] = one_hot(row == column % 64 * 4 + column // 64)
    weave[1] = one_hot(column == row % 64 * 4 + row // 64)
    images = nt((iota((8, 512), 1) // 64).astype(F32).astype(BF16), pick[...])
    own = jnp.where(iota((8, 512), 1) // 64 == iota((8, 512), 0), images, 0.0).astype(BF16)
    image_of[...] = nn(own, one_hot(iota((512, 256), 0) % 64 == iota((512, 256), 1) // 4))


def as_column(row):
    row = row.astype(F32)
    row = jnp.concatenate([row, jnp.zeros((128 - row.shape[0], row.shape[1]), F32)], axis=0)
    return jnp.transpose(row)


def owner_tables_back(send_ref, pick_back):
    pick_back[...] = one_hot(iota((512, 512), 1) == as_column(send_ref[...])[:, 0:1].astype(jnp.int32))


def cameras_of(cam_ref, image_of):
    image = image_of[...]
    masks = [image == float(i) for i in range(8)]
    cams = cam_ref[...]
    out = []
    for t in range(12):
        value = jnp.zeros((8, 256), F32)
        for i in range(8):
            value = jnp.where(masks[i], cams[i:i + 1, t:t + 1], value)
        out.append(value)
    return out


def owner_forward(cam_ref, pick, image_of, weave, par3, shown3, shape, put):
    shown = project([par3[c] for c in range(59)], cameras_of(cam_ref, image_of), shape)
    for q in range(9):
        shown3[q] = shown[q]
    for q in range(9, 16):
        shown3[q] = jnp.zeros((8, 256), F32)
    flat = shown3[0:10].reshape(80, 256)
    shown3[0:10] = fold(nn(jnp.concatenate(pieces(flat, 3), axis=0), weave[0]), 3).reshape(10, 8, 256)
    rows = [[], [], [], []]
    for p in range(2):
        at = slice(128 * p, 128 * (p + 1))
        for t in range(4):
            even, odd = exchange_halves(shown3[:, 2 * t, at], shown3[:, 2 * t + 1, at])
            rows[2 * p].append(even)
            rows[2 * p + 1].append(odd)
    rows = jnp.concatenate([jnp.concatenate(row, axis=1) for row in rows], axis=0)
    put(by_image(fold(nn(jnp.concatenate(pieces(rows, 3), axis=0), pick[...]), 3)))


def owner_pullback(cam_ref, image_of, par3):
    cams = cameras_of(cam_ref, image_of)
    return jax.vjp(lambda v: project(v, cams), [par3[c] for c in range(59)])[1]


def owner_gradient(got, pullback, pick_back, weave, shown3, grad3):
    spread = fold(nn(jnp.concatenate(pieces(from_images(got), 2), axis=0), pick_back[...]), 2)
    for p in range(2):
        at = slice(128 * p, 128 * (p + 1))
        for t in range(4):
            lanes = slice(128 * t, 128 * (t + 1))
            even, odd = exchange_halves(spread[32 * p:32 * p + 16, lanes], spread[32 * p + 16:32 * p + 32, lanes])
            shown3[:, 2 * t, at] = even
            shown3[:, 2 * t + 1, at] = odd
    flat = shown3[0:10].reshape(80, 256)
    slopes = fold(nn(jnp.concatenate(pieces(flat, 2), axis=0), weave[1]), 2).reshape(10, 8, 256)
    (grads,) = pullback([slopes[q] for q in range(9)])
    for c in range(59):
        grad3[c] = grads[c]


def renderer_tables(
    lists_ref, order_ref, where_ref, live_ref, target_ref, listed, sort, place, tri, wanted, listed_back, sort_back, power,
    tile3, coef3, grad3,
):
    def owner_at(h, spot):
        column = 24 * h + spot % 24
        return jnp.where(column < 64, spot // 24 * 64 + column, -1)

    column = as_column(lists_ref[...])[:, 0:1].astype(jnp.int32)
    for h in range(3):
        listed[h] = one_hot(owner_at(h, iota((192, 512), 0)) == lists_ref[...])
        listed_back[h] = one_hot(owner_at(h, iota((512, 192), 1)) == column)

    def one_tile(n, carry):
        order = order_ref[pl.ds(n, 1), :]
        key = (order % 4) * 128 + (n % 2) * 64 + order // 4
        sort[n] = one_hot(iota((512, 256), 0) == key)
        return carry

    lax.fori_loop(0, 8, one_tile, 0)
    order = order_ref[...]
    column = as_column((order % 4) * 128 + (iota((8, 256), 0) % 2) * 64 + order // 4)
    for n in range(8):
        sort_back[n] = one_hot(iota((256, 512), 1) == column[:, n:n + 1].astype(jnp.int32))
    lane = iota((8, 512), 1)
    tile = lane // 64
    where = jnp.zeros((8, 512), jnp.int32)
    live = jnp.zeros((8, 512), jnp.int32)
    for n in range(8):
        where = jnp.where(tile == n, where_ref[0:1, n:n + 1], where)
        live = jnp.where(tile == n, live_ref[0:1, n:n + 1], live)
    place[0] = (where % 32 * 16 + 8).astype(F32)
    place[1] = (where // 32 * 16 + 8).astype(F32)
    place[2] = jnp.where(lane % 64 < live, 1.0, 0.0)
    tri[0] = one_hot(iota((512, 256), 0) % 256 < iota((512, 256), 1))
    tri[1] = one_hot(iota((512, 256), 0) % 256 > iota((512, 256), 1))
    for n in range(8):
        rows = [target_ref[n:n + 1, 256 * ch:256 * (ch + 1)] for ch in range(3)]
        wanted[n] = jnp.transpose(jnp.concatenate(rows + [jnp.zeros((125, 256), F32)], axis=0))[:, 0:8]
    power[...] = monomials(iota((256, 48), 0), iota((256, 48), 1) % 16)
    for held in (tile3, coef3, grad3):
        held[...] = jnp.zeros(held.shape, F32)


def monomials(pixel, term):
    x = (pixel % 16).astype(F32) - 7.5
    y = (pixel // 16).astype(F32) - 7.5
    out = jnp.zeros(pixel.shape, F32)
    for t, value in enumerate((jnp.ones_like(x), x, y, x * x, x * y, y * y)):
        out = jnp.where(term == t, value, out)
    return out.astype(BF16)


def render(
    got, listed, sort, place, tri, wanted, listed_back, sort_back, power, tile3, coef3, grad3, front3, alpha3, weight3, split3, put
):
    rows = turned(got)
    tiles = jnp.zeros((48, 512), F32)
    for h in range(3):
        third = jnp.concatenate([rows[40 * h:40 * h + 40], jnp.zeros((8, 192), F32)], axis=0)
        tiles = tiles + fold(nn(jnp.concatenate(pieces(third, 3), axis=0), listed[h]), 3)
    for b in range(4):
        tile3[0:10, b, :] = tiles[10 * b:10 * b + 10]
    centre_x, centre_y, live = place[0, 0:4], place[1, 0:4], place[2, 0:4]

    def geometry():
        u, v, cxx, cxy, cyy, log_op = (tile3[q, 0:4] for q in range(6))
        return u - centre_x, v - centre_y, cxx, cxy, cyy, log_op

    u, v, cxx, cxy, cyy, log_op = geometry()
    a, b2, c2 = -0.5 * LOG2E * cxx, -LOG2E * cxy, -0.5 * LOG2E * cyy
    constant = a * u * u + b2 * u * v + c2 * v * v + LOG2E * log_op
    coefs = [
        jnp.where(live > 0.0, constant, -1e5),
        jnp.where(live > 0.0, -2.0 * a * u - b2 * v, 0.0),
        jnp.where(live > 0.0, -2.0 * c2 * v - b2 * u, 0.0),
        jnp.where(live > 0.0, a, 0.0),
        jnp.where(live > 0.0, b2, 0.0),
        jnp.where(live > 0.0, c2, 0.0),
    ] + [tile3[q, 0:4] for q in range(6, 9)]
    for c in range(9):
        coef3[c, 0:4] = coefs[c]
    column = iota((16, 256), 0).astype(F32) - 7.5
    zero8 = jnp.zeros((8, 256), F32)

    for n in range(8):
        pair = slice(128 * (n // 2), 128 * (n // 2) + 128)
        mine = jnp.concatenate([coef3[:, b, pair] for b in range(4)], axis=1)
        sorted_parts = nn(jnp.concatenate(pieces(mine, 3), axis=0), sort[n])
        front = fold(sorted_parts, 3)
        front3[n] = jnp.where(iota((8, 256), 0) < 3, pltpu.roll(front, 10, 0)[0:8], 0.0)
        alpha = jnp.exp2(nn(power[...], sorted_parts.astype(BF16)))
        alpha3[n] = alpha
        split3[n] = jnp.concatenate(pieces(jnp.log(1.0 - alpha), 2), axis=1)
    for n in range(8):
        weight = jnp.exp(nn(split3[n], tri[0])) * alpha3[n]
        weight3[n] = weight
        split3[n] = jnp.concatenate(pieces(weight, 2), axis=1)
    for n in range(8):
        colour = front3[n]
        c_all = jnp.concatenate(pieces(colour, 2), axis=0)
        both = nt(split3[n], jnp.concatenate([c_all, c_all], axis=1))
        residual = both[:, 0:8] + both[:, 8:16] - wanted[n]
        weight = weight3[n]
        gain = jnp.zeros((256, 256), F32)
        shades = []
        for ch in range(3):
            gain = gain + residual[:, ch:ch + 1] * colour[ch:ch + 1]
            shades.append(jnp.sum(residual[:, ch:ch + 1] * weight, axis=0, keepdims=True))
        passed = weight * gain
        weight3[n] = passed
        split3[n] = jnp.concatenate(pieces(passed, 2), axis=1)
        front3[n] = jnp.concatenate(shades + [zero8[0:5]], axis=0)
    for n in range(8):
        alpha = alpha3[n]
        keep = 1.0 - alpha
        guess = pl.reciprocal(keep, approx=True)
        inverse = guess * (2.0 - keep * guess)
        behind = nn(split3[n], tri[1])
        change = (weight3[n] - behind * (alpha * inverse)).reshape(16, 16, 256)
        s0, s1, s2 = change[0], -7.5 * change[0], 56.25 * change[0]
        for y in range(1, 16):
            s0 = s0 + change[y]
            s1 = s1 + (y - 7.5) * change[y]
            s2 = s2 + (y - 7.5) * (y - 7.5) * change[y]
        moments = [s0, s0 * column, s1, s0 * column * column, s1 * column, s2]
        back = jnp.concatenate([jnp.sum(m, axis=0, keepdims=True) for m in moments] + [zero8[0:2], front3[n]], axis=0)
        pair = slice(128 * (n // 2), 128 * (n // 2) + 128)
        spread = fold(nn(jnp.concatenate(pieces(back, 3), axis=0), sort_back[n]), 3)
        for b in range(4):
            grad3[:, b, pair] += spread[:, 128 * b:128 * (b + 1)]

    m0, mx, my, mxx, mxy, myy = (grad3[t, 0:4] for t in range(6))
    u, v, cxx, cxy, cyy, _ = geometry()
    hx, hy = mx - u * m0, my - v * m0
    hxx = mxx - 2.0 * u * mx + u * u * m0
    hxy = mxy - u * my - v * mx + u * v * m0
    hyy = myy - 2.0 * v * my + v * v * m0
    results = [cxx * hx + cxy * hy, cxy * hx + cyy * hy, -0.5 * hxx, -hxy, -0.5 * hyy, m0]
    results += [grad3[8 + ch, 0:4] for ch in range(3)]
    for q in range(9):
        tile3[q, 0:4] = results[q]
    for q in range(9, 16):
        tile3[q, 0:4] = jnp.zeros((4, 512), F32)
    rows = jnp.concatenate([tile3[0:10, b, :] for b in range(4)] + [jnp.zeros((8, 512), F32)], axis=0)
    parts = jnp.concatenate(pieces(rows, 2), axis=0)
    put(thirds([fold(nn(parts, listed_back[h]), 2)[0:40] for h in range(3)]))


def rate_column():
    row = iota((59, 1), 0)
    rate = jnp.full((59, 1), 0.000125, F32)
    for end, value in ((14, 0.0025), (11, 0.05), (10, 0.001), (6, 0.005), (3, 0.00016)):
        rate = jnp.where(row < end, value, rate)
    return rate


def adam(both_ref, params_ref, first_ref, out_params, out_first, out_second, held_p, held_f, held_s, sems):
    rate = rate_column()
    copies = []
    for c in range(8):
        at = slice(8 * c, min(8 * c + 8, 59))
        gradient = both_ref[0, at, :]
        first = 0.9 * first_ref[at, :] + 0.1 * gradient
        second = 0.999 * both_ref[1, at, :] + 0.001 * gradient * gradient
        held_f[at, :] = first
        held_s[at, :] = second
        held_p[at, :] = params_ref[at, :] - rate[at] * first / (jnp.sqrt(second) + 1e-15)
        for part, (held, out) in enumerate(((held_p, out_params), (held_f, out_first), (held_s, out_second))):
            copy = pltpu.make_async_copy(held.at[at, :], out.at[at, :], sems.at[3 * c + part])
            copy.start()
            copies.append(copy)
    for copy in copies:
        copy.wait()


OWNER_SCRATCH = [
    pltpu.VMEM((512, 512), BF16),
    pltpu.VMEM((8, 256), F32),
    pltpu.VMEM((2, 256, 256), BF16),
    pltpu.VMEM((59, 8, 256), F32),
    pltpu.VMEM((16, 8, 256), F32),
    pltpu.VMEM((512, 512), BF16),
]
RENDER_SCRATCH = [
    pltpu.VMEM((3, 192, 512), BF16),
    pltpu.VMEM((8, 512, 256), BF16),
    pltpu.VMEM((3, 8, 512), F32),
    pltpu.VMEM((2, 512, 256), BF16),
    pltpu.VMEM((8, 256, 8), F32),
    pltpu.VMEM((3, 512, 192), BF16),
    pltpu.VMEM((8, 256, 512), BF16),
    pltpu.VMEM((256, 48), BF16),
    pltpu.VMEM((16, 8, 512), F32),
    pltpu.VMEM((16, 8, 512), F32),
    pltpu.VMEM((16, 8, 512), F32),
    pltpu.VMEM((8, 8, 256), F32),
    pltpu.VMEM((8, 256, 256), F32),
    pltpu.VMEM((8, 256, 256), F32),
    pltpu.VMEM((8, 256, 512), BF16),
]


def landed(ref, sem):
    pltpu.make_async_copy(ref, ref, sem).wait()


def step(
    params_hbm, send_hbm, lists_hbm, order_hbm, where_hbm, live_hbm, target_hbm, camera_hbm, second_hbm, out_ref,
    send_ref, lists_ref, order_ref, where_ref, live_ref, target_ref, camera_ref, in_sems,
    pick, image_of, weave, par3, shown3, pick_back, owner3,
    listed, sort, place, tri, wanted, listed_back, sort_back, power, tile3, coef3, grad3, front3, alpha3, weight3, split3,
    cam_row, cams, shown_out, shown_mid, back_send, back_in, shown_send, shown_in, back_out, back_mid, send_sems, recv_sems, own_sem,
):
    i = lax.axis_index("img")
    j = lax.axis_index("dev")
    mesh_ids = pl.DeviceIdType.MESH

    barrier = pltpu.get_barrier_semaphore()
    @pl.loop(1, 64, unroll=9)
    def _(s):
        pl.semaphore_signal(barrier, inc=1, device_id=(i, lax.rem(j + s, 64)), device_id_type=mesh_ids)

    for s in range(1, 8):
        pl.semaphore_signal(barrier, inc=1, device_id=(lax.rem(i + s, 8), j), device_id_type=mesh_ids)

    loads = [
        pltpu.make_async_copy(source, target, in_sems.at[c])
        for c, (source, target) in enumerate(
            [(camera_hbm, camera_ref), (send_hbm, send_ref)]
            + [(params_hbm.at[:, pl.ds(256 * g, 256)], par3.at[:, g, :]) for g in range(8)]
            + [(lists_hbm, lists_ref), (order_hbm, order_ref), (where_hbm, where_ref), (live_hbm, live_ref)]
            + [(target_hbm, target_ref), (second_hbm, out_ref.at[1])]
        )
    ]
    for load in loads:
        load.start()
    cam_row[...] = jnp.zeros((8, 128), F32)
    loads[0].wait()
    cam_row[0:1, 0:12] = camera_ref[...]
    pl.semaphore_wait(barrier, 70)

    def to_img(source, target, phase):
        for s in (4, 3, 5, 2, 6, 1, 7):
            t = lax.rem(i + s, 8)
            pltpu.make_async_remote_copy(
                src_ref=source(t),
                dst_ref=target,
                send_sem=send_sems.at[phase],
                recv_sem=recv_sems.at[phase],
                device_id=(t, j),
                device_id_type=mesh_ids,
            ).start()
        own = pltpu.make_async_copy(source(i), target, own_sem)
        own.start()
        own.wait()

    def to_dev(source, target, phase):
        def one(s, carry):
            t = lax.rem(j + s, 64)
            pltpu.make_async_remote_copy(
                src_ref=source.at[t],
                dst_ref=target.at[j],
                send_sem=send_sems.at[phase],
                recv_sem=recv_sems.at[phase],
                device_id=(i, t),
                device_id_type=mesh_ids,
            ).start()
            return carry

        lax.fori_loop(1, 64, one, 0)
        own = pltpu.make_async_copy(source.at[j], target.at[j], own_sem)
        own.start()
        own.wait()

    to_img(lambda t: cam_row.at[pl.ds(0, 1)], cams.at[pl.ds(i, 1)], 0)
    loads[1].wait()
    owner_tables(send_ref, pick, image_of, weave)
    for load in loads[2:10]:
        load.wait()
    shape = shape_of([par3[c] for c in range(59)])
    landed(cams.at[pl.ds(0, 7)], recv_sems.at[0])

    def put_shown(x):
        for r in range(3):
            shown_out[:, r, :] = x[64 * r:64 * (r + 1)]

    owner_forward(cams, pick, image_of, weave, par3, shown3, shape, put_shown)
    to_dev(shown_out, shown_mid, 1)
    for load in loads[10:]:
        load.wait()
    renderer_tables(
        lists_ref, order_ref, where_ref, live_ref, target_ref,
        listed, sort, place, tri, wanted, listed_back, sort_back, power, tile3, coef3, grad3,
    )
    landed(shown_mid.at[pl.ds(0, 63)], recv_sems.at[1])
    for r in range(3):
        rows = [shown_mid[0:24, r, :], shown_mid[24:48, r, :]]
        rows.append(jnp.concatenate([shown_mid[48:64, r, :], jnp.zeros((8, 128), F32)], axis=0))
        for g in range(3 if r < 2 else 2):
            shown_send[3 * g + r] = regroup(rows, 24, g)
    to_img(lambda t: shown_send.at[t], shown_in.at[i], 2)
    owner_tables_back(send_ref, pick_back)
    landed(shown_in.at[pl.ds(0, 7)], recv_sems.at[2])

    def put_back(x):
        back_out[...] = x.reshape(8, 24, 128)

    render(
        shown_in[...].reshape(192, 128),
        listed, sort, place, tri, wanted, listed_back, sort_back, power, tile3, coef3, grad3, front3, alpha3, weight3, split3,
        put_back,
    )
    to_img(lambda t: back_out.at[t], back_mid.at[i], 3)
    landed(back_mid.at[pl.ds(0, 7)], recv_sems.at[3])
    for r in range(3):
        for h in range(3):
            count = 24 if h < 2 else 16
            rows = [back_mid[3 * g + r, 0:count, :] for g in range(3 if r < 2 else 2)]
            back_send[24 * h:24 * h + count, r, :] = regroup(rows, count, h)
    to_dev(back_send, back_in, 4)
    pullback = owner_pullback(cams, image_of, par3)
    landed(back_in.at[pl.ds(0, 63)], recv_sems.at[4])
    got = jnp.concatenate([back_in[:, p, :] for p in range(3)], axis=0)
    owner_gradient(got, pullback, pick_back, weave, shown3, owner3)
    for g in range(8):
        out_ref[0, :, 256 * g:256 * (g + 1)] = owner3[:, g, :]
    landed(cams.at[pl.ds(0, 7)], send_sems.at[0])
    landed(shown_out.at[pl.ds(0, 63)], send_sems.at[1])
    landed(shown_send.at[pl.ds(0, 7)], send_sems.at[2])
    landed(back_out.at[pl.ds(0, 7)], send_sems.at[3])
    landed(back_send.at[pl.ds(0, 63)], send_sems.at[4])


def local(
    params, first_moment, second_moment, send_blocks, tile_blocks, tile_live, depth_order, tile_where, target, camera
):
    vmem = pl.BlockSpec(memory_space=pltpu.VMEM)
    whole = pl.BlockSpec(memory_space=pltpu.HBM)
    integer = jnp.int32
    by_dev = pltpu.VMEM((64, 3, 128), F32)
    by_img = pltpu.VMEM((8, 24, 128), F32)
    operands = (
        params,
        send_blocks,
        tile_blocks.reshape(1, 512),
        depth_order.reshape(8, 256),
        tile_where,
        tile_live,
        target.reshape(8, 768),
        camera,
        second_moment,
    )
    shape = jax.ShapeDtypeStruct((59, 2048), F32)
    gradient_second = pl.pallas_call(
        step,
        out_shape=jax.ShapeDtypeStruct((2, 59, 2048), F32),
        in_specs=[whole] * 9,
        out_specs=vmem,
        scratch_shapes=[
            pltpu.VMEM((1, 512), integer),
            pltpu.VMEM((1, 512), integer),
            pltpu.VMEM((8, 256), integer),
            pltpu.VMEM((1, 8), integer),
            pltpu.VMEM((1, 8), integer),
            pltpu.VMEM((8, 768), F32),
            pltpu.VMEM((1, 12), F32),
            pltpu.SemaphoreType.DMA((16,)),
        ]
        + OWNER_SCRATCH
        + [pltpu.VMEM((59, 8, 256), F32)]
        + RENDER_SCRATCH
        + [pltpu.VMEM((8, 128), F32)] * 2
        + [by_dev] * 4
        + [by_img] * 4
        + [pltpu.SemaphoreType.DMA((5,)), pltpu.SemaphoreType.DMA((5,)), pltpu.SemaphoreType.DMA],
        compiler_params=pltpu.CompilerParams(collective_id=0, has_side_effects=True, vmem_limit_bytes=24 << 20),
    )(*[pltpu.with_memory_space_constraint(operand, pltpu.HBM) for operand in operands])
    return pl.pallas_call(
        adam,
        out_shape=(shape, shape, shape),
        in_specs=[vmem] * 3,
        out_specs=(whole, whole, whole),
        scratch_shapes=[pltpu.VMEM((59, 2048), F32)] * 3 + [pltpu.SemaphoreType.DMA((24,))],
        compiler_params=pltpu.CompilerParams(vmem_limit_bytes=16 << 20),
    )(gradient_second, params, first_moment)


def solution(mesh):
    return jax.shard_map(
        local,
        mesh=mesh,
        in_specs=(
            P(None, ("img", "dev")),
            P(None, ("img", "dev")),
            P(None, ("img", "dev")),
            P(("img", "dev"), None),
            P("img", "dev", None),
            P("img", "dev"),
            P("img", "dev", None),
            P("img", "dev"),
            P("img", "dev", None),
            P("img", None),
        ),
        out_specs=(P(None, ("img", "dev")), P(None, ("img", "dev")), P(None, ("img", "dev"))),
        check_vma=False,
    )
```

```python
import functools

import jax
import jax.numpy as jnp
from jax import lax
from jax.experimental import pallas as pl
from jax.experimental.pallas import tpu as pltpu
from jax.sharding import PartitionSpec as P

F32, BF16 = jnp.float32, jnp.bfloat16
LOG2E = 1.4426950408889634
FOCAL = 1024.0
CENTRE_U, CENTRE_V = 256.0, 128.0

HARMONIC_ZERO = 0.28209479177387814
HARMONIC_ONE = 0.4886025119029199
HARMONIC_TWO = (
    1.0925484305920792,
    -1.0925484305920792,
    0.31539156525252005,
    -1.0925484305920792,
    0.5462742152960396,
)
HARMONIC_THREE = (
    -0.5900435899266435,
    2.890611442640554,
    -0.4570457994644658,
    0.3731763325901154,
    -0.4570457994644658,
    1.445305721320277,
    -0.5900435899266435,
)


def harmonics(dir_x, dir_y, dir_z):
    square_x = dir_x * dir_x
    square_y = dir_y * dir_y
    square_z = dir_z * dir_z
    return [
        -HARMONIC_ONE * dir_y,
        HARMONIC_ONE * dir_z,
        -HARMONIC_ONE * dir_x,
        HARMONIC_TWO[0] * dir_x * dir_y,
        HARMONIC_TWO[1] * dir_y * dir_z,
        HARMONIC_TWO[2] * (2.0 * square_z - square_x - square_y),
        HARMONIC_TWO[3] * dir_x * dir_z,
        HARMONIC_TWO[4] * (square_x - square_y),
        HARMONIC_THREE[0] * dir_y * (3.0 * square_x - square_y),
        HARMONIC_THREE[1] * dir_x * dir_y * dir_z,
        HARMONIC_THREE[2] * dir_y * (4.0 * square_z - square_x - square_y),
        HARMONIC_THREE[3] * dir_z * (2.0 * square_z - 3.0 * square_x - 3.0 * square_y),
        HARMONIC_THREE[4] * dir_x * (4.0 * square_z - square_x - square_y),
        HARMONIC_THREE[5] * dir_z * (square_x - square_y),
        HARMONIC_THREE[6] * dir_x * (square_x - 3.0 * square_y),
    ]


def shape_of(values):
    scales = [jnp.exp(values[3 + c]) for c in range(3)]
    norm = jnp.sqrt(values[6] * values[6] + values[7] * values[7] + values[8] * values[8] + values[9] * values[9])
    inverse_norm = 1.0 / norm
    w, x, y, z = (values[6 + c] * inverse_norm for c in range(4))
    rot = [
        [1.0 - 2.0 * (y * y + z * z), 2.0 * (x * y - w * z), 2.0 * (x * z + w * y)],
        [2.0 * (x * y + w * z), 1.0 - 2.0 * (x * x + z * z), 2.0 * (y * z - w * x)],
        [2.0 * (x * z - w * y), 2.0 * (y * z + w * x), 1.0 - 2.0 * (x * x + y * y)],
    ]
    return rot, scales, -jnp.log(1.0 + jnp.exp(-values[10]))


def project(values, cam, shape=None):
    rot, scales, log_opacity = shape_of(values) if shape is None else shape
    m = [[cam[3 * r + c] for c in range(3)] for r in range(3)]
    viewed = [m[r][0] * values[0] + m[r][1] * values[1] + m[r][2] * values[2] + cam[9 + r] for r in range(3)]
    inverse_z = 1.0 / viewed[2]
    centre_u = FOCAL * viewed[0] * inverse_z + CENTRE_U
    centre_v = FOCAL * viewed[1] * inverse_z + CENTRE_V
    focal_z = FOCAL * inverse_z
    jac = [[focal_z * (m[r][c] - viewed[r] * inverse_z * m[2][c]) for c in range(3)] for r in range(2)]
    proj = [
        [(jac[r][0] * rot[0][c] + jac[r][1] * rot[1][c] + jac[r][2] * rot[2][c]) * scales[c] for c in range(3)]
        for r in range(2)
    ]
    cov_xx = proj[0][0] * proj[0][0] + proj[0][1] * proj[0][1] + proj[0][2] * proj[0][2] + 0.3
    cov_xy = proj[0][0] * proj[1][0] + proj[0][1] * proj[1][1] + proj[0][2] * proj[1][2]
    cov_yy = proj[1][0] * proj[1][0] + proj[1][1] * proj[1][1] + proj[1][2] * proj[1][2] + 0.3
    inverse_det = 1.0 / (cov_xx * cov_yy - cov_xy * cov_xy)
    inverse_distance = 1.0 / jnp.sqrt(viewed[0] * viewed[0] + viewed[1] * viewed[1] + viewed[2] * viewed[2])
    terms = harmonics(*[viewed[c] * inverse_distance for c in range(3)])
    colour = []
    for ch in range(3):
        total = 0.5 + HARMONIC_ZERO * values[11 + ch]
        for k in range(1, 16):
            total = total + terms[k - 1] * values[11 + 3 * k + ch]
        colour.append(jnp.maximum(total, 0.0))
    return [centre_u, centre_v, cov_yy * inverse_det, -cov_xy * inverse_det, cov_xx * inverse_det, log_opacity] + colour


def iota(shape, dim):
    return lax.broadcasted_iota(jnp.int32, shape, dim)


def one_hot(truth):
    return jnp.where(truth, 1.0, 0.0).astype(BF16)


def pieces(x, count):
    out = []
    for _ in range(count - 1):
        part = x.astype(BF16)
        out.append(part)
        x = x - part.astype(F32)
    out.append(x.astype(BF16))
    return out


def nn(a, b):
    return lax.dot_general(a, b, (((1,), (0,)), ((), ())), preferred_element_type=F32)


def nt(a, b):
    return lax.dot_general(a, b, (((1,), (1,)), ((), ())), preferred_element_type=F32)


def turned(x):
    rows, columns = x.shape
    side = -columns % 128
    if side:
        x = jnp.concatenate([x, jnp.zeros((rows, side), F32)], axis=1)
    return jnp.transpose(x)[0:columns]


def thirds(x):
    return turned(jnp.concatenate(list(x) + [jnp.zeros((8, 192), F32)], axis=0))


def by_image(x):
    x = jnp.concatenate([x[16 * b:16 * b + 10] for b in range(4)], axis=0)
    last = jnp.concatenate([x[:, 384:512], jnp.zeros((40, 64), F32)], axis=1)
    return thirds([x[:, 0:192], x[:, 192:384], last])


def from_images(x):
    down = turned(x)
    down = jnp.concatenate([down[0:40], down[40:80], down[80:120, 0:128]], axis=1)
    rest = jnp.zeros((6, 512), F32)
    return jnp.concatenate([part for b in range(4) for part in (down[10 * b:10 * b + 10], rest)], axis=0)


def regroup(rows, count, kept):
    lane = iota((count, 128), 1)
    total = jnp.zeros((count, 128), F32)
    for g, x in enumerate(rows):
        moved = x if g == kept else pltpu.roll(x, 40 * (g - kept) % 128, 1)
        total = jnp.where((lane >= 40 * g) & (lane < 40 * g + 40), moved, total)
    return total


def exchange_halves(a, b):
    first = iota(a.shape, len(a.shape) - 1) < 64
    turned_a, turned_b = pltpu.roll(a, 64, len(a.shape) - 1), pltpu.roll(b, 64, len(b.shape) - 1)
    return jnp.where(first, a, turned_b), jnp.where(first, turned_a, b)


def fold(x, count):
    rows = x.shape[0] // count
    total = x[:rows]
    for c in range(1, count):
        total = total + x[c * rows:(c + 1) * rows]
    return total


def owner_tables(send_ref, pick, image_of, weave):
    pick[...] = one_hot(iota((512, 512), 0) == send_ref[...])
    row, column = iota((256, 256), 0), iota((256, 256), 1)
    weave[0] = one_hot(row == column % 64 * 4 + column // 64)
    weave[1] = one_hot(column == row % 64 * 4 + row // 64)
    images = nt((iota((8, 512), 1) // 64).astype(F32).astype(BF16), pick[...])
    own = jnp.where(iota((8, 512), 1) // 64 == iota((8, 512), 0), images, 0.0).astype(BF16)
    image_of[...] = nn(own, one_hot(iota((512, 256), 0) % 64 == iota((512, 256), 1) // 4))


def as_column(row):
    row = row.astype(F32)
    row = jnp.concatenate([row, jnp.zeros((128 - row.shape[0], row.shape[1]), F32)], axis=0)
    return jnp.transpose(row)


def owner_tables_back(send_ref, pick_back):
    pick_back[...] = one_hot(iota((512, 512), 1) == as_column(send_ref[...])[:, 0:1].astype(jnp.int32))


def cameras_of(cam_ref, image_of):
    image = image_of[...]
    masks = [image == float(i) for i in range(8)]
    cams = cam_ref[...]
    out = []
    for t in range(12):
        value = jnp.zeros((8, 256), F32)
        for i in range(8):
            value = jnp.where(masks[i], cams[i:i + 1, t:t + 1], value)
        out.append(value)
    return out


def owner_forward(cam_ref, pick, image_of, weave, par3, shown3, shape, put):
    shown = project([par3[c] for c in range(59)], cameras_of(cam_ref, image_of), shape)
    for q in range(9):
        shown3[q] = shown[q]
    for q in range(9, 16):
        shown3[q] = jnp.zeros((8, 256), F32)
    flat = shown3[0:10].reshape(80, 256)
    shown3[0:10] = fold(nn(jnp.concatenate(pieces(flat, 3), axis=0), weave[0]), 3).reshape(10, 8, 256)
    rows = [[], [], [], []]
    for p in range(2):
        at = slice(128 * p, 128 * (p + 1))
        for t in range(4):
            even, odd = exchange_halves(shown3[:, 2 * t, at], shown3[:, 2 * t + 1, at])
            rows[2 * p].append(even)
            rows[2 * p + 1].append(odd)
    rows = jnp.concatenate([jnp.concatenate(row, axis=1) for row in rows], axis=0)
    put(by_image(fold(nn(jnp.concatenate(pieces(rows, 3), axis=0), pick[...]), 3)))


def owner_pullback(cam_ref, image_of, par3):
    cams = cameras_of(cam_ref, image_of)
    return jax.vjp(lambda v: project(v, cams), [par3[c] for c in range(59)])[1]


def owner_gradient(got, pullback, pick_back, weave, shown3, grad3):
    spread = fold(nn(jnp.concatenate(pieces(from_images(got), 2), axis=0), pick_back[...]), 2)
    for p in range(2):
        at = slice(128 * p, 128 * (p + 1))
        for t in range(4):
            lanes = slice(128 * t, 128 * (t + 1))
            even, odd = exchange_halves(spread[32 * p:32 * p + 16, lanes], spread[32 * p + 16:32 * p + 32, lanes])
            shown3[:, 2 * t, at] = even
            shown3[:, 2 * t + 1, at] = odd
    flat = shown3[0:10].reshape(80, 256)
    slopes = fold(nn(jnp.concatenate(pieces(flat, 2), axis=0), weave[1]), 2).reshape(10, 8, 256)
    (grads,) = pullback([slopes[q] for q in range(9)])
    for c in range(59):
        grad3[c] = grads[c]


def renderer_tables(
    lists_ref, order_ref, where_ref, live_ref, target_ref, listed, sort, place, tri, wanted, listed_back, sort_back, power,
    tile3, coef3, grad3,
):
    def owner_at(h, spot):
        column = 24 * h + spot % 24
        return jnp.where(column < 64, spot // 24 * 64 + column, -1)

    column = as_column(lists_ref[...])[:, 0:1].astype(jnp.int32)
    for h in range(3):
        listed[h] = one_hot(owner_at(h, iota((192, 512), 0)) == lists_ref[...])
        listed_back[h] = one_hot(owner_at(h, iota((512, 192), 1)) == column)

    def one_tile(n, carry):
        order = order_ref[pl.ds(n, 1), :]
        key = (order % 4) * 128 + (n % 2) * 64 + order // 4
        sort[n] = one_hot(iota((512, 256), 0) == key)
        return carry

    lax.fori_loop(0, 8, one_tile, 0)
    order = order_ref[...]
    column = as_column((order % 4) * 128 + (iota((8, 256), 0) % 2) * 64 + order // 4)
    for n in range(8):
        sort_back[n] = one_hot(iota((256, 512), 1) == column[:, n:n + 1].astype(jnp.int32))
    lane = iota((8, 512), 1)
    tile = lane // 64
    where = jnp.zeros((8, 512), jnp.int32)
    live = jnp.zeros((8, 512), jnp.int32)
    for n in range(8):
        where = jnp.where(tile == n, where_ref[0:1, n:n + 1], where)
        live = jnp.where(tile == n, live_ref[0:1, n:n + 1], live)
    place[0] = (where % 32 * 16 + 8).astype(F32)
    place[1] = (where // 32 * 16 + 8).astype(F32)
    place[2] = jnp.where(lane % 64 < live, 1.0, 0.0)
    tri[0] = one_hot(iota((512, 256), 0) % 256 < iota((512, 256), 1))
    tri[1] = one_hot(iota((512, 256), 0) % 256 > iota((512, 256), 1))
    for n in range(8):
        rows = [target_ref[n:n + 1, 256 * ch:256 * (ch + 1)] for ch in range(3)]
        wanted[n] = jnp.transpose(jnp.concatenate(rows + [jnp.zeros((125, 256), F32)], axis=0))[:, 0:8]
    power[...] = monomials(iota((256, 48), 0), iota((256, 48), 1) % 16)
    for held in (tile3, coef3, grad3):
        held[...] = jnp.zeros(held.shape, F32)


def monomials(pixel, term):
    x = (pixel % 16).astype(F32) - 7.5
    y = (pixel // 16).astype(F32) - 7.5
    out = jnp.zeros(pixel.shape, F32)
    for t, value in enumerate((jnp.ones_like(x), x, y, x * x, x * y, y * y)):
        out = jnp.where(term == t, value, out)
    return out.astype(BF16)


def render(
    got, listed, sort, place, tri, wanted, listed_back, sort_back, power, tile3, coef3, grad3, front3, alpha3, weight3, split3, put
):
    rows = turned(got)
    tiles = jnp.zeros((48, 512), F32)
    for h in range(3):
        third = jnp.concatenate([rows[40 * h:40 * h + 40], jnp.zeros((8, 192), F32)], axis=0)
        tiles = tiles + fold(nn(jnp.concatenate(pieces(third, 3), axis=0), listed[h]), 3)
    for b in range(4):
        tile3[0:10, b, :] = tiles[10 * b:10 * b + 10]
    centre_x, centre_y, live = place[0, 0:4], place[1, 0:4], place[2, 0:4]

    def geometry():
        u, v, cxx, cxy, cyy, log_op = (tile3[q, 0:4] for q in range(6))
        return u - centre_x, v - centre_y, cxx, cxy, cyy, log_op

    u, v, cxx, cxy, cyy, log_op = geometry()
    a, b2, c2 = -0.5 * LOG2E * cxx, -LOG2E * cxy, -0.5 * LOG2E * cyy
    constant = a * u * u + b2 * u * v + c2 * v * v + LOG2E * log_op
    coefs = [
        jnp.where(live > 0.0, constant, -1e5),
        jnp.where(live > 0.0, -2.0 * a * u - b2 * v, 0.0),
        jnp.where(live > 0.0, -2.0 * c2 * v - b2 * u, 0.0),
        jnp.where(live > 0.0, a, 0.0),
        jnp.where(live > 0.0, b2, 0.0),
        jnp.where(live > 0.0, c2, 0.0),
    ] + [tile3[q, 0:4] for q in range(6, 9)]
    for c in range(9):
        coef3[c, 0:4] = coefs[c]
    column = iota((16, 256), 0).astype(F32) - 7.5
    zero8 = jnp.zeros((8, 256), F32)

    for n in range(8):
        pair = slice(128 * (n // 2), 128 * (n // 2) + 128)
        mine = jnp.concatenate([coef3[:, b, pair] for b in range(4)], axis=1)
        sorted_parts = nn(jnp.concatenate(pieces(mine, 3), axis=0), sort[n])
        front = fold(sorted_parts, 3)
        front3[n] = jnp.where(iota((8, 256), 0) < 3, pltpu.roll(front, 10, 0)[0:8], 0.0)
        alpha = jnp.minimum(jnp.exp2(nn(power[...], sorted_parts.astype(BF16))), 0.9999999)
        alpha3[n] = alpha
        split3[n] = jnp.concatenate(pieces(jnp.log(1.0 - alpha), 2), axis=1)
    for n in range(8):
        weight = jnp.exp(nn(split3[n], tri[0])) * alpha3[n]
        weight3[n] = weight
        split3[n] = jnp.concatenate(pieces(weight, 2), axis=1)
    for n in range(8):
        colour = front3[n]
        c_all = jnp.concatenate(pieces(colour, 2), axis=0)
        both = nt(split3[n], jnp.concatenate([c_all, c_all], axis=1))
        residual = both[:, 0:8] + both[:, 8:16] - wanted[n]
        weight = weight3[n]
        gain = jnp.zeros((256, 256), F32)
        shades = []
        for ch in range(3):
            gain = gain + residual[:, ch:ch + 1] * colour[ch:ch + 1]
            shades.append(jnp.sum(residual[:, ch:ch + 1] * weight, axis=0, keepdims=True))
        passed = weight * gain
        weight3[n] = passed
        split3[n] = jnp.concatenate(pieces(passed, 2), axis=1)
        front3[n] = jnp.concatenate(shades + [zero8[0:5]], axis=0)
    for n in range(8):
        alpha = alpha3[n]
        keep = 1.0 - alpha
        guess = pl.reciprocal(keep, approx=True)
        inverse = guess * (2.0 - keep * guess)
        behind = nn(split3[n], tri[1])
        change = (weight3[n] - behind * (alpha * inverse)).reshape(16, 16, 256)
        s0, s1, s2 = change[0], -7.5 * change[0], 56.25 * change[0]
        for y in range(1, 16):
            s0 = s0 + change[y]
            s1 = s1 + (y - 7.5) * change[y]
            s2 = s2 + (y - 7.5) * (y - 7.5) * change[y]
        moments = [s0, s0 * column, s1, s0 * column * column, s1 * column, s2]
        back = jnp.concatenate([jnp.sum(m, axis=0, keepdims=True) for m in moments] + [zero8[0:2], front3[n]], axis=0)
        pair = slice(128 * (n // 2), 128 * (n // 2) + 128)
        spread = fold(nn(jnp.concatenate(pieces(back, 3), axis=0), sort_back[n]), 3)
        for b in range(4):
            grad3[:, b, pair] += spread[:, 128 * b:128 * (b + 1)]

    m0, mx, my, mxx, mxy, myy = (grad3[t, 0:4] for t in range(6))
    u, v, cxx, cxy, cyy, _ = geometry()
    hx, hy = mx - u * m0, my - v * m0
    hxx = mxx - 2.0 * u * mx + u * u * m0
    hxy = mxy - u * my - v * mx + u * v * m0
    hyy = myy - 2.0 * v * my + v * v * m0
    results = [cxx * hx + cxy * hy, cxy * hx + cyy * hy, -0.5 * hxx, -hxy, -0.5 * hyy, m0]
    results += [grad3[8 + ch, 0:4] for ch in range(3)]
    for q in range(9):
        tile3[q, 0:4] = results[q]
    for q in range(9, 16):
        tile3[q, 0:4] = jnp.zeros((4, 512), F32)
    rows = jnp.concatenate([tile3[0:10, b, :] for b in range(4)] + [jnp.zeros((8, 512), F32)], axis=0)
    parts = jnp.concatenate(pieces(rows, 2), axis=0)
    put(thirds([fold(nn(parts, listed_back[h]), 2)[0:40] for h in range(3)]))


def rate_column():
    row = iota((59, 1), 0)
    rate = jnp.full((59, 1), 0.000125, F32)
    for end, value in ((14, 0.0025), (11, 0.05), (10, 0.001), (6, 0.005), (3, 0.00016)):
        rate = jnp.where(row < end, value, rate)
    return rate


def adam(both_ref, params_ref, first_ref, out_params, out_first, out_second, held_p, held_f, held_s, sems):
    rate = rate_column()
    copies = []
    for c in range(8):
        at = slice(8 * c, min(8 * c + 8, 59))
        gradient = both_ref[0, at, :]
        first = 0.9 * first_ref[at, :] + 0.1 * gradient
        second = 0.999 * both_ref[1, at, :] + 0.001 * gradient * gradient
        held_f[at, :] = first
        held_s[at, :] = second
        held_p[at, :] = params_ref[at, :] - rate[at] * first / (jnp.sqrt(second) + 1e-15)
        for part, (held, out) in enumerate(((held_p, out_params), (held_f, out_first), (held_s, out_second))):
            copy = pltpu.make_async_copy(held.at[at, :], out.at[at, :], sems.at[3 * c + part])
            copy.start()
            copies.append(copy)
    for copy in copies:
        copy.wait()


OWNER_SCRATCH = [
    pltpu.VMEM((512, 512), BF16),
    pltpu.VMEM((8, 256), F32),
    pltpu.VMEM((2, 256, 256), BF16),
    pltpu.VMEM((59, 8, 256), F32),
    pltpu.VMEM((16, 8, 256), F32),
    pltpu.VMEM((512, 512), BF16),
]
RENDER_SCRATCH = [
    pltpu.VMEM((3, 192, 512), BF16),
    pltpu.VMEM((8, 512, 256), BF16),
    pltpu.VMEM((3, 8, 512), F32),
    pltpu.VMEM((2, 512, 256), BF16),
    pltpu.VMEM((8, 256, 8), F32),
    pltpu.VMEM((3, 512, 192), BF16),
    pltpu.VMEM((8, 256, 512), BF16),
    pltpu.VMEM((256, 48), BF16),
    pltpu.VMEM((16, 8, 512), F32),
    pltpu.VMEM((16, 8, 512), F32),
    pltpu.VMEM((16, 8, 512), F32),
    pltpu.VMEM((8, 8, 256), F32),
    pltpu.VMEM((8, 256, 256), F32),
    pltpu.VMEM((8, 256, 256), F32),
    pltpu.VMEM((8, 256, 512), BF16),
]


def landed(ref, sem):
    pltpu.make_async_copy(ref, ref, sem).wait()


def step(
    params_hbm, send_hbm, lists_hbm, order_hbm, where_hbm, live_hbm, target_hbm, camera_hbm, second_hbm, out_ref,
    send_ref, lists_ref, order_ref, where_ref, live_ref, target_ref, camera_ref, in_sems,
    pick, image_of, weave, par3, shown3, pick_back, owner3,
    listed, sort, place, tri, wanted, listed_back, sort_back, power, tile3, coef3, grad3, front3, alpha3, weight3, split3,
    cam_row, cams, shown_out, shown_mid, back_send, back_in, shown_send, shown_in, back_out, back_mid, send_sems, recv_sems, own_sem,
):
    i = lax.axis_index("img")
    j = lax.axis_index("dev")
    mesh_ids = pl.DeviceIdType.MESH

    barrier = pltpu.get_barrier_semaphore()
    @pl.loop(1, 64, unroll=9)
    def _(s):
        pl.semaphore_signal(barrier, inc=1, device_id=(i, lax.rem(j + s, 64)), device_id_type=mesh_ids)

    for s in range(1, 8):
        pl.semaphore_signal(barrier, inc=1, device_id=(lax.rem(i + s, 8), j), device_id_type=mesh_ids)

    loads = [
        pltpu.make_async_copy(source, target, in_sems.at[c])
        for c, (source, target) in enumerate(
            [(camera_hbm, camera_ref), (send_hbm, send_ref)]
            + [(params_hbm.at[:, pl.ds(256 * g, 256)], par3.at[:, g, :]) for g in range(8)]
            + [(lists_hbm, lists_ref), (order_hbm, order_ref), (where_hbm, where_ref), (live_hbm, live_ref)]
            + [(target_hbm, target_ref), (second_hbm, out_ref.at[1])]
        )
    ]
    for load in loads:
        load.start()
    cam_row[...] = jnp.zeros((8, 128), F32)
    loads[0].wait()
    cam_row[0:1, 0:12] = camera_ref[...]
    pl.semaphore_wait(barrier, 70)

    def to_img(source, target, phase):
        for s in (4, 3, 5, 2, 6, 1, 7):
            t = lax.rem(i + s, 8)
            pltpu.make_async_remote_copy(
                src_ref=source(t),
                dst_ref=target,
                send_sem=send_sems.at[phase],
                recv_sem=recv_sems.at[phase],
                device_id=(t, j),
                device_id_type=mesh_ids,
            ).start()
        own = pltpu.make_async_copy(source(i), target, own_sem)
        own.start()
        own.wait()

    def to_dev(source, target, phase):
        def one(s, carry):
            t = lax.rem(j + s, 64)
            pltpu.make_async_remote_copy(
                src_ref=source.at[t],
                dst_ref=target.at[j],
                send_sem=send_sems.at[phase],
                recv_sem=recv_sems.at[phase],
                device_id=(i, t),
                device_id_type=mesh_ids,
            ).start()
            return carry

        lax.fori_loop(1, 64, one, 0)
        own = pltpu.make_async_copy(source.at[j], target.at[j], own_sem)
        own.start()
        own.wait()

    to_img(lambda t: cam_row.at[pl.ds(0, 1)], cams.at[pl.ds(i, 1)], 0)
    loads[1].wait()
    owner_tables(send_ref, pick, image_of, weave)
    for load in loads[2:10]:
        load.wait()
    shape = shape_of([par3[c] for c in range(59)])
    landed(cams.at[pl.ds(0, 7)], recv_sems.at[0])

    def put_shown(x):
        for r in range(3):
            shown_out[:, r, :] = x[64 * r:64 * (r + 1)]

    owner_forward(cams, pick, image_of, weave, par3, shown3, shape, put_shown)
    to_dev(shown_out, shown_mid, 1)
    for load in loads[10:]:
        load.wait()
    renderer_tables(
        lists_ref, order_ref, where_ref, live_ref, target_ref,
        listed, sort, place, tri, wanted, listed_back, sort_back, power, tile3, coef3, grad3,
    )
    landed(shown_mid.at[pl.ds(0, 63)], recv_sems.at[1])
    for r in range(3):
        rows = [shown_mid[0:24, r, :], shown_mid[24:48, r, :]]
        rows.append(jnp.concatenate([shown_mid[48:64, r, :], jnp.zeros((8, 128), F32)], axis=0))
        for g in range(3 if r < 2 else 2):
            shown_send[3 * g + r] = regroup(rows, 24, g)
    to_img(lambda t: shown_send.at[t], shown_in.at[i], 2)
    owner_tables_back(send_ref, pick_back)
    landed(shown_in.at[pl.ds(0, 7)], recv_sems.at[2])

    def put_back(x):
        back_out[...] = x.reshape(8, 24, 128)

    render(
        shown_in[...].reshape(192, 128),
        listed, sort, place, tri, wanted, listed_back, sort_back, power, tile3, coef3, grad3, front3, alpha3, weight3, split3,
        put_back,
    )
    to_img(lambda t: back_out.at[t], back_mid.at[i], 3)
    landed(back_mid.at[pl.ds(0, 7)], recv_sems.at[3])
    for r in range(3):
        for h in range(3):
            count = 24 if h < 2 else 16
            rows = [back_mid[3 * g + r, 0:count, :] for g in range(3 if r < 2 else 2)]
            back_send[24 * h:24 * h + count, r, :] = regroup(rows, count, h)
    to_dev(back_send, back_in, 4)
    pullback = owner_pullback(cams, image_of, par3)
    landed(back_in.at[pl.ds(0, 63)], recv_sems.at[4])
    got = jnp.concatenate([back_in[:, p, :] for p in range(3)], axis=0)
    owner_gradient(got, pullback, pick_back, weave, shown3, owner3)
    for g in range(8):
        out_ref[0, :, 256 * g:256 * (g + 1)] = owner3[:, g, :]
    landed(cams.at[pl.ds(0, 7)], send_sems.at[0])
    landed(shown_out.at[pl.ds(0, 63)], send_sems.at[1])
    landed(shown_send.at[pl.ds(0, 7)], send_sems.at[2])
    landed(back_out.at[pl.ds(0, 7)], send_sems.at[3])
    landed(back_send.at[pl.ds(0, 63)], send_sems.at[4])


def local(
    params, first_moment, second_moment, send_blocks, tile_blocks, tile_live, depth_order, tile_where, target, camera
):
    vmem = pl.BlockSpec(memory_space=pltpu.VMEM)
    whole = pl.BlockSpec(memory_space=pltpu.HBM)
    integer = jnp.int32
    by_dev = pltpu.VMEM((64, 3, 128), F32)
    by_img = pltpu.VMEM((8, 24, 128), F32)
    operands = (
        params,
        send_blocks,
        tile_blocks.reshape(1, 512),
        depth_order.reshape(8, 256),
        tile_where,
        tile_live,
        target.reshape(8, 768),
        camera,
        second_moment,
    )
    shape = jax.ShapeDtypeStruct((59, 2048), F32)
    gradient_second = pl.pallas_call(
        step,
        out_shape=jax.ShapeDtypeStruct((2, 59, 2048), F32),
        in_specs=[whole] * 9,
        out_specs=vmem,
        scratch_shapes=[
            pltpu.VMEM((1, 512), integer),
            pltpu.VMEM((1, 512), integer),
            pltpu.VMEM((8, 256), integer),
            pltpu.VMEM((1, 8), integer),
            pltpu.VMEM((1, 8), integer),
            pltpu.VMEM((8, 768), F32),
            pltpu.VMEM((1, 12), F32),
            pltpu.SemaphoreType.DMA((16,)),
        ]
        + OWNER_SCRATCH
        + [pltpu.VMEM((59, 8, 256), F32)]
        + RENDER_SCRATCH
        + [pltpu.VMEM((8, 128), F32)] * 2
        + [by_dev] * 4
        + [by_img] * 4
        + [pltpu.SemaphoreType.DMA((5,)), pltpu.SemaphoreType.DMA((5,)), pltpu.SemaphoreType.DMA],
        compiler_params=pltpu.CompilerParams(collective_id=0, has_side_effects=True, vmem_limit_bytes=24 << 20),
    )(*[pltpu.with_memory_space_constraint(operand, pltpu.HBM) for operand in operands])
    return pl.pallas_call(
        adam,
        out_shape=(shape, shape, shape),
        in_specs=[vmem] * 3,
        out_specs=(whole, whole, whole),
        scratch_shapes=[pltpu.VMEM((59, 2048), F32)] * 3 + [pltpu.SemaphoreType.DMA((24,))],
        compiler_params=pltpu.CompilerParams(vmem_limit_bytes=16 << 20),
    )(gradient_second, params, first_moment)


def solution(mesh):
    return jax.shard_map(
        local,
        mesh=mesh,
        in_specs=(
            P(None, ("img", "dev")),
            P(None, ("img", "dev")),
            P(None, ("img", "dev")),
            P(("img", "dev"), None),
            P("img", "dev", None),
            P("img", "dev"),
            P("img", "dev", None),
            P("img", "dev"),
            P("img", "dev", None),
            P("img", None),
        ),
        out_specs=(P(None, ("img", "dev")), P(None, ("img", "dev")), P(None, ("img", "dev"))),
        check_vma=False,
    )
```
